32 devices in a mesh: dp: 2 (over x), wide: 4 (over y, core), narrow: 4 (over z).
Axes of the slice: x: 2, y: 2, z: 4, core: 2. Of those that a mesh axis runs over, the one named last changes fastest.
Arguments:
- out_grad: bfloat16 [512, 2048], P(('dp', 'wide', 'narrow')), may hold values from -6 to 6
- routes: int32 [512, 8], P(('dp', 'wide', 'narrow')), may hold values from 0 to 15, as said below
- gates: bfloat16 [512, 8], P(('dp', 'wide', 'narrow')), may hold values from 0.029907227 to 0.59765625
- pre_gate: bfloat16 [2, 16, 256, 768], P('dp', ('wide', 'narrow')), may hold values from -5 to 5
- pre_up: bfloat16 [2, 16, 256, 768], P('dp', ('wide', 'narrow')), may hold values from -5 to 5
- down_weight: bfloat16 [16, 768, 2048], P(('wide', 'narrow')), may hold values from -0.125 to 0.125
Outputs:
- grad_down: bfloat16 [16, 768, 2048], P(('wide', 'narrow'), None, 'dp')
- grad_pre_gate: bfloat16 [2, 16, 256, 768], P('dp', ('wide', 'narrow'))
- grad_pre_up: bfloat16 [2, 16, 256, 768], P('dp', ('wide', 'narrow'))
- grad_gates: float32 [512, 8], P(('dp', 'wide', 'narrow'))
The draws below stay inside these ranges and needn't reach their ends.
Inputs may be any that keep to these rules, and one draw needn't show every extreme that they name: `routes`: each token names 8 different experts. The tokens of one device name each expert either 0 or 16 times. In every group some expert is named 16 times by every device of the group.
All inputs are finite; a program needn't handle non-finite values.
Results may differ from the reference program's by a relative error of at most 0.012.
Values may be sent and summed in bfloat16 or wider, within the bound.
No kernel may reach another device: no remote copies, remote signals or barrier semaphores. Data moves between devices by JAX's collectives and lax.ppermute only.
A program may use at most 64 MiB of HBM per device.

```python
import math
import jax
import jax.numpy as jnp
from jax import lax

D = 2048
FF = 768
TOPK = 8
TOK_DEV = 16
EXPERTS = 16
GROUPS = 2
TOKENS = 512
CAP = 16
SLOTS = 256


def draw_routes(key, part):
    devices = TOKENS // TOK_DEV
    residues = EXPERTS // TOPK
    used_count = max(residues // 2, 1)
    key_perm = jax.random.fold_in(key, 11)
    key_order = jax.random.fold_in(key, 12)
    key_hot = jax.random.fold_in(key, 13)
    orders = jax.vmap(lambda subkey: jax.random.permutation(subkey, EXPERTS))(jax.random.split(key_perm, devices)).astype(jnp.int32)
    picked = jax.vmap(lambda subkey: jax.random.permutation(subkey, residues))(jax.random.split(key_order, devices)).astype(jnp.int32)
    hot_expert = jnp.repeat(jax.random.randint(key_hot, (GROUPS,), 0, EXPERTS, dtype=jnp.int32), devices // GROUPS)
    position_ids = jnp.arange(EXPERTS, dtype=jnp.int32)[None, :]
    where_hot = jnp.sum(jnp.where(orders == hot_expert[:, None], position_ids, 0), axis=1)
    first_pick = picked[:, 0]
    value_first = jnp.take_along_axis(orders, first_pick[:, None], axis=1)[:, 0]
    orders = jnp.where(position_ids == first_pick[:, None], hot_expert[:, None], jnp.where(position_ids == where_hot[:, None], value_first[:, None], orders))
    token_ids = jnp.arange(TOK_DEV, dtype=jnp.int32)
    residue = picked[:, token_ids % used_count]
    slot_places = residue[:, :, None] + jnp.arange(TOPK, dtype=jnp.int32)[None, None, :] * residues
    chosen = jnp.take_along_axis(orders, slot_places.reshape(devices, TOK_DEV * TOPK), axis=1)
    return chosen.reshape(TOKENS, TOPK).astype(jnp.int32)


def block_scale(rng, shape, cuts, least, top_value):
    level = 1.0
    for axis_at, shards_of in cuts:
        steps = jax.random.uniform(jax.random.fold_in(jax.random.fold_in(rng, 6), axis_at), (shards_of,), jnp.float32, least / len(cuts), top_value / len(cuts))
        level = level * jnp.repeat(jnp.exp(steps), shape[axis_at] // shards_of).reshape((-1,) + (1,) * (len(shape) - 1 - axis_at))
    return level


def gaussian(own_key, extent, spread, limit, pieces=(), held_as=jnp.bfloat16):
    loudness = block_scale(own_key, extent, pieces, -0.22, 0.18) if pieces else 1.0
    drawn = jax.random.normal(own_key, extent, jnp.float32) * spread * loudness
    return jnp.minimum(jnp.maximum(drawn, -limit), limit).astype(held_as)


def setup_inputs(seed: int = 0) -> dict:
    seeds = jax.random.split(jax.random.key(seed), 7)
    return {
        "out_grad": gaussian(seeds[0], (TOKENS, D), 1.0, 6.0, ((0, 32),)),
        "routes": draw_routes(jax.random.fold_in(seeds[6], 71), 0),
        "gates": jnp.clip(jnp.exp(math.log(0.59765625) - 2.99491561 * jax.random.uniform(seeds[2], (TOKENS, TOPK), jnp.float32) ** block_scale(seeds[2], (TOKENS, TOPK), ((0, 32),), -0.2, 0.2)), 0.029907227, 0.59765625).astype(jnp.bfloat16),
        "pre_gate": gaussian(seeds[3], (GROUPS, EXPERTS, SLOTS, FF), 1.0, 5.0, ((0, 2), (1, 16))),
        "pre_up": gaussian(seeds[4], (GROUPS, EXPERTS, SLOTS, FF), 1.0, 5.0, ((0, 2), (1, 16))),
        "down_weight": gaussian(seeds[5], (EXPERTS, FF, D), D ** -0.5, 0.125, ((0, 16),)),
    }


def reference(out_grad, routes, gates, pre_gate, pre_up, down_weight):
    token_ids = jnp.arange(TOKENS, dtype=jnp.int32)
    device = token_ids // TOK_DEV
    group_ids = device // EXPERTS
    source = device % EXPERTS
    expert_ids = jnp.arange(EXPERTS, dtype=jnp.int32)
    named_hits = (routes[:, :, None] == expert_ids[None, None, :]).astype(jnp.int32)
    hit_counts = jnp.sum(named_hits, axis=1).reshape(TOKENS // TOK_DEV, TOK_DEV, EXPERTS)
    before = (jnp.cumsum(hit_counts, axis=1) - hit_counts).reshape(TOKENS, EXPERTS)
    position = jnp.sum(named_hits * before[:, None, :], axis=2).astype(jnp.int32)
    slot_ids = source[:, None] * CAP + position
    flat_index = ((group_ids[:, None] * EXPERTS + routes) * SLOTS + slot_ids).reshape(-1).astype(jnp.int32)
    owners = jnp.broadcast_to(token_ids[:, None], (TOKENS, TOPK)).reshape(-1).astype(jnp.int32)
    slot_token = jnp.full((GROUPS * EXPERTS * SLOTS,), TOKENS, jnp.int32).at[flat_index].set(owners)
    slot_token = slot_token.reshape(GROUPS, EXPERTS, SLOTS)
    slot_gate = jnp.zeros((GROUPS * EXPERTS * SLOTS,), gates.dtype).at[flat_index].set(gates.reshape(-1))
    slot_gate = slot_gate.reshape(GROUPS, EXPERTS, SLOTS)
    padded = jnp.concatenate([out_grad, jnp.zeros((1, D), out_grad.dtype)], axis=0)

    def per_expert(expert):
        weight = down_weight[expert]
        total_grad = jnp.zeros((FF, D), jnp.float32)
        grads_gate = []
        grads_up = []
        slot_sums = []
        for group_index in range(GROUPS):
            routed_rows = padded[slot_token[group_index, expert]]
            gate_col = slot_gate[group_index, expert].astype(jnp.float32)
            gate_pre = pre_gate[group_index, expert].astype(jnp.float32)
            up_pre = pre_up[group_index, expert].astype(jnp.float32)
            sigmoid_a = jax.nn.sigmoid(gate_pre)
            hidden = (gate_pre * sigmoid_a * up_pre).astype(jnp.bfloat16)
            back_prop = lax.dot_general(routed_rows, weight, (((1,), (1,)), ((), ())),
                                        preferred_element_type=jnp.float32)
            slot_sums.append(jnp.sum(hidden.astype(jnp.float32) * back_prop, axis=1))
            carried = gate_col[:, None] * back_prop
            grads_gate.append((carried * up_pre * sigmoid_a * (1.0 + gate_pre * (1.0 - sigmoid_a))).astype(jnp.bfloat16))
            grads_up.append((carried * gate_pre * sigmoid_a).astype(jnp.bfloat16))
            scaled = (gate_col[:, None] * hidden.astype(jnp.float32)).astype(jnp.bfloat16)
            total_grad = total_grad + lax.dot_general(scaled, routed_rows, (((0,), (0,)), ((), ())),
                                                      preferred_element_type=jnp.float32)
        return (total_grad.astype(jnp.bfloat16), jnp.stack(grads_gate), jnp.stack(grads_up), jnp.stack(slot_sums))

    grad_down, grad_a, grad_b, slot_grad = lax.map(per_expert, expert_ids)
    grad_pre_gate = jnp.transpose(grad_a, (1, 0, 2, 3))
    grad_pre_up = jnp.transpose(grad_b, (1, 0, 2, 3))
    grad_gates = jnp.transpose(slot_grad, (1, 0, 2)).reshape(-1)[flat_index].reshape(TOKENS, TOPK)
    return grad_down, grad_pre_gate, grad_pre_up, grad_gates
```

```python
import functools

import jax
import jax.numpy as jnp
from jax import lax
from jax.experimental import pallas as pl
from jax.experimental.pallas import tpu as pltpu
from jax.sharding import PartitionSpec as P

LANES = 128
VMEM_LIMIT = 48 * 1024 * 1024


def shards_exchange(out_grad, routes, gates, pre_gate, pre_up, down_weight):
    wide_count = lax.axis_size("wide")
    narrow_count = lax.axis_size("narrow")
    experts = wide_count * narrow_count
    token_count, top_count = routes.shape
    slot_count = pre_gate.shape[2]
    capacity = slot_count // experts
    expert_ids = jnp.arange(experts, dtype=jnp.int32)
    named_hits = (routes[:, :, None] == expert_ids[None, None, :]).astype(jnp.int32)
    hit_counts = jnp.sum(named_hits, axis=1)
    before = jnp.cumsum(hit_counts, axis=0) - hit_counts
    position = jnp.sum(named_hits * before[:, None, :], axis=2)
    target = routes * capacity + position
    slot_ids = jnp.arange(slot_count, dtype=jnp.int32)
    placed = target[:, :, None] == slot_ids[None, None, :]
    choose = jnp.sum(placed.astype(jnp.bfloat16), axis=1)
    outgoing = lax.dot_general(
        choose, out_grad, (((0,), (0,)), ((), ())), preferred_element_type=jnp.float32
    ).astype(jnp.bfloat16)
    gate_out = jnp.sum(
        jnp.where(placed, gates[:, :, None].astype(jnp.float32), 0.0), axis=(0, 1)
    ).astype(jnp.bfloat16)
    outgoing = outgoing.reshape(wide_count, narrow_count, capacity, outgoing.shape[1])
    gate_out = gate_out.reshape(wide_count, narrow_count, capacity)
    incoming, gate_in = (
        lax.all_to_all(
            lax.all_to_all(outgoing, "wide", split_axis=0, concat_axis=0, tiled=True),
            "narrow",
            split_axis=1,
            concat_axis=1,
            tiled=True,
        ),
        lax.all_to_all(
            lax.all_to_all(gate_out, "wide", split_axis=0, concat_axis=0, tiled=True),
            "narrow",
            split_axis=1,
            concat_axis=1,
            tiled=True,
        ),
    )
    routed_rows = incoming.reshape(slot_count, incoming.shape[3])
    gate_col = gate_in.reshape(slot_count).astype(jnp.float32)
    gate_pre = pre_gate[0, 0].astype(jnp.float32)
    up_pre = pre_up[0, 0].astype(jnp.float32)
    weight = down_weight[0]
    sigmoid_a = jax.nn.sigmoid(gate_pre)
    hidden = (gate_pre * sigmoid_a * up_pre).astype(jnp.bfloat16)
    back_prop = lax.dot_general(
        routed_rows, weight, (((1,), (1,)), ((), ())), preferred_element_type=jnp.float32
    )
    slot_grad = jnp.sum(hidden.astype(jnp.float32) * back_prop, axis=1)
    carried = gate_col[:, None] * back_prop
    grad_a = (carried * up_pre * sigmoid_a * (1.0 + gate_pre * (1.0 - sigmoid_a))).astype(
        jnp.bfloat16
    )
    grad_b = (carried * gate_pre * sigmoid_a).astype(jnp.bfloat16)
    scaled = (gate_col[:, None] * hidden.astype(jnp.float32)).astype(jnp.bfloat16)
    all_scaled = lax.all_gather(scaled, "dp", axis=0, tiled=True)
    columns = lax.all_to_all(routed_rows, "dp", split_axis=1, concat_axis=0, tiled=True)
    grad_down = lax.dot_general(
        all_scaled, columns, (((0,), (0,)), ((), ())), preferred_element_type=jnp.float32
    ).astype(jnp.bfloat16)
    slot_back = slot_grad.reshape(wide_count, narrow_count, capacity)
    returned = lax.all_to_all(
        lax.all_to_all(slot_back, "wide", split_axis=0, concat_axis=0, tiled=True),
        "narrow",
        split_axis=1,
        concat_axis=1,
        tiled=True,
    )
    grad_gates = jnp.take(returned.reshape(slot_count), target.reshape(-1)).reshape(
        token_count, top_count
    )
    return (grad_down[None], grad_a[None, None], grad_b[None, None], grad_gates)


def swap(x, axis, bits):
    count = lax.axis_size(axis)
    return lax.ppermute(x, axis, [(i, i ^ bits) for i in range(count)])


def call(kernel, outs, cost, *args):
    flops, moved = cost
    return pl.pallas_call(
        kernel,
        out_shape=outs,
        in_specs=[pl.BlockSpec(memory_space=pltpu.VMEM)] * len(args),
        out_specs=jax.tree.map(lambda _: pl.BlockSpec(memory_space=pltpu.VMEM), outs),
        compiler_params=pltpu.CompilerParams(vmem_limit_bytes=VMEM_LIMIT),
        cost_estimate=pl.CostEstimate(flops=flops, bytes_accessed=moved, transcendentals=0),
    )(*args)


def peer(xors):
    wide_bits, narrow_bits = xors
    return (lax.axis_index("wide") ^ wide_bits) * lax.axis_size("narrow") + (
        lax.axis_index("narrow") ^ narrow_bits
    )


def payload_kernel(grad_ref, routes_ref, gates_ref, out_ref):
    features = grad_ref.shape[1]
    rows = grad_ref.shape[0]
    out_ref[:, :features] = grad_ref[...]
    routes = routes_ref[...]
    gates = gates_ref[...].astype(jnp.float32)
    ids = lax.broadcasted_iota(jnp.int32, (LANES, rows), 0)
    table = jnp.zeros((LANES, rows), jnp.float32)
    for k in range(routes.shape[0]):
        table = table + jnp.where(ids == routes[k : k + 1, :], gates[k : k + 1, :], 0.0)
    table = jnp.concatenate([table, jnp.zeros((LANES, LANES - rows), jnp.float32)], axis=1)
    out_ref[:, features:] = table.T[:rows, :].astype(out_ref.dtype)


def hidden_kernel(order, rows, pre_gate_ref, pre_up_ref, out_ref):
    for place, xors in enumerate(order):
        source = pl.ds(pl.multiple_of(peer(xors) * rows, rows), rows)
        value = pre_gate_ref[source, :].astype(jnp.float32)
        up = pre_up_ref[source, :].astype(jnp.float32)
        out_ref[place * rows : (place + 1) * rows, :] = (
            value * jax.nn.sigmoid(value) * up
        ).astype(out_ref.dtype)


def back_kernel(features, half_ref, rest_ref, weight_ref, hidden_ref, back_ref, sums_ref):
    rows = half_ref.shape[0]
    for part, ref in enumerate((half_ref, rest_ref)):
        here = slice(part * rows, (part + 1) * rows)
        back = lax.dot_general(
            ref[:, :features],
            weight_ref[...],
            (((1,), (1,)), ((), ())),
            preferred_element_type=jnp.float32,
        )
        back_ref[here, :] = back
        product = hidden_ref[here, :].astype(jnp.float32) * back
        folded = product[:, :LANES]
        for at in range(LANES, product.shape[1], LANES):
            folded = folded + product[:, at : at + LANES]
        for at in range(0, rows, LANES):
            row = (part * rows + at) // LANES
            sums_ref[row : row + 1, :] = jnp.sum(
                folded[at : at + LANES, :].T, axis=0, keepdims=True
            )


def own_gates(table):
    lane = lax.broadcasted_iota(jnp.int32, table.shape, 1)
    return jnp.sum(
        jnp.where(lane == peer((0, 0)), table.astype(jnp.float32), 0.0), axis=1, keepdims=True
    )


def grads_kernel(
    order,
    rows,
    features,
    half_ref,
    rest_ref,
    back_ref,
    hidden_ref,
    pre_gate_ref,
    pre_up_ref,
    grad_gate_ref,
    grad_up_ref,
    scaled_ref,
):
    per = half_ref.shape[0] // rows
    for place, xors in enumerate(order):
        ref = (half_ref, rest_ref)[place // per]
        start = (place % per) * rows
        gate = own_gates(ref[start : start + rows, features:])
        here = slice(place * rows, (place + 1) * rows)
        source = pl.ds(pl.multiple_of(peer(xors) * rows, rows), rows)
        value = pre_gate_ref[source, :].astype(jnp.float32)
        up = pre_up_ref[source, :].astype(jnp.float32)
        sig = jax.nn.sigmoid(value)
        carried = gate * back_ref[here, :]
        grad_gate_ref[source, :] = (carried * up * sig * (1.0 + value * (1.0 - sig))).astype(
            grad_gate_ref.dtype
        )
        grad_up_ref[source, :] = (carried * value * sig).astype(grad_up_ref.dtype)
        scaled_ref[here, :] = (gate * hidden_ref[here, :].astype(jnp.float32)).astype(
            scaled_ref.dtype
        )


def down_kernel(pairs, scaled_ref, half_ref, rest_ref, *refs):
    out_ref = refs[-1]
    columns = out_ref.shape[1]
    rows = half_ref.shape[0]
    contract = (((0,), (0,)), ((), ()))
    mine = pl.ds(pl.multiple_of(lax.axis_index("dp") * columns, columns), columns)
    scaled = [scaled_ref[...]]
    tokens = [half_ref[:, mine], rest_ref[:, mine]]
    for pair in range(pairs):
        hidden_ref, one_ref, two_ref = refs[3 * pair : 3 * pair + 3]
        gate = jnp.concatenate(
            [own_gates(one_ref[:, columns:]), own_gates(two_ref[:, columns:])], axis=0
        )
        scaled.append((gate * hidden_ref[...].astype(jnp.float32)).astype(scaled_ref.dtype))
        tokens += [one_ref[:, :columns], two_ref[:, :columns]]
    out_ref[...] = lax.dot_general(
        jnp.concatenate(scaled, axis=0),
        jnp.concatenate(tokens, axis=0),
        contract,
        preferred_element_type=jnp.float32,
    ).astype(out_ref.dtype)


def pick_kernel(order, back_order, rows, routes_ref, sums_ref, out_ref):
    routes = routes_ref[...]
    total = jnp.zeros(out_ref.shape, jnp.float32)
    for line, xors in enumerate(back_order):
        start = order.index(xors) * rows
        at = start % LANES
        found = sums_ref[line, start // LANES : start // LANES + 1, :][:, at : at + rows]
        total = total + jnp.where(routes == peer(xors), found, 0.0)
    out_ref[...] = total


def shards_gather(out_grad, routes, gates, pre_gate, pre_up, down_weight):
    dp_count = lax.axis_size("dp")
    wide_count = lax.axis_size("wide")
    narrow_count = lax.axis_size("narrow")
    rows, features = out_grad.shape
    slot_count, units = pre_gate.shape[2:]
    columns = features // dp_count
    routes_t = routes.T
    gates_t = gates.T
    pre_gate = pre_gate[0, 0]
    pre_up = pre_up[0, 0]
    weight = down_weight[0]
    bf16, f32 = jnp.bfloat16, jnp.float32
    shape = jax.ShapeDtypeStruct

    payload = call(
        payload_kernel,
        shape((rows, features + LANES), bf16),
        (rows * features, 4 * rows * features),
        out_grad,
        routes_t,
        gates_t,
    )
    held = jnp.concatenate(
        [payload] + [swap(payload, "narrow", bits) for bits in range(1, narrow_count)], axis=0
    )
    order = [(0, bits) for bits in range(narrow_count)]
    wide_bits = [1 << b for b in range(1, wide_count.bit_length() - 1)]
    for bits in wide_bits:
        held = jnp.concatenate([held, swap(held, "wide", bits)], axis=0)
        order += [(w ^ bits, n) for w, n in order]
    rest = swap(held, "wide", 1)
    order += [(w ^ 1, n) for w, n in order]
    order = tuple(order)

    hidden = call(
        functools.partial(hidden_kernel, order, rows),
        shape((slot_count, units), bf16),
        (20 * slot_count * units, 6 * slot_count * units),
        pre_gate,
        pre_up,
    )
    others = []
    for bits in range(1, dp_count):
        partner = lax.axis_index("dp") ^ bits
        cut = lax.dynamic_slice_in_dim(held[:, :features], partner * columns, columns, axis=1)
        one = swap(jnp.concatenate([cut, held[:, features:]], axis=1), "dp", bits)
        others += [swap(hidden, "dp", bits), one, swap(one, "wide", 1)]

    back, sums = call(
        functools.partial(back_kernel, features),
        (shape((slot_count, units), f32), shape((slot_count // LANES, LANES), f32)),
        (2 * slot_count * units * features, 2 * units * features),
        held,
        rest,
        weight,
        hidden,
    )
    grad_a, grad_b, scaled = call(
        functools.partial(grads_kernel, order, rows, features),
        (shape((slot_count, units), bf16),) * 3,
        (30 * slot_count * units, 12 * slot_count * units),
        held,
        rest,
        back,
        hidden,
        pre_gate,
        pre_up,
    )
    grad_down = call(
        functools.partial(down_kernel, dp_count - 1),
        shape((units, columns), bf16),
        (2 * dp_count * slot_count * units * columns, 4 * units * columns),
        scaled,
        held,
        rest,
        *others,
    )
    found = sums[None]
    back_order = [(0, 0)]
    for axis, bits in (
        [("wide", 1)]
        + [("wide", b) for b in wide_bits]
        + [("narrow", 1 << b) for b in range(narrow_count.bit_length() - 1)]
    ):
        found = jnp.concatenate([found, swap(found, axis, bits)], axis=0)
        step = (bits, 0) if axis == "wide" else (0, bits)
        back_order += [(w ^ step[0], n ^ step[1]) for w, n in back_order]
    picked = call(
        functools.partial(pick_kernel, order, tuple(back_order), rows),
        shape(routes_t.shape, f32),
        (slot_count, slot_count),
        routes_t,
        found,
    )
    return (grad_down[None], grad_a[None, None], grad_b[None, None], picked.T)


def shards(out_grad, routes, gates, pre_gate, pre_up, down_weight):
    wide_count = lax.axis_size("wide")
    narrow_count = lax.axis_size("narrow")
    experts = wide_count * narrow_count
    rows = out_grad.shape[0]
    slot_count = pre_gate.shape[2]
    whole_blocks = (
        slot_count == experts * rows
        and wide_count > 1
        and all(n & (n - 1) == 0 for n in (lax.axis_size("dp"), wide_count, narrow_count))
        and experts <= LANES
        and LANES % rows == 0
        and (slot_count // 2) % LANES == 0
    )
    plan = shards_gather if whole_blocks else shards_exchange
    return plan(out_grad, routes, gates, pre_gate, pre_up, down_weight)


def solution(mesh):
    placed = (
        P(("dp", "wide", "narrow"), None),
        P(("dp", "wide", "narrow"), None),
        P(("dp", "wide", "narrow"), None),
        P("dp", ("wide", "narrow"), None, None),
        P("dp", ("wide", "narrow"), None, None),
        P(("wide", "narrow"), None, None),
    )
    return jax.shard_map(
        shards,
        mesh=mesh,
        in_specs=placed,
        out_specs=(
            P(("wide", "narrow"), None, "dp"),
            P("dp", ("wide", "narrow"), None, None),
            P("dp", ("wide", "narrow"), None, None),
            P(("dp", "wide", "narrow"), None),
        ),
        check_vma=False,
    )
```

```python
import functools

import jax
import jax.numpy as jnp
from jax import lax
from jax.experimental import pallas as pl
from jax.experimental.pallas import tpu as pltpu
from jax.sharding import PartitionSpec as P

LANES = 128
FIRST_LIMIT = 16 * 1024 * 1024
VMEM_LIMIT = 24 * 1024 * 1024


def shards_exchange(out_grad, routes, gates, pre_gate, pre_up, down_weight):
    wide_count = lax.axis_size("wide")
    narrow_count = lax.axis_size("narrow")
    experts = wide_count * narrow_count
    token_count, top_count = routes.shape
    slot_count = pre_gate.shape[2]
    capacity = slot_count // experts
    expert_ids = jnp.arange(experts, dtype=jnp.int32)
    named_hits = (routes[:, :, None] == expert_ids[None, None, :]).astype(jnp.int32)
    hit_counts = jnp.sum(named_hits, axis=1)
    before = jnp.cumsum(hit_counts, axis=0) - hit_counts
    position = jnp.sum(named_hits * before[:, None, :], axis=2)
    target = routes * capacity + position
    slot_ids = jnp.arange(slot_count, dtype=jnp.int32)
    placed = target[:, :, None] == slot_ids[None, None, :]
    choose = jnp.sum(placed.astype(jnp.bfloat16), axis=1)
    outgoing = lax.dot_general(
        choose, out_grad, (((0,), (0,)), ((), ())), preferred_element_type=jnp.float32
    ).astype(jnp.bfloat16)
    gate_out = jnp.sum(
        jnp.where(placed, gates[:, :, None].astype(jnp.float32), 0.0), axis=(0, 1)
    ).astype(jnp.bfloat16)
    outgoing = outgoing.reshape(wide_count, narrow_count, capacity, outgoing.shape[1])
    gate_out = gate_out.reshape(wide_count, narrow_count, capacity)
    incoming, gate_in = (
        lax.all_to_all(
            lax.all_to_all(outgoing, "wide", split_axis=0, concat_axis=0, tiled=True),
            "narrow",
            split_axis=1,
            concat_axis=1,
            tiled=True,
        ),
        lax.all_to_all(
            lax.all_to_all(gate_out, "wide", split_axis=0, concat_axis=0, tiled=True),
            "narrow",
            split_axis=1,
            concat_axis=1,
            tiled=True,
        ),
    )
    routed_rows = incoming.reshape(slot_count, incoming.shape[3])
    gate_col = gate_in.reshape(slot_count).astype(jnp.float32)
    gate_pre = pre_gate[0, 0].astype(jnp.float32)
    up_pre = pre_up[0, 0].astype(jnp.float32)
    weight = down_weight[0]
    sigmoid_a = jax.nn.sigmoid(gate_pre)
    hidden = (gate_pre * sigmoid_a * up_pre).astype(jnp.bfloat16)
    back_prop = lax.dot_general(
        routed_rows, weight, (((1,), (1,)), ((), ())), preferred_element_type=jnp.float32
    )
    slot_grad = jnp.sum(hidden.astype(jnp.float32) * back_prop, axis=1)
    carried = gate_col[:, None] * back_prop
    grad_a = (carried * up_pre * sigmoid_a * (1.0 + gate_pre * (1.0 - sigmoid_a))).astype(
        jnp.bfloat16
    )
    grad_b = (carried * gate_pre * sigmoid_a).astype(jnp.bfloat16)
    scaled = (gate_col[:, None] * hidden.astype(jnp.float32)).astype(jnp.bfloat16)
    all_scaled = lax.all_gather(scaled, "dp", axis=0, tiled=True)
    columns = lax.all_to_all(routed_rows, "dp", split_axis=1, concat_axis=0, tiled=True)
    grad_down = lax.dot_general(
        all_scaled, columns, (((0,), (0,)), ((), ())), preferred_element_type=jnp.float32
    ).astype(jnp.bfloat16)
    slot_back = slot_grad.reshape(wide_count, narrow_count, capacity)
    returned = lax.all_to_all(
        lax.all_to_all(slot_back, "wide", split_axis=0, concat_axis=0, tiled=True),
        "narrow",
        split_axis=1,
        concat_axis=1,
        tiled=True,
    )
    grad_gates = jnp.take(returned.reshape(slot_count), target.reshape(-1)).reshape(
        token_count, top_count
    )
    return (grad_down[None], grad_a[None, None], grad_b[None, None], grad_gates)


def swap(x, axis, bits):
    count = lax.axis_size(axis)
    return lax.ppermute(x, axis, [(i, i ^ bits) for i in range(count)])


def after(x, *done):
    return lax.optimization_barrier((x,) + done)[0]


def call(kernel, outs, cost, *args, hbm=0, scratch=(), deps=(), limit=VMEM_LIMIT):
    flops, moved = cost
    body = kernel
    if deps:

        def body(*refs):
            return kernel(*refs[: len(args)], *refs[len(args) + len(deps) :])

    return pl.pallas_call(
        body,
        out_shape=outs,
        in_specs=[pl.BlockSpec(memory_space=pltpu.HBM)] * hbm
        + [pl.BlockSpec(memory_space=pltpu.VMEM)] * (len(args) - hbm)
        + [pl.BlockSpec(memory_space=pl.ANY)] * len(deps),
        out_specs=jax.tree.map(lambda _: pl.BlockSpec(memory_space=pltpu.VMEM), outs),
        scratch_shapes=scratch,
        compiler_params=pltpu.CompilerParams(vmem_limit_bytes=limit),
        cost_estimate=pl.CostEstimate(flops=flops, bytes_accessed=moved, transcendentals=0),
    )(*args, *deps)


def peer(xors):
    wide_bits, narrow_bits = xors
    return (lax.axis_index("wide") ^ wide_bits) * lax.axis_size("narrow") + (
        lax.axis_index("narrow") ^ narrow_bits
    )


def first_kernel(
    order,
    grad_hbm,
    routes_hbm,
    gates_hbm,
    pre_gate_hbm,
    pre_up_hbm,
    out_ref,
    hidden_ref,
    rest_ref,
    routes_ref,
    gates_ref,
    pre_gate_ref,
    pre_up_ref,
    sems,
):
    rows, features = grad_hbm.shape
    copies = [
        pltpu.make_async_copy(source, target, sems.at[at])
        for at, (source, target) in enumerate(
            (
                (routes_hbm, routes_ref),
                (gates_hbm, gates_ref),
                (grad_hbm, out_ref.at[:, pl.ds(0, features)]),
                (pre_gate_hbm, pre_gate_ref),
                (pre_up_hbm, pre_up_ref),
            )
        )
    ]
    for copy in copies:
        copy.start()
    copies[0].wait()
    copies[1].wait()
    routes = routes_ref[...]
    gates = gates_ref[...].astype(jnp.float32)
    ids = lax.broadcasted_iota(jnp.int32, (LANES, rows), 0)
    table = jnp.zeros((LANES, rows), jnp.float32)
    for k in range(routes.shape[0]):
        table = table + jnp.where(ids == routes[k : k + 1, :], gates[k : k + 1, :], 0.0)
    table = jnp.concatenate([table, jnp.zeros((LANES, LANES - rows), jnp.float32)], axis=1)
    out_ref[:, features:] = table.T[:rows, :].astype(out_ref.dtype)
    for copy in copies[2:]:
        copy.wait()
    half = len(order) // 2
    for place, xors in enumerate(order):
        source = pl.ds(pl.multiple_of(peer(xors) * rows, rows), rows)
        value = pre_gate_ref[source, :].astype(jnp.float32)
        up = pre_up_ref[source, :].astype(jnp.float32)
        result = (value * jax.nn.sigmoid(value) * up).astype(hidden_ref.dtype)
        hidden_ref[place * rows : (place + 1) * rows, :] = result
        if place >= half:
            rest_ref[(place - half) * rows : (place - half + 1) * rows, :] = result


def back_kernel(
    features,
    held_ref,
    weight_ref,
    other_weight_ref,
    hidden_ref,
    other_hidden_ref,
    back_ref,
    other_back_ref,
    sums_ref,
):
    rows = held_ref.shape[0]
    for expert, (matrix_ref, act_ref, result_ref) in enumerate(
        (
            (weight_ref, hidden_ref, back_ref),
            (other_weight_ref, other_hidden_ref, other_back_ref),
        )
    ):
        back = lax.dot_general(
            held_ref[:, :features],
            matrix_ref[...],
            (((1,), (1,)), ((), ())),
            preferred_element_type=jnp.float32,
        )
        result_ref[...] = back
        product = act_ref[:rows, :].astype(jnp.float32) * back
        folded = product[:, :LANES]
        for at in range(LANES, product.shape[1], LANES):
            folded = folded + product[:, at : at + LANES]
        for at in range(0, rows, LANES):
            row = (expert * rows + at) // LANES
            sums_ref[row : row + 1, :] = jnp.sum(
                folded[at : at + LANES, :].T, axis=0, keepdims=True
            )


def own_gates(table):
    lane = lax.broadcasted_iota(jnp.int32, table.shape, 1)
    return jnp.sum(
        jnp.where(lane == peer((0, 0)), table.astype(jnp.float32), 0.0), axis=1, keepdims=True
    )


def grads_kernel(
    order,
    rows,
    features,
    held_ref,
    rest_ref,
    back_ref,
    rest_back_ref,
    hidden_ref,
    pre_gate_ref,
    pre_up_ref,
    grad_gate_ref,
    grad_up_ref,
    scaled_ref,
):
    half = len(order) // 2
    for place, xors in enumerate(order):
        tokens_ref, products_ref = ((held_ref, back_ref), (rest_ref, rest_back_ref))[place // half]
        there = slice((place % half) * rows, (place % half + 1) * rows)
        gate = own_gates(tokens_ref[there, features:])
        here = slice(place * rows, (place + 1) * rows)
        source = pl.ds(pl.multiple_of(peer(xors) * rows, rows), rows)
        value = pre_gate_ref[source, :].astype(jnp.float32)
        up = pre_up_ref[source, :].astype(jnp.float32)
        sig = jax.nn.sigmoid(value)
        carried = gate * products_ref[there, :]
        grad_gate_ref[source, :] = (carried * up * sig * (1.0 + value * (1.0 - sig))).astype(
            grad_gate_ref.dtype
        )
        grad_up_ref[source, :] = (carried * value * sig).astype(grad_up_ref.dtype)
        scaled_ref[here, :] = (gate * hidden_ref[here, :].astype(jnp.float32)).astype(
            scaled_ref.dtype
        )


def down_kernel(pairs, scaled_ref, held_ref, rest_ref, *refs):
    out_ref, token_ref = refs[-2:]
    token_ref[...] = jnp.zeros(token_ref.shape, token_ref.dtype)
    columns = out_ref.shape[1]
    mine = pl.ds(pl.multiple_of(lax.axis_index("dp") * columns, columns), columns)
    scaled = [scaled_ref[...]]
    tokens = [held_ref[:, mine], rest_ref[:, mine]]
    for pair in range(pairs):
        hidden_ref, one_ref, two_ref = refs[3 * pair : 3 * pair + 3]
        gate = jnp.concatenate(
            [own_gates(one_ref[:, columns:]), own_gates(two_ref[:, columns:])], axis=0
        )
        scaled.append((gate * hidden_ref[...].astype(jnp.float32)).astype(scaled_ref.dtype))
        tokens += [one_ref[:, :columns], two_ref[:, :columns]]
    out_ref[...] = lax.dot_general(
        jnp.concatenate(scaled, axis=0),
        jnp.concatenate(tokens, axis=0),
        (((0,), (0,)), ((), ())),
        preferred_element_type=jnp.float32,
    ).astype(out_ref.dtype)


def pick_kernel(order, back_order, rows, routes_ref, sums_ref, out_ref):
    routes = routes_ref[...]
    total = jnp.zeros(out_ref.shape, jnp.float32)
    per = sums_ref.shape[1] // 2
    for line, (wide_bits, narrow_bits) in enumerate(back_order):
        start = order.index((wide_bits, narrow_bits)) * rows
        at = start % LANES
        for expert in range(2):
            row = expert * per + start // LANES
            found = sums_ref[line, row : row + 1, :][:, at : at + rows]
            chosen = routes == peer((wide_bits ^ expert, narrow_bits))
            total = total + jnp.where(chosen, found, 0.0)
    out_ref[...] = total


def shards_gather(out_grad, routes, gates, pre_gate, pre_up, down_weight):
    dp_count = lax.axis_size("dp")
    wide_count = lax.axis_size("wide")
    narrow_count = lax.axis_size("narrow")
    rows, features = out_grad.shape
    slot_count, units = pre_gate.shape[2:]
    half_count = slot_count // 2
    columns = features // dp_count
    routes_t = routes.T
    gates_t = gates.T
    pre_gate = pre_gate[0, 0]
    pre_up = pre_up[0, 0]
    weight = down_weight[0]
    bf16, f32 = jnp.bfloat16, jnp.float32
    shape = jax.ShapeDtypeStruct

    near = max(narrow_count // 2, 1)
    wide_bits = [1 << b for b in range(1, wide_count.bit_length() - 1)]
    order = [(0, bits) for bits in range(narrow_count)]
    for bits in wide_bits + [1]:
        order += [(w ^ bits, n) for w, n in order]
    order = tuple(order)

    payload, hidden, rest_hidden = call(
        functools.partial(first_kernel, order),
        (
            shape((rows, features + LANES), bf16),
            shape((slot_count, units), bf16),
            shape((half_count, units), bf16),
        ),
        (20 * slot_count * units, 6 * slot_count * units),
        *(
            pltpu.with_memory_space_constraint(x, pltpu.HBM)
            for x in (out_grad, routes_t, gates_t, pre_gate, pre_up)
        ),
        hbm=5,
        limit=FIRST_LIMIT,
        scratch=[
            pltpu.VMEM(routes_t.shape, routes_t.dtype),
            pltpu.VMEM(gates_t.shape, gates_t.dtype),
            pltpu.VMEM(pre_gate.shape, pre_gate.dtype),
            pltpu.VMEM(pre_up.shape, pre_up.dtype),
            pltpu.SemaphoreType.DMA((5,)),
        ],
    )
    along = [payload] + [swap(payload, "narrow", bits) for bits in range(1, narrow_count)]
    groups = [jnp.concatenate(along[:near], axis=0)]
    if along[near:]:
        groups.append(jnp.concatenate(along[near:], axis=0))
    for bits in wide_bits:
        groups += [swap(group, "wide", bits) for group in groups]
    held = jnp.concatenate(groups, axis=0)
    late = along[near % len(along)]
    other_weight = swap(weight, "wide", 1)
    other_hidden = swap(after(rest_hidden, late), "wide", 1)
    over = [swap(after(hidden, late), "dp", bits) for bits in range(1, dp_count)]
    back, other_back, sums = call(
        functools.partial(back_kernel, features),
        (
            shape((half_count, units), f32),
            shape((half_count, units), f32),
            shape((slot_count // LANES, LANES), f32),
        ),
        (2 * slot_count * units * features, 4 * units * features),
        held,
        weight,
        other_weight,
        hidden,
        other_hidden,
    )
    steps = [("wide", b) for b in wide_bits] + [
        ("narrow", 1 << b) for b in range(narrow_count.bit_length() - 1)
    ]
    found = sums[None]
    back_order = [(0, 0)]
    waits = []
    for axis, bits in steps:
        found = jnp.concatenate([after(found, *waits), swap(found, axis, bits)], axis=0)
        step = (bits, 0) if axis == "wide" else (0, bits)
        back_order += [(w ^ step[0], n ^ step[1]) for w, n in back_order]
        if len(back_order) == 2:
            rest = swap(after(held, sums), "wide", 1)
            rest_back = swap(other_back, "wide", 1)
            crossed = []
            for bits in range(1, dp_count):
                partner = lax.axis_index("dp") ^ bits
                cut = lax.dynamic_slice_in_dim(
                    held[:, :features], partner * columns, columns, axis=1
                )
                cut = jnp.concatenate([cut, held[:, features:]], axis=1)
                crossed.append(swap(after(cut, found, *over), "dp", bits))
        if len(back_order) == 4:
            grad_a, grad_b, scaled = call(
                functools.partial(grads_kernel, order, rows, features),
                (shape((slot_count, units), bf16),) * 3,
                (30 * slot_count * units, 12 * slot_count * units),
                held,
                rest,
                back,
                rest_back,
                hidden,
                pre_gate,
                pre_up,
            )
            waits = [scaled]
            half_found = found
    others = []
    for bits in range(1, dp_count):
        one = after(crossed[bits - 1], half_found)
        others += [over[bits - 1], one, swap(one, "wide", 1)]
    grad_down, token = call(
        functools.partial(down_kernel, dp_count - 1),
        (shape((units, columns), bf16), shape((8, LANES), f32)),
        (2 * dp_count * slot_count * units * columns, 4 * units * columns),
        scaled,
        held,
        rest,
        *others,
    )
    picked = call(
        functools.partial(pick_kernel, order, tuple(back_order), rows),
        shape(routes_t.shape, f32),
        (slot_count, slot_count),
        routes_t,
        found,
        deps=(token,),
    )
    return (grad_down[None], grad_a[None, None], grad_b[None, None], picked.T)


def shards(out_grad, routes, gates, pre_gate, pre_up, down_weight):
    wide_count = lax.axis_size("wide")
    narrow_count = lax.axis_size("narrow")
    experts = wide_count * narrow_count
    rows = out_grad.shape[0]
    slot_count = pre_gate.shape[2]
    whole_blocks = (
        slot_count == experts * rows
        and wide_count > 1
        and all(n & (n - 1) == 0 for n in (lax.axis_size("dp"), wide_count, narrow_count))
        and experts <= LANES
        and LANES % rows == 0
        and (slot_count // 2) % LANES == 0
    )
    plan = shards_gather if whole_blocks else shards_exchange
    return plan(out_grad, routes, gates, pre_gate, pre_up, down_weight)


def solution(mesh):
    placed = (
        P(("dp", "wide", "narrow"), None),
        P(("dp", "wide", "narrow"), None),
        P(("dp", "wide", "narrow"), None),
        P("dp", ("wide", "narrow"), None, None),
        P("dp", ("wide", "narrow"), None, None),
        P(("wide", "narrow"), None, None),
    )
    return jax.shard_map(
        shards,
        mesh=mesh,
        in_specs=placed,
        out_specs=(
            P(("wide", "narrow"), None, "dp"),
            P("dp", ("wide", "narrow"), None, None),
            P("dp", ("wide", "narrow"), None, None),
            P(("dp", "wide", "narrow"), None),
        ),
        check_vma=False,
    )
```

```python
import functools

import jax
import jax.numpy as jnp
from jax import lax
from jax.experimental import pallas as pl
from jax.experimental.pallas import tpu as pltpu
from jax.sharding import PartitionSpec as P

LANES = 128
VMEM_LIMIT = 14 * 1024 * 1024


def shards_exchange(out_grad, routes, gates, pre_gate, pre_up, down_weight):
    wide_count = lax.axis_size("wide")
    narrow_count = lax.axis_size("narrow")
    experts = wide_count * narrow_count
    token_count, top_count = routes.shape
    slot_count = pre_gate.shape[2]
    capacity = slot_count // experts
    expert_ids = jnp.arange(experts, dtype=jnp.int32)
    named_hits = (routes[:, :, None] == expert_ids[None, None, :]).astype(jnp.int32)
    hit_counts = jnp.sum(named_hits, axis=1)
    before = jnp.cumsum(hit_counts, axis=0) - hit_counts
    position = jnp.sum(named_hits * before[:, None, :], axis=2)
    target = routes * capacity + position
    slot_ids = jnp.arange(slot_count, dtype=jnp.int32)
    placed = target[:, :, None] == slot_ids[None, None, :]
    choose = jnp.sum(placed.astype(jnp.bfloat16), axis=1)
    outgoing = lax.dot_general(
        choose, out_grad, (((0,), (0,)), ((), ())), preferred_element_type=jnp.float32
    ).astype(jnp.bfloat16)
    gate_out = jnp.sum(
        jnp.where(placed, gates[:, :, None].astype(jnp.float32), 0.0), axis=(0, 1)
    ).astype(jnp.bfloat16)
    outgoing = outgoing.reshape(wide_count, narrow_count, capacity, outgoing.shape[1])
    gate_out = gate_out.reshape(wide_count, narrow_count, capacity)
    incoming, gate_in = (
        lax.all_to_all(
            lax.all_to_all(outgoing, "wide", split_axis=0, concat_axis=0, tiled=True),
            "narrow",
            split_axis=1,
            concat_axis=1,
            tiled=True,
        ),
        lax.all_to_all(
            lax.all_to_all(gate_out, "wide", split_axis=0, concat_axis=0, tiled=True),
            "narrow",
            split_axis=1,
            concat_axis=1,
            tiled=True,
        ),
    )
    routed_rows = incoming.reshape(slot_count, incoming.shape[3])
    gate_col = gate_in.reshape(slot_count).astype(jnp.float32)
    gate_pre = pre_gate[0, 0].astype(jnp.float32)
    up_pre = pre_up[0, 0].astype(jnp.float32)
    weight = down_weight[0]
    sigmoid_a = jax.nn.sigmoid(gate_pre)
    hidden = (gate_pre * sigmoid_a * up_pre).astype(jnp.bfloat16)
    back_prop = lax.dot_general(
        routed_rows, weight, (((1,), (1,)), ((), ())), preferred_element_type=jnp.float32
    )
    slot_grad = jnp.sum(hidden.astype(jnp.float32) * back_prop, axis=1)
    carried = gate_col[:, None] * back_prop
    grad_a = (carried * up_pre * sigmoid_a * (1.0 + gate_pre * (1.0 - sigmoid_a))).astype(
        jnp.bfloat16
    )
    grad_b = (carried * gate_pre * sigmoid_a).astype(jnp.bfloat16)
    scaled = (gate_col[:, None] * hidden.astype(jnp.float32)).astype(jnp.bfloat16)
    all_scaled = lax.all_gather(scaled, "dp", axis=0, tiled=True)
    columns = lax.all_to_all(routed_rows, "dp", split_axis=1, concat_axis=0, tiled=True)
    grad_down = lax.dot_general(
        all_scaled, columns, (((0,), (0,)), ((), ())), preferred_element_type=jnp.float32
    ).astype(jnp.bfloat16)
    slot_back = slot_grad.reshape(wide_count, narrow_count, capacity)
    returned = lax.all_to_all(
        lax.all_to_all(slot_back, "wide", split_axis=0, concat_axis=0, tiled=True),
        "narrow",
        split_axis=1,
        concat_axis=1,
        tiled=True,
    )
    grad_gates = jnp.take(returned.reshape(slot_count), target.reshape(-1)).reshape(
        token_count, top_count
    )
    return (grad_down[None], grad_a[None, None], grad_b[None, None], grad_gates)


def swap(x, axis, bits):
    count = lax.axis_size(axis)
    return lax.ppermute(x, axis, [(i, i ^ bits) for i in range(count)])


def after(x, *done):
    return lax.optimization_barrier((x,) + done)[0]


def call(kernel, outs, cost, *args, hbm=0, scratch=(), deps=(), limit=VMEM_LIMIT):
    flops, moved = cost
    body = kernel
    if deps:

        def body(*refs):
            return kernel(*refs[: len(args)], *refs[len(args) + len(deps) :])

    return pl.pallas_call(
        body,
        out_shape=outs,
        in_specs=[pl.BlockSpec(memory_space=pltpu.HBM)] * hbm
        + [pl.BlockSpec(memory_space=pltpu.VMEM)] * (len(args) - hbm)
        + [pl.BlockSpec(memory_space=pl.ANY)] * len(deps),
        out_specs=jax.tree.map(lambda _: pl.BlockSpec(memory_space=pltpu.VMEM), outs),
        scratch_shapes=scratch,
        compiler_params=pltpu.CompilerParams(vmem_limit_bytes=limit),
        cost_estimate=pl.CostEstimate(flops=flops, bytes_accessed=moved, transcendentals=0),
    )(*args, *deps)


def in_hbm(*arrays):
    return [pltpu.with_memory_space_constraint(x, pltpu.HBM) for x in arrays]


def peer(xors):
    wide_bits, narrow_bits = xors
    return (lax.axis_index("wide") ^ wide_bits) * lax.axis_size("narrow") + (
        lax.axis_index("narrow") ^ narrow_bits
    )


def first_kernel(
    grad_hbm, routes_hbm, gates_hbm, out_ref, token_ref, routes_ref, gates_ref, sems
):
    rows, features = grad_hbm.shape
    token_ref[...] = jnp.zeros(token_ref.shape, token_ref.dtype)
    copies = [
        pltpu.make_async_copy(routes_hbm, routes_ref, sems.at[0]),
        pltpu.make_async_copy(gates_hbm, gates_ref, sems.at[1]),
        pltpu.make_async_copy(grad_hbm, out_ref.at[:, pl.ds(0, features)], sems.at[2]),
    ]
    for copy in copies:
        copy.start()
    copies[0].wait()
    copies[1].wait()
    routes = routes_ref[...]
    gates = gates_ref[...].astype(jnp.float32)
    ids = lax.broadcasted_iota(jnp.int32, (LANES, rows), 0)
    table = jnp.zeros((LANES, rows), jnp.float32)
    for k in range(routes.shape[0]):
        table = table + jnp.where(ids == routes[k : k + 1, :], gates[k : k + 1, :], 0.0)
    table = jnp.concatenate([table, jnp.zeros((LANES, LANES - rows), jnp.float32)], axis=1)
    out_ref[:, features:] = table.T[:rows, :].astype(out_ref.dtype)
    copies[2].wait()


def hidden_kernel(
    order, rows, pre_gate_hbm, pre_up_hbm, hidden_ref, rest_ref, pre_gate_ref, pre_up_ref, sems
):
    copies = [
        pltpu.make_async_copy(pre_gate_hbm, pre_gate_ref, sems.at[0]),
        pltpu.make_async_copy(pre_up_hbm, pre_up_ref, sems.at[1]),
    ]
    for copy in copies:
        copy.start()
    for copy in copies:
        copy.wait()
    half = len(order) // 2
    for place, xors in enumerate(order):
        source = pl.ds(pl.multiple_of(peer(xors) * rows, rows), rows)
        value = pre_gate_ref[source, :].astype(jnp.float32)
        up = pre_up_ref[source, :].astype(jnp.float32)
        result = (value * jax.nn.sigmoid(value) * up).astype(hidden_ref.dtype)
        hidden_ref[place * rows : (place + 1) * rows, :] = result
        if place >= half:
            rest_ref[(place - half) * rows : (place - half + 1) * rows, :] = result


def turn_kernel(one_hbm, two_hbm, one_out, two_out, one_ref, two_ref, sems):
    units, features = one_ref.shape
    moves = [
        (at, source, held, out)
        for source, held, out in ((one_hbm, one_ref, one_out), (two_hbm, two_ref, two_out))
        for at in range(0, units, LANES)
    ]
    copies = [
        pltpu.make_async_copy(
            source.at[pl.ds(at, LANES)], held.at[pl.ds(at, LANES)], sems.at[step]
        )
        for step, (at, source, held, _) in enumerate(moves)
    ]
    for copy in copies:
        copy.start()
    for copy, (at, _, held, out) in zip(copies, moves):
        copy.wait()
        for to in range(0, features, LANES):
            out[to : to + LANES, at : at + LANES] = held[at : at + LANES, to : to + LANES].T


def back_kernel(
    features,
    held_ref,
    turned_ref,
    other_turned_ref,
    hidden_ref,
    other_hidden_ref,
    back_ref,
    other_back_ref,
    sums_ref,
):
    rows = held_ref.shape[0]
    for expert, (matrix_ref, act_ref, result_ref) in enumerate(
        ((turned_ref, hidden_ref, back_ref), (other_turned_ref, other_hidden_ref, other_back_ref))
    ):
        back = jnp.dot(
            held_ref[:, :features], matrix_ref[...], preferred_element_type=jnp.float32
        )
        result_ref[...] = back
        product = act_ref[:rows, :].astype(jnp.float32) * back
        folded = product[:, :LANES]
        for at in range(LANES, product.shape[1], LANES):
            folded = folded + product[:, at : at + LANES]
        for at in range(0, rows, LANES):
            row = (expert * rows + at) // LANES
            sums_ref[row : row + 1, :] = jnp.sum(
                folded[at : at + LANES, :].T, axis=0, keepdims=True
            )


def own_gates(table):
    lane = lax.broadcasted_iota(jnp.int32, table.shape, 1)
    return jnp.sum(
        jnp.where(lane == peer((0, 0)), table.astype(jnp.float32), 0.0), axis=1, keepdims=True
    )


def grads_kernel(
    order,
    rows,
    features,
    held_ref,
    rest_ref,
    back_ref,
    rest_back_ref,
    hidden_ref,
    pre_gate_ref,
    pre_up_ref,
    grad_gate_ref,
    grad_up_ref,
    scaled_ref,
):
    half = len(order) // 2
    for place, xors in enumerate(order):
        tokens_ref, products_ref = ((held_ref, back_ref), (rest_ref, rest_back_ref))[place // half]
        there = slice((place % half) * rows, (place % half + 1) * rows)
        gate = own_gates(tokens_ref[there, features:])
        here = slice(place * rows, (place + 1) * rows)
        source = pl.ds(pl.multiple_of(peer(xors) * rows, rows), rows)
        value = pre_gate_ref[source, :].astype(jnp.float32)
        up = pre_up_ref[source, :].astype(jnp.float32)
        sig = jax.nn.sigmoid(value)
        carried = gate * products_ref[there, :]
        grad_gate_ref[source, :] = (carried * up * sig * (1.0 + value * (1.0 - sig))).astype(
            grad_gate_ref.dtype
        )
        grad_up_ref[source, :] = (carried * value * sig).astype(grad_up_ref.dtype)
        scaled_ref[here, :] = (gate * hidden_ref[here, :].astype(jnp.float32)).astype(
            scaled_ref.dtype
        )


def down_kernel(pairs, scaled_ref, held_ref, rest_ref, *refs):
    out_ref = refs[-1]
    columns = out_ref.shape[1]
    mine = pl.ds(pl.multiple_of(lax.axis_index("dp") * columns, columns), columns)
    scaled = [scaled_ref[...]]
    tokens = [held_ref[:, mine], rest_ref[:, mine]]
    for pair in range(pairs):
        hidden_ref, one_ref, two_ref = refs[3 * pair : 3 * pair + 3]
        gate = jnp.concatenate(
            [own_gates(one_ref[:, columns:]), own_gates(two_ref[:, columns:])], axis=0
        )
        scaled.append((gate * hidden_ref[...].astype(jnp.float32)).astype(scaled_ref.dtype))
        tokens += [one_ref[:, :columns], two_ref[:, :columns]]
    out_ref[...] = lax.dot_general(
        jnp.concatenate(scaled, axis=0),
        jnp.concatenate(tokens, axis=0),
        (((0,), (0,)), ((), ())),
        preferred_element_type=jnp.float32,
    ).astype(out_ref.dtype)


def pick_kernel(order, back_order, rows, routes_ref, sums_ref, out_ref):
    routes = routes_ref[...]
    total = jnp.zeros(out_ref.shape, jnp.float32)
    per = sums_ref.shape[1] // 2
    for line, (wide_bits, narrow_bits) in enumerate(back_order):
        start = order.index((wide_bits, narrow_bits)) * rows
        at = start % LANES
        for expert in range(2):
            row = expert * per + start // LANES
            found = sums_ref[line, row : row + 1, :][:, at : at + rows]
            chosen = routes == peer((wide_bits ^ expert, narrow_bits))
            total = total + jnp.where(chosen, found, 0.0)
    out_ref[...] = total


def shards_gather(out_grad, routes, gates, pre_gate, pre_up, down_weight):
    dp_count = lax.axis_size("dp")
    wide_count = lax.axis_size("wide")
    narrow_count = lax.axis_size("narrow")
    rows, features = out_grad.shape
    slot_count, units = pre_gate.shape[2:]
    half_count = slot_count // 2
    columns = features // dp_count
    routes_t = routes.T
    gates_t = gates.T
    pre_gate = pre_gate[0, 0]
    pre_up = pre_up[0, 0]
    weight = down_weight[0]
    bf16, f32 = jnp.bfloat16, jnp.float32
    shape = jax.ShapeDtypeStruct

    near = max(narrow_count // 2, 1)
    wide_bits = [1 << b for b in range(1, wide_count.bit_length() - 1)]
    reach = [0] + list(range(near, narrow_count)) + list(range(1, near))
    order = [(0, bits) for bits in reach]
    for bits in wide_bits + [1]:
        order += [(w ^ bits, n) for w, n in order]
    order = tuple(order)

    other_weight = swap(weight, "wide", 1)
    payload, token = call(
        first_kernel,
        (shape((rows, features + LANES), bf16), shape((8, LANES), f32)),
        (rows * features, 4 * rows * features),
        *in_hbm(out_grad, routes_t, gates_t),
        hbm=3,
        scratch=[
            pltpu.VMEM(routes_t.shape, routes_t.dtype),
            pltpu.VMEM(gates_t.shape, gates_t.dtype),
            pltpu.SemaphoreType.DMA((3,)),
        ],
    )
    along = [swap(payload, "narrow", bits) if bits else payload for bits in reach]
    hidden, rest_hidden = call(
        functools.partial(hidden_kernel, order, rows),
        (shape((slot_count, units), bf16), shape((half_count, units), bf16)),
        (20 * slot_count * units, 6 * slot_count * units),
        *in_hbm(pre_gate, pre_up),
        hbm=2,
        deps=(token,),
        scratch=[
            pltpu.VMEM(pre_gate.shape, pre_gate.dtype),
            pltpu.VMEM(pre_up.shape, pre_up.dtype),
            pltpu.SemaphoreType.DMA((2,)),
        ],
    )
    turned = call(
        turn_kernel,
        (shape((features, units), bf16),) * 2,
        (0, 8 * features * units),
        *in_hbm(weight, other_weight),
        hbm=2,
        deps=(token,),
        scratch=[
            pltpu.VMEM(weight.shape, weight.dtype),
            pltpu.VMEM(weight.shape, weight.dtype),
            pltpu.SemaphoreType.DMA((2 * units // LANES,)),
        ],
    )
    over = [swap(after(hidden, *along[near:]), "dp", bits) for bits in range(1, dp_count)]
    other_hidden = swap(rest_hidden, "wide", 1)
    groups = [after(jnp.concatenate(along[:near], axis=0), hidden)]
    if along[near:]:
        groups.append(jnp.concatenate(along[near:], axis=0))
    for bits in wide_bits:
        groups += [swap(group, "wide", bits) for group in groups]
    held = jnp.concatenate([after(groups[0], *turned)] + groups[1:], axis=0)
    back, other_back, sums = call(
        functools.partial(back_kernel, features),
        (
            shape((half_count, units), f32),
            shape((half_count, units), f32),
            shape((slot_count // LANES, LANES), f32),
        ),
        (2 * slot_count * units * features, 4 * units * features),
        held,
        *turned,
        hidden,
        other_hidden,
    )
    steps = [("wide", b) for b in wide_bits] + [
        ("narrow", 1 << b) for b in range(narrow_count.bit_length() - 1)
    ]
    found = sums[None]
    back_order = [(0, 0)]
    waits = []
    for axis, bits in steps:
        found = after(found, *waits)
        kept = after(found, scaled) if len(back_order) >= 4 else found
        found = jnp.concatenate([kept, swap(found, axis, bits)], axis=0)
        step = (bits, 0) if axis == "wide" else (0, bits)
        back_order += [(w ^ step[0], n ^ step[1]) for w, n in back_order]
        if len(back_order) == 2:
            rest = swap(after(held, sums), "wide", 1)
            rest_back = swap(other_back, "wide", 1)
            crossed = []
            for bits in range(1, dp_count):
                partner = lax.axis_index("dp") ^ bits
                cut = lax.dynamic_slice_in_dim(
                    held[:, :features], partner * columns, columns, axis=1
                )
                cut = jnp.concatenate([cut, held[:, features:]], axis=1)
                crossed.append(swap(after(cut, sums), "dp", bits))
        if len(back_order) == 4:
            grad_a, grad_b, scaled = call(
                functools.partial(grads_kernel, order, rows, features),
                (shape((slot_count, units), bf16),) * 3,
                (30 * slot_count * units, 12 * slot_count * units),
                held,
                rest,
                back,
                rest_back,
                hidden,
                pre_gate,
                pre_up,
            )
            waits = [*over]
    others = []
    for bits in range(1, dp_count):
        one = after(crossed[bits - 1], found)
        others += [over[bits - 1], one, swap(one, "wide", 1)]
    grad_down = call(
        functools.partial(down_kernel, dp_count - 1),
        shape((units, columns), bf16),
        (2 * dp_count * slot_count * units * columns, 4 * units * columns),
        scaled,
        held,
        rest,
        *others,
    )
    picked = call(
        functools.partial(pick_kernel, order, tuple(back_order), rows),
        shape(routes_t.shape, f32),
        (slot_count, slot_count),
        routes_t,
        found,
    )
    return (grad_down[None], grad_a[None, None], grad_b[None, None], picked.T)


def shards(out_grad, routes, gates, pre_gate, pre_up, down_weight):
    wide_count = lax.axis_size("wide")
    narrow_count = lax.axis_size("narrow")
    experts = wide_count * narrow_count
    rows = out_grad.shape[0]
    slot_count = pre_gate.shape[2]
    whole_blocks = (
        slot_count == experts * rows
        and wide_count > 1
        and all(n & (n - 1) == 0 for n in (lax.axis_size("dp"), wide_count, narrow_count))
        and experts <= LANES
        and LANES % rows == 0
        and (slot_count // 2) % LANES == 0
    )
    plan = shards_gather if whole_blocks else shards_exchange
    return plan(out_grad, routes, gates, pre_gate, pre_up, down_weight)


def solution(mesh):
    placed = (
        P(("dp", "wide", "narrow"), None),
        P(("dp", "wide", "narrow"), None),
        P(("dp", "wide", "narrow"), None),
        P("dp", ("wide", "narrow"), None, None),
        P("dp", ("wide", "narrow"), None, None),
        P(("wide", "narrow"), None, None),
    )
    return jax.shard_map(
        shards,
        mesh=mesh,
        in_specs=placed,
        out_specs=(
            P(("wide", "narrow"), None, "dp"),
            P("dp", ("wide", "narrow"), None, None),
            P("dp", ("wide", "narrow"), None, None),
            P(("dp", "wide", "narrow"), None),
        ),
        check_vma=False,
    )
```

```python
import functools

import jax
import jax.numpy as jnp
from jax import lax
from jax.experimental import pallas as pl
from jax.experimental.pallas import tpu as pltpu
from jax.sharding import PartitionSpec as P

LANES = 128
PARTS = 4
VMEM_LIMIT = 14 * 1024 * 1024


def shards_exchange(out_grad, routes, gates, pre_gate, pre_up, down_weight):
    wide_count = lax.axis_size("wide")
    narrow_count = lax.axis_size("narrow")
    experts = wide_count * narrow_count
    token_count, top_count = routes.shape
    slot_count = pre_gate.shape[2]
    capacity = slot_count // experts
    expert_ids = jnp.arange(experts, dtype=jnp.int32)
    named_hits = (routes[:, :, None] == expert_ids[None, None, :]).astype(jnp.int32)
    hit_counts = jnp.sum(named_hits, axis=1)
    before = jnp.cumsum(hit_counts, axis=0) - hit_counts
    position = jnp.sum(named_hits * before[:, None, :], axis=2)
    target = routes * capacity + position
    slot_ids = jnp.arange(slot_count, dtype=jnp.int32)
    placed = target[:, :, None] == slot_ids[None, None, :]
    choose = jnp.sum(placed.astype(jnp.bfloat16), axis=1)
    outgoing = lax.dot_general(
        choose, out_grad, (((0,), (0,)), ((), ())), preferred_element_type=jnp.float32
    ).astype(jnp.bfloat16)
    gate_out = jnp.sum(
        jnp.where(placed, gates[:, :, None].astype(jnp.float32), 0.0), axis=(0, 1)
    ).astype(jnp.bfloat16)
    outgoing = outgoing.reshape(wide_count, narrow_count, capacity, outgoing.shape[1])
    gate_out = gate_out.reshape(wide_count, narrow_count, capacity)
    incoming, gate_in = (
        lax.all_to_all(
            lax.all_to_all(outgoing, "wide", split_axis=0, concat_axis=0, tiled=True),
            "narrow",
            split_axis=1,
            concat_axis=1,
            tiled=True,
        ),
        lax.all_to_all(
            lax.all_to_all(gate_out, "wide", split_axis=0, concat_axis=0, tiled=True),
            "narrow",
            split_axis=1,
            concat_axis=1,
            tiled=True,
        ),
    )
    routed_rows = incoming.reshape(slot_count, incoming.shape[3])
    gate_col = gate_in.reshape(slot_count).astype(jnp.float32)
    gate_pre = pre_gate[0, 0].astype(jnp.float32)
    up_pre = pre_up[0, 0].astype(jnp.float32)
    weight = down_weight[0]
    sigmoid_a = jax.nn.sigmoid(gate_pre)
    hidden = (gate_pre * sigmoid_a * up_pre).astype(jnp.bfloat16)
    back_prop = lax.dot_general(
        routed_rows, weight, (((1,), (1,)), ((), ())), preferred_element_type=jnp.float32
    )
    slot_grad = jnp.sum(hidden.astype(jnp.float32) * back_prop, axis=1)
    carried = gate_col[:, None] * back_prop
    grad_a = (carried * up_pre * sigmoid_a * (1.0 + gate_pre * (1.0 - sigmoid_a))).astype(
        jnp.bfloat16
    )
    grad_b = (carried * gate_pre * sigmoid_a).astype(jnp.bfloat16)
    scaled = (gate_col[:, None] * hidden.astype(jnp.float32)).astype(jnp.bfloat16)
    all_scaled = lax.all_gather(scaled, "dp", axis=0, tiled=True)
    columns = lax.all_to_all(routed_rows, "dp", split_axis=1, concat_axis=0, tiled=True)
    grad_down = lax.dot_general(
        all_scaled, columns, (((0,), (0,)), ((), ())), preferred_element_type=jnp.float32
    ).astype(jnp.bfloat16)
    slot_back = slot_grad.reshape(wide_count, narrow_count, capacity)
    returned = lax.all_to_all(
        lax.all_to_all(slot_back, "wide", split_axis=0, concat_axis=0, tiled=True),
        "narrow",
        split_axis=1,
        concat_axis=1,
        tiled=True,
    )
    grad_gates = jnp.take(returned.reshape(slot_count), target.reshape(-1)).reshape(
        token_count, top_count
    )
    return (grad_down[None], grad_a[None, None], grad_b[None, None], grad_gates)


def swap(x, axis, bits):
    count = lax.axis_size(axis)
    return lax.ppermute(x, axis, [(i, i ^ bits) for i in range(count)])


def after(x, *done):
    return lax.optimization_barrier((x,) + done)[0]


def call(kernel, outs, cost, *args, hbm=0, scratch=(), deps=(), out_space=pltpu.VMEM):
    flops, moved = cost
    body = kernel
    if deps:

        def body(*refs):
            return kernel(*refs[: len(args)], *refs[len(args) + len(deps) :])

    return pl.pallas_call(
        body,
        out_shape=outs,
        in_specs=[pl.BlockSpec(memory_space=pltpu.HBM)] * hbm
        + [pl.BlockSpec(memory_space=pltpu.VMEM)] * (len(args) - hbm)
        + [pl.BlockSpec(memory_space=pl.ANY)] * len(deps),
        out_specs=jax.tree.map(lambda _: pl.BlockSpec(memory_space=out_space), outs),
        scratch_shapes=scratch,
        compiler_params=pltpu.CompilerParams(vmem_limit_bytes=VMEM_LIMIT),
        cost_estimate=pl.CostEstimate(flops=flops, bytes_accessed=moved, transcendentals=0),
    )(*args, *deps)


def in_hbm(*arrays):
    return [pltpu.with_memory_space_constraint(x, pltpu.HBM) for x in arrays]


def peer(xors):
    wide_bits, narrow_bits = xors
    return (lax.axis_index("wide") ^ wide_bits) * lax.axis_size("narrow") + (
        lax.axis_index("narrow") ^ narrow_bits
    )


def first_kernel(
    order,
    grad_hbm,
    routes_hbm,
    gates_hbm,
    pre_gate_hbm,
    pre_up_hbm,
    out_ref,
    hidden_ref,
    rest_ref,
    token_ref,
    routes_ref,
    gates_ref,
    pre_gate_ref,
    pre_up_ref,
    sems,
):
    rows, features = grad_hbm.shape
    copies = [
        pltpu.make_async_copy(source, target, sems.at[at])
        for at, (source, target) in enumerate(
            (
                (routes_hbm, routes_ref),
                (gates_hbm, gates_ref),
                (grad_hbm, out_ref.at[:, pl.ds(0, features)]),
                (pre_gate_hbm, pre_gate_ref),
                (pre_up_hbm, pre_up_ref),
            )
        )
    ]
    for copy in copies:
        copy.start()
    token_ref[...] = jnp.zeros(token_ref.shape, token_ref.dtype)
    copies[0].wait()
    copies[1].wait()
    routes = routes_ref[...]
    gates = gates_ref[...].astype(jnp.float32)
    ids = lax.broadcasted_iota(jnp.int32, (LANES, rows), 0)
    table = jnp.zeros((LANES, rows), jnp.float32)
    for k in range(routes.shape[0]):
        table = table + jnp.where(ids == routes[k : k + 1, :], gates[k : k + 1, :], 0.0)
    table = jnp.concatenate([table, jnp.zeros((LANES, LANES - rows), jnp.float32)], axis=1)
    out_ref[:, features:] = table.T[:rows, :].astype(out_ref.dtype)
    for copy in copies[2:]:
        copy.wait()
    half = len(order) // 2
    for place, xors in enumerate(order):
        source = pl.ds(pl.multiple_of(peer(xors) * rows, rows), rows)
        value = pre_gate_ref[source, :].astype(jnp.float32)
        up = pre_up_ref[source, :].astype(jnp.float32)
        result = (value * jax.nn.sigmoid(value) * up).astype(hidden_ref.dtype)
        hidden_ref[place * rows : (place + 1) * rows, :] = result
        if place >= half:
            rest_ref[(place - half) * rows : (place - half + 1) * rows, :] = result


def turn_kernel(one_hbm, two_ref, *refs):
    one_ref, sems = refs[-2:]
    outs = refs[:-2]
    units, features = one_ref.shape
    cut = outs[0].shape[0]
    copies = [
        pltpu.make_async_copy(
            one_hbm.at[pl.ds(at, LANES)], one_ref.at[pl.ds(at, LANES)], sems.at[step]
        )
        for step, at in enumerate(range(0, units, LANES))
    ]
    for copy in copies:
        copy.start()
    for held, parts, waits in ((two_ref, outs[PARTS:], ()), (one_ref, outs[:PARTS], copies)):
        for step, at in enumerate(range(0, units, LANES)):
            if waits:
                waits[step].wait()
            for to in range(0, features, LANES):
                line = to % cut
                parts[to // cut][line : line + LANES, at : at + LANES] = held[
                    at : at + LANES, to : to + LANES
                ].T


def back_kernel(features, held_ref, hidden_ref, other_hidden_ref, *refs):
    back_ref, other_back_ref, sums_ref = refs[-3:]
    rows = held_ref.shape[0]
    for expert, (act_ref, result_ref) in enumerate(
        ((hidden_ref, back_ref), (other_hidden_ref, other_back_ref))
    ):
        back = jnp.zeros(result_ref.shape, jnp.float32)
        for part in range(PARTS):
            part_ref = refs[expert * PARTS + part]
            depth = part_ref.shape[0]
            back = back + jnp.dot(
                held_ref[:, part * depth : (part + 1) * depth],
                part_ref[...],
                preferred_element_type=jnp.float32,
            )
        result_ref[...] = back
        product = act_ref[:rows, :].astype(jnp.float32) * back
        folded = product[:, :LANES]
        for at in range(LANES, product.shape[1], LANES):
            folded = folded + product[:, at : at + LANES]
        for at in range(0, rows, LANES):
            row = (expert * rows + at) // LANES
            sums_ref[row : row + 1, :] = jnp.sum(
                folded[at : at + LANES, :].T, axis=0, keepdims=True
            )


def own_gates(table):
    lane = lax.broadcasted_iota(jnp.int32, table.shape, 1)
    return jnp.sum(
        jnp.where(lane == peer((0, 0)), table.astype(jnp.float32), 0.0), axis=1, keepdims=True
    )


def grads_kernel(
    order,
    rows,
    features,
    held_ref,
    rest_ref,
    back_ref,
    rest_back_ref,
    hidden_ref,
    pre_gate_ref,
    pre_up_ref,
    grad_gate_ref,
    grad_up_ref,
    scaled_ref,
):
    half = len(order) // 2
    for place, xors in enumerate(order):
        tokens_ref, products_ref = ((held_ref, back_ref), (rest_ref, rest_back_ref))[place // half]
        there = slice((place % half) * rows, (place % half + 1) * rows)
        gate = own_gates(tokens_ref[there, features:])
        here = slice(place * rows, (place + 1) * rows)
        source = pl.ds(pl.multiple_of(peer(xors) * rows, rows), rows)
        value = pre_gate_ref[source, :].astype(jnp.float32)
        up = pre_up_ref[source, :].astype(jnp.float32)
        sig = jax.nn.sigmoid(value)
        carried = gate * products_ref[there, :]
        grad_gate_ref[source, :] = (carried * up * sig * (1.0 + value * (1.0 - sig))).astype(
            grad_gate_ref.dtype
        )
        grad_up_ref[source, :] = (carried * value * sig).astype(grad_up_ref.dtype)
        scaled_ref[here, :] = (gate * hidden_ref[here, :].astype(jnp.float32)).astype(
            scaled_ref.dtype
        )


def down_kernel(pairs, scaled_ref, held_ref, rest_ref, *refs):
    out_ref, held_out_ref, sems = refs[-3:]
    columns = out_ref.shape[1]
    mine = pl.ds(pl.multiple_of(lax.axis_index("dp") * columns, columns), columns)
    scaled = [scaled_ref[...]]
    tokens = [held_ref[:, mine], rest_ref[:, mine]]
    for pair in range(pairs):
        hidden_ref, one_ref, two_ref = refs[3 * pair : 3 * pair + 3]
        gate = jnp.concatenate(
            [own_gates(one_ref[:, columns:]), own_gates(two_ref[:, columns:])], axis=0
        )
        scaled.append((gate * hidden_ref[...].astype(jnp.float32)).astype(scaled_ref.dtype))
        tokens += [one_ref[:, :columns], two_ref[:, :columns]]
    scaled = jnp.concatenate(scaled, axis=0)
    tokens = jnp.concatenate(tokens, axis=0)
    copies = []
    for at in range(0, out_ref.shape[0], 2 * LANES):
        here = pl.ds(at, 2 * LANES)
        held_out_ref[here, :] = lax.dot_general(
            scaled[:, at : at + 2 * LANES],
            tokens,
            (((0,), (0,)), ((), ())),
            preferred_element_type=jnp.float32,
        ).astype(out_ref.dtype)
        copies.append(
            pltpu.make_async_copy(held_out_ref.at[here], out_ref.at[here], sems.at[len(copies)])
        )
        copies[-1].start()
    for copy in copies:
        copy.wait()


def pick_kernel(order, back_order, rows, routes_ref, sums_ref, out_ref):
    routes = routes_ref[...]
    total = jnp.zeros(out_ref.shape, jnp.float32)
    per = sums_ref.shape[1] // 2
    for line, (wide_bits, narrow_bits) in enumerate(back_order):
        start = order.index((wide_bits, narrow_bits)) * rows
        at = start % LANES
        for expert in range(2):
            row = expert * per + start // LANES
            found = sums_ref[line, row : row + 1, :][:, at : at + rows]
            chosen = routes == peer((wide_bits ^ expert, narrow_bits))
            total = total + jnp.where(chosen, found, 0.0)
    out_ref[...] = total


def shards_gather(out_grad, routes, gates, pre_gate, pre_up, down_weight):
    dp_count = lax.axis_size("dp")
    wide_count = lax.axis_size("wide")
    narrow_count = lax.axis_size("narrow")
    rows, features = out_grad.shape
    slot_count, units = pre_gate.shape[2:]
    half_count = slot_count // 2
    columns = features // dp_count
    routes_t = routes.T
    gates_t = gates.T
    pre_gate = pre_gate[0, 0]
    pre_up = pre_up[0, 0]
    weight = down_weight[0]
    bf16, f32 = jnp.bfloat16, jnp.float32
    shape = jax.ShapeDtypeStruct

    near = max(narrow_count // 2, 1)
    wide_bits = [1 << b for b in range(1, wide_count.bit_length() - 1)]
    reach = [0] + list(range(near, narrow_count)) + list(range(1, near))
    order = [(0, bits) for bits in reach]
    for bits in wide_bits + [1]:
        order += [(w ^ bits, n) for w, n in order]
    order = tuple(order)

    other_weight = swap(weight, "wide", 1)
    payload, hidden, rest_hidden, token = call(
        functools.partial(first_kernel, order),
        (
            shape((rows, features + LANES), bf16),
            shape((slot_count, units), bf16),
            shape((half_count, units), bf16),
            shape((8, LANES), f32),
        ),
        (20 * slot_count * units, 6 * slot_count * units),
        *in_hbm(out_grad, routes_t, gates_t, pre_gate, pre_up),
        hbm=5,
        scratch=[
            pltpu.VMEM(routes_t.shape, routes_t.dtype),
            pltpu.VMEM(gates_t.shape, gates_t.dtype),
            pltpu.VMEM(pre_gate.shape, pre_gate.dtype),
            pltpu.VMEM(pre_up.shape, pre_up.dtype),
            pltpu.SemaphoreType.DMA((5,)),
        ],
    )
    along = [swap(payload, "narrow", bits) if bits else payload for bits in reach]
    turned = call(
        turn_kernel,
        (shape((features // PARTS, units), bf16),) * (2 * PARTS),
        (0, 8 * features * units),
        *in_hbm(weight),
        other_weight,
        hbm=1,
        deps=(token,),
        scratch=[
            pltpu.VMEM(weight.shape, weight.dtype),
            pltpu.SemaphoreType.DMA((units // LANES,)),
        ],
    )
    over = [swap(hidden, "dp", bits) for bits in range(1, dp_count)]
    other_hidden = swap(after(rest_hidden, *along[near:]), "wide", 1)
    groups = [jnp.concatenate(along[:near], axis=0)]
    if along[near:]:
        groups.append(jnp.concatenate(along[near:], axis=0))
    for bits in wide_bits:
        groups += [swap(group, "wide", bits) for group in groups]
    held = jnp.concatenate([after(groups[0], *turned, *over)] + groups[1:], axis=0)
    back, other_back, sums = call(
        functools.partial(back_kernel, features),
        (
            shape((half_count, units), f32),
            shape((half_count, units), f32),
            shape((slot_count // LANES, LANES), f32),
        ),
        (2 * slot_count * units * features, 4 * units * features),
        held,
        hidden,
        other_hidden,
        *turned,
    )
    found = sums[None]
    back_order = [(0, 0)]
    for bits in wide_bits:
        found = jnp.concatenate([found, swap(found, "wide", bits)], axis=0)
        back_order += [(w ^ bits, n) for w, n in back_order]
    rest = swap(after(held, sums), "wide", 1)
    rest_back = swap(other_back, "wide", 1)
    crossed = []
    for bits in range(1, dp_count):
        partner = lax.axis_index("dp") ^ bits
        cut = lax.dynamic_slice_in_dim(held[:, :features], partner * columns, columns, axis=1)
        cut = jnp.concatenate([cut, held[:, features:]], axis=1)
        crossed.append(swap(after(cut, sums), "dp", bits))
    grad_a, grad_b, scaled = call(
        functools.partial(grads_kernel, order, rows, features),
        (shape((slot_count, units), bf16),) * 3,
        (30 * slot_count * units, 12 * slot_count * units),
        held,
        rest,
        back,
        rest_back,
        hidden,
        pre_gate,
        pre_up,
    )
    mine = found
    parts = [swap(mine, "narrow", bits) for bits in reach[1:]]
    found = jnp.concatenate([after(mine, scaled)] + parts, axis=0)
    back_order = [(w, n ^ bits) for bits in reach for w, n in back_order]
    others = []
    for bits in range(1, dp_count):
        one = after(crossed[bits - 1], found)
        others += [over[bits - 1], one, swap(one, "wide", 1)]
    grad_down = call(
        functools.partial(down_kernel, dp_count - 1),
        shape((units, columns), bf16),
        (2 * dp_count * slot_count * units * columns, 4 * units * columns),
        scaled,
        held,
        rest,
        *others,
        out_space=pltpu.HBM,
        scratch=[
            pltpu.VMEM((units, columns), bf16),
            pltpu.SemaphoreType.DMA((units // (2 * LANES),)),
        ],
    )
    picked = call(
        functools.partial(pick_kernel, order, tuple(back_order), rows),
        shape(routes_t.shape, f32),
        (slot_count, slot_count),
        routes_t,
        found,
    )
    return (grad_down[None], grad_a[None, None], grad_b[None, None], picked.T)


def shards(out_grad, routes, gates, pre_gate, pre_up, down_weight):
    wide_count = lax.axis_size("wide")
    narrow_count = lax.axis_size("narrow")
    experts = wide_count * narrow_count
    rows = out_grad.shape[0]
    slot_count = pre_gate.shape[2]
    whole_blocks = (
        slot_count == experts * rows
        and wide_count > 1
        and all(n & (n - 1) == 0 for n in (lax.axis_size("dp"), wide_count, narrow_count))
        and experts <= LANES
        and LANES % rows == 0
        and (slot_count // 2) % LANES == 0
    )
    plan = shards_gather if whole_blocks else shards_exchange
    return plan(out_grad, routes, gates, pre_gate, pre_up, down_weight)


def solution(mesh):
    placed = (
        P(("dp", "wide", "narrow"), None),
        P(("dp", "wide", "narrow"), None),
        P(("dp", "wide", "narrow"), None),
        P("dp", ("wide", "narrow"), None, None),
        P("dp", ("wide", "narrow"), None, None),
        P(("wide", "narrow"), None, None),
    )
    return jax.shard_map(
        shards,
        mesh=mesh,
        in_specs=placed,
        out_specs=(
            P(("wide", "narrow"), None, "dp"),
            P("dp", ("wide", "narrow"), None, None),
            P("dp", ("wide", "narrow"), None, None),
            P(("dp", "wide", "narrow"), None),
        ),
        check_vma=False,
    )
```

```python
import functools

import jax
import jax.numpy as jnp
from jax import lax
from jax.experimental import pallas as pl
from jax.experimental.pallas import tpu as pltpu
from jax.sharding import PartitionSpec as P

LANES = 128
PIECES = 3
PARTS = 4
VMEM_LIMIT = 14 * 1024 * 1024


def shards_exchange(out_grad, routes, gates, pre_gate, pre_up, down_weight):
    wide_count = lax.axis_size("wide")
    narrow_count = lax.axis_size("narrow")
    experts = wide_count * narrow_count
    token_count, top_count = routes.shape
    slot_count = pre_gate.shape[2]
    capacity = slot_count // experts
    expert_ids = jnp.arange(experts, dtype=jnp.int32)
    named_hits = (routes[:, :, None] == expert_ids[None, None, :]).astype(jnp.int32)
    hit_counts = jnp.sum(named_hits, axis=1)
    before = jnp.cumsum(hit_counts, axis=0) - hit_counts
    position = jnp.sum(named_hits * before[:, None, :], axis=2)
    target = routes * capacity + position
    slot_ids = jnp.arange(slot_count, dtype=jnp.int32)
    placed = target[:, :, None] == slot_ids[None, None, :]
    choose = jnp.sum(placed.astype(jnp.bfloat16), axis=1)
    outgoing = lax.dot_general(
        choose, out_grad, (((0,), (0,)), ((), ())), preferred_element_type=jnp.float32
    ).astype(jnp.bfloat16)
    gate_out = jnp.sum(
        jnp.where(placed, gates[:, :, None].astype(jnp.float32), 0.0), axis=(0, 1)
    ).astype(jnp.bfloat16)
    outgoing = outgoing.reshape(wide_count, narrow_count, capacity, outgoing.shape[1])
    gate_out = gate_out.reshape(wide_count, narrow_count, capacity)
    incoming, gate_in = (
        lax.all_to_all(
            lax.all_to_all(outgoing, "wide", split_axis=0, concat_axis=0, tiled=True),
            "narrow",
            split_axis=1,
            concat_axis=1,
            tiled=True,
        ),
        lax.all_to_all(
            lax.all_to_all(gate_out, "wide", split_axis=0, concat_axis=0, tiled=True),
            "narrow",
            split_axis=1,
            concat_axis=1,
            tiled=True,
        ),
    )
    routed_rows = incoming.reshape(slot_count, incoming.shape[3])
    gate_col = gate_in.reshape(slot_count).astype(jnp.float32)
    gate_pre = pre_gate[0, 0].astype(jnp.float32)
    up_pre = pre_up[0, 0].astype(jnp.float32)
    weight = down_weight[0]
    sigmoid_a = jax.nn.sigmoid(gate_pre)
    hidden = (gate_pre * sigmoid_a * up_pre).astype(jnp.bfloat16)
    back_prop = lax.dot_general(
        routed_rows, weight, (((1,), (1,)), ((), ())), preferred_element_type=jnp.float32
    )
    slot_grad = jnp.sum(hidden.astype(jnp.float32) * back_prop, axis=1)
    carried = gate_col[:, None] * back_prop
    grad_a = (carried * up_pre * sigmoid_a * (1.0 + gate_pre * (1.0 - sigmoid_a))).astype(
        jnp.bfloat16
    )
    grad_b = (carried * gate_pre * sigmoid_a).astype(jnp.bfloat16)
    scaled = (gate_col[:, None] * hidden.astype(jnp.float32)).astype(jnp.bfloat16)
    all_scaled = lax.all_gather(scaled, "dp", axis=0, tiled=True)
    columns = lax.all_to_all(routed_rows, "dp", split_axis=1, concat_axis=0, tiled=True)
    grad_down = lax.dot_general(
        all_scaled, columns, (((0,), (0,)), ((), ())), preferred_element_type=jnp.float32
    ).astype(jnp.bfloat16)
    slot_back = slot_grad.reshape(wide_count, narrow_count, capacity)
    returned = lax.all_to_all(
        lax.all_to_all(slot_back, "wide", split_axis=0, concat_axis=0, tiled=True),
        "narrow",
        split_axis=1,
        concat_axis=1,
        tiled=True,
    )
    grad_gates = jnp.take(returned.reshape(slot_count), target.reshape(-1)).reshape(
        token_count, top_count
    )
    return (grad_down[None], grad_a[None, None], grad_b[None, None], grad_gates)


def swap(x, axis, bits):
    count = lax.axis_size(axis)
    return lax.ppermute(x, axis, [(i, i ^ bits) for i in range(count)])


def after(x, *done):
    return lax.optimization_barrier((x,) + done)[0]


def call(kernel, outs, cost, *args, hbm=0, scratch=(), deps=(), out_space=pltpu.VMEM):
    flops, moved = cost
    body = kernel
    if deps:

        def body(*refs):
            return kernel(*refs[: len(args)], *refs[len(args) + len(deps) :])

    return pl.pallas_call(
        body,
        out_shape=outs,
        in_specs=[pl.BlockSpec(memory_space=pltpu.HBM)] * hbm
        + [pl.BlockSpec(memory_space=pltpu.VMEM)] * (len(args) - hbm)
        + [pl.BlockSpec(memory_space=pl.ANY)] * len(deps),
        out_specs=jax.tree.map(lambda _: pl.BlockSpec(memory_space=out_space), outs),
        scratch_shapes=scratch,
        compiler_params=pltpu.CompilerParams(vmem_limit_bytes=VMEM_LIMIT),
        cost_estimate=pl.CostEstimate(flops=flops, bytes_accessed=moved, transcendentals=0),
    )(*args, *deps)


def in_hbm(*arrays):
    return [pltpu.with_memory_space_constraint(x, pltpu.HBM) for x in arrays]


def peer(xors):
    wide_bits, narrow_bits = xors
    return (lax.axis_index("wide") ^ wide_bits) * lax.axis_size("narrow") + (
        lax.axis_index("narrow") ^ narrow_bits
    )


def first_kernel(
    grad_hbm, routes_hbm, gates_hbm, out_ref, token_ref, routes_ref, gates_ref, sems
):
    rows, features = grad_hbm.shape
    token_ref[...] = jnp.zeros(token_ref.shape, token_ref.dtype)
    copies = [
        pltpu.make_async_copy(routes_hbm, routes_ref, sems.at[0]),
        pltpu.make_async_copy(gates_hbm, gates_ref, sems.at[1]),
        pltpu.make_async_copy(grad_hbm, out_ref.at[:, pl.ds(0, features)], sems.at[2]),
    ]
    for copy in copies:
        copy.start()
    copies[0].wait()
    copies[1].wait()
    routes = routes_ref[...]
    gates = gates_ref[...].astype(jnp.float32)
    ids = lax.broadcasted_iota(jnp.int32, (LANES, rows), 0)
    table = jnp.zeros((LANES, rows), jnp.float32)
    for k in range(routes.shape[0]):
        table = table + jnp.where(ids == routes[k : k + 1, :], gates[k : k + 1, :], 0.0)
    table = jnp.concatenate([table, jnp.zeros((LANES, LANES - rows), jnp.float32)], axis=1)
    out_ref[:, features:] = table.T[:rows, :].astype(out_ref.dtype)
    copies[2].wait()


def hidden_kernel(
    order, rows, pre_gate_hbm, pre_up_hbm, hidden_ref, rest_ref, pre_gate_ref, pre_up_ref, sems
):
    copies = [
        pltpu.make_async_copy(pre_gate_hbm, pre_gate_ref, sems.at[0]),
        pltpu.make_async_copy(pre_up_hbm, pre_up_ref, sems.at[1]),
    ]
    for copy in copies:
        copy.start()
    for copy in copies:
        copy.wait()
    half = len(order) // 2
    for place, xors in enumerate(order):
        source = pl.ds(pl.multiple_of(peer(xors) * rows, rows), rows)
        value = pre_gate_ref[source, :].astype(jnp.float32)
        up = pre_up_ref[source, :].astype(jnp.float32)
        result = (value * jax.nn.sigmoid(value) * up).astype(hidden_ref.dtype)
        hidden_ref[place * rows : (place + 1) * rows, :] = result
        if place >= half:
            rest_ref[(place - half) * rows : (place - half + 1) * rows, :] = result


def turn_kernel(one_hbm, two_ref, *refs):
    one_ref, sems = refs[-2:]
    outs = refs[:-2]
    units, features = one_ref.shape
    cut = outs[0].shape[0]
    copies = [
        pltpu.make_async_copy(
            one_hbm.at[pl.ds(at, LANES)], one_ref.at[pl.ds(at, LANES)], sems.at[step]
        )
        for step, at in enumerate(range(0, units, LANES))
    ]
    for copy in copies:
        copy.start()
    for held, parts, waits in ((two_ref, outs[PARTS:], ()), (one_ref, outs[:PARTS], copies)):
        for step, at in enumerate(range(0, units, LANES)):
            if waits:
                waits[step].wait()
            for to in range(0, features, LANES):
                line = to % cut
                parts[to // cut][line : line + LANES, at : at + LANES] = held[
                    at : at + LANES, to : to + LANES
                ].T


def back_kernel(features, blocks, columns, hidden_ref, other_hidden_ref, *refs):
    group_refs, refs = refs[:blocks], refs[blocks:]
    turned_refs, refs = refs[: 2 * PARTS], refs[2 * PARTS :]
    back_ref, other_back_ref, sums_ref, *cut_refs = refs
    held = jnp.concatenate([group_ref[...] for group_ref in group_refs], axis=0)
    rows = held.shape[0]
    for expert, (act_ref, result_ref) in enumerate(
        ((hidden_ref, back_ref), (other_hidden_ref, other_back_ref))
    ):
        back = jnp.zeros(result_ref.shape, jnp.float32)
        for part in range(PARTS):
            part_ref = turned_refs[expert * PARTS + part]
            depth = part_ref.shape[0]
            back = back + jnp.dot(
                held[:, part * depth : (part + 1) * depth],
                part_ref[...],
                preferred_element_type=jnp.float32,
            )
        result_ref[...] = back
        product = act_ref[:rows, :].astype(jnp.float32) * back
        folded = product[:, :LANES]
        for at in range(LANES, product.shape[1], LANES):
            folded = folded + product[:, at : at + LANES]
        for at in range(0, rows, LANES):
            row = (expert * rows + at) // LANES
            sums_ref[row : row + 1, :] = jnp.sum(
                folded[at : at + LANES, :].T, axis=0, keepdims=True
            )
    step = rows // blocks
    for bits, cut_ref in enumerate(cut_refs):
        start = pl.multiple_of((lax.axis_index("dp") ^ bits) * columns, columns)
        for block, group_ref in enumerate(group_refs):
            here = slice(block * step, (block + 1) * step)
            cut_ref[here, :columns] = group_ref[:, pl.ds(start, columns)]
            cut_ref[here, columns:] = group_ref[:, features:]


def own_gates(table):
    lane = lax.broadcasted_iota(jnp.int32, table.shape, 1)
    return jnp.sum(
        jnp.where(lane == peer((0, 0)), table.astype(jnp.float32), 0.0), axis=1, keepdims=True
    )


def grads_kernel(
    order,
    rows,
    columns,
    held_ref,
    rest_ref,
    back_ref,
    rest_back_ref,
    hidden_ref,
    pre_gate_ref,
    pre_up_ref,
    grad_gate_ref,
    grad_up_ref,
    scaled_ref,
):
    half = len(order) // 2
    for place, xors in enumerate(order):
        tokens_ref, products_ref = ((held_ref, back_ref), (rest_ref, rest_back_ref))[place // half]
        there = slice((place % half) * rows, (place % half + 1) * rows)
        gate = own_gates(tokens_ref[there, columns:])
        here = slice(place * rows, (place + 1) * rows)
        source = pl.ds(pl.multiple_of(peer(xors) * rows, rows), rows)
        value = pre_gate_ref[source, :].astype(jnp.float32)
        up = pre_up_ref[source, :].astype(jnp.float32)
        sig = jax.nn.sigmoid(value)
        carried = gate * products_ref[there, :]
        grad_gate_ref[source, :] = (carried * up * sig * (1.0 + value * (1.0 - sig))).astype(
            grad_gate_ref.dtype
        )
        grad_up_ref[source, :] = (carried * value * sig).astype(grad_up_ref.dtype)
        scaled_ref[here, :] = (gate * hidden_ref[here, :].astype(jnp.float32)).astype(
            scaled_ref.dtype
        )


def scale(hidden, table):
    return (own_gates(table) * hidden.astype(jnp.float32)).astype(jnp.bfloat16)


def first_down_kernel(scaled_ref, held_ref, rest_ref, *refs):
    sum_refs, refs = refs[-PIECES:], refs[:-PIECES]
    depth, columns = sum_refs[0].shape
    scaled, tokens = [scaled_ref[...]], [held_ref[:, :columns], rest_ref[:, :columns]]
    for hidden_ref, one_ref in zip(refs[::2], refs[1::2]):
        scaled.append(scale(hidden_ref[: one_ref.shape[0], :], one_ref[:, columns:]))
        tokens.append(one_ref[:, :columns])
    scaled = jnp.concatenate(scaled, axis=0)
    tokens = jnp.concatenate(tokens, axis=0)
    for at, sum_ref in enumerate(sum_refs):
        sum_ref[...] = lax.dot_general(
            scaled[:, at * depth : (at + 1) * depth],
            tokens,
            (((0,), (0,)), ((), ())),
            preferred_element_type=jnp.float32,
        )


def last_down_kernel(*refs):
    out_ref, held_out_ref, sems = refs[-3:]
    sum_refs, refs = refs[:PIECES], refs[PIECES:-3]
    depth, columns = sum_refs[0].shape
    scaled, tokens = [], []
    for hidden_ref, two_ref in zip(refs[::2], refs[1::2]):
        rows = two_ref.shape[0]
        scaled.append(scale(hidden_ref[rows:, :], two_ref[:, columns:]))
        tokens.append(two_ref[:, :columns])
    scaled = jnp.concatenate(scaled, axis=0)
    tokens = jnp.concatenate(tokens, axis=0)
    copies = []
    for at, sum_ref in enumerate(sum_refs):
        here = pl.ds(at * depth, depth)
        held_out_ref[here, :] = (
            sum_ref[...]
            + lax.dot_general(
                scaled[:, at * depth : (at + 1) * depth],
                tokens,
                (((0,), (0,)), ((), ())),
                preferred_element_type=jnp.float32,
            )
        ).astype(out_ref.dtype)
        copies.append(
            pltpu.make_async_copy(held_out_ref.at[here], out_ref.at[here], sems.at[at])
        )
        copies[-1].start()
    for copy in copies:
        copy.wait()


def pick_kernel(order, back_order, rows, routes_ref, sums_ref, out_ref):
    routes = routes_ref[...]
    total = jnp.zeros(out_ref.shape, jnp.float32)
    per = sums_ref.shape[1] // 2
    for line, (wide_bits, narrow_bits) in enumerate(back_order):
        start = order.index((wide_bits, narrow_bits)) * rows
        at = start % LANES
        for expert in range(2):
            row = expert * per + start // LANES
            found = sums_ref[line, row : row + 1, :][:, at : at + rows]
            chosen = routes == peer((wide_bits ^ expert, narrow_bits))
            total = total + jnp.where(chosen, found, 0.0)
    out_ref[...] = total


def shards_gather(out_grad, routes, gates, pre_gate, pre_up, down_weight):
    dp_count = lax.axis_size("dp")
    wide_count = lax.axis_size("wide")
    narrow_count = lax.axis_size("narrow")
    rows, features = out_grad.shape
    slot_count, units = pre_gate.shape[2:]
    half_count = slot_count // 2
    columns = features // dp_count
    routes_t = routes.T
    gates_t = gates.T
    pre_gate = pre_gate[0, 0]
    pre_up = pre_up[0, 0]
    weight = down_weight[0]
    bf16, f32 = jnp.bfloat16, jnp.float32
    shape = jax.ShapeDtypeStruct

    near = max(narrow_count // 2, 1)
    wide_bits = [1 << b for b in range(1, wide_count.bit_length() - 1)]
    reach = [0] + list(range(near, narrow_count)) + list(range(1, near))
    order = [(0, bits) for bits in reach]
    for bits in wide_bits + [1]:
        order += [(w ^ bits, n) for w, n in order]
    order = tuple(order)

    payload, token = call(
        first_kernel,
        (shape((rows, features + LANES), bf16), shape((8, LANES), f32)),
        (rows * features, 4 * rows * features),
        *in_hbm(out_grad, routes_t, gates_t),
        hbm=3,
        scratch=[
            pltpu.VMEM(routes_t.shape, routes_t.dtype),
            pltpu.VMEM(gates_t.shape, gates_t.dtype),
            pltpu.SemaphoreType.DMA((3,)),
        ],
    )
    hidden, rest_hidden = call(
        functools.partial(hidden_kernel, order, rows),
        (shape((slot_count, units), bf16), shape((half_count, units), bf16)),
        (20 * slot_count * units, 6 * slot_count * units),
        *in_hbm(pre_gate, pre_up),
        hbm=2,
        deps=(token,),
        scratch=[
            pltpu.VMEM(pre_gate.shape, pre_gate.dtype),
            pltpu.VMEM(pre_up.shape, pre_up.dtype),
            pltpu.SemaphoreType.DMA((2,)),
        ],
    )
    other_weight = swap(after(weight, token), "wide", 1)
    along = [swap(payload, "narrow", bits) if bits else payload for bits in reach]
    turned = call(
        turn_kernel,
        (shape((features // PARTS, units), bf16),) * (2 * PARTS),
        (0, 8 * features * units),
        *in_hbm(weight),
        other_weight,
        hbm=1,
        deps=(token,),
        scratch=[
            pltpu.VMEM(weight.shape, weight.dtype),
            pltpu.SemaphoreType.DMA((units // LANES,)),
        ],
    )
    over = [swap(hidden, "dp", bits) for bits in range(1, dp_count)]
    other_hidden = swap(after(rest_hidden, *along[near:]), "wide", 1)
    groups = [jnp.concatenate(along[:near], axis=0)]
    if along[near:]:
        groups.append(jnp.concatenate(along[near:], axis=0))
    for bits in wide_bits:
        groups += [swap(group, "wide", bits) for group in groups]
    middle = len(groups) // 2
    groups[middle] = after(groups[middle], *turned, *over)
    back, other_back, sums, *cuts = call(
        functools.partial(back_kernel, features, len(groups), columns),
        (
            shape((half_count, units), f32),
            shape((half_count, units), f32),
            shape((slot_count // LANES, LANES), f32),
        )
        + (shape((half_count, columns + LANES), bf16),) * dp_count,
        (2 * slot_count * units * features, 4 * units * features),
        hidden,
        other_hidden,
        *groups,
        *turned,
    )
    found = sums[None]
    back_order = [(0, 0)]
    for bits in wide_bits:
        found = jnp.concatenate([found, swap(found, "wide", bits)], axis=0)
        back_order += [(w ^ bits, n) for w, n in back_order]
    held, *cuts = cuts
    rest = swap(held, "wide", 1)
    rest_back = swap(other_back, "wide", 1)
    crossed = [swap(cut, "dp", bits) for bits, cut in enumerate(cuts, 1)]
    grad_a, grad_b, scaled = call(
        functools.partial(grads_kernel, order, rows, columns),
        (shape((slot_count, units), bf16),) * 3,
        (30 * slot_count * units, 12 * slot_count * units),
        held,
        rest,
        back,
        rest_back,
        hidden,
        pre_gate,
        pre_up,
    )
    sums_down = call(
        first_down_kernel,
        (shape((units // PIECES, columns), f32),) * PIECES,
        (2 * slot_count * units * columns, 4 * units * columns),
        scaled,
        held,
        rest,
        *(x for pair in zip(over, crossed) for x in pair),
    )
    bits_of = [1 << b for b in range(narrow_count.bit_length() - 1)]
    for bits, done in zip(bits_of, [scaled] * (len(bits_of) - 1) + [sums_down[-1]]):
        found = jnp.concatenate([after(found, done), swap(found, "narrow", bits)], axis=0)
        back_order += [(w, n ^ bits) for w, n in back_order]
    across = [swap(after(one, found), "wide", 1) for one in crossed]
    grad_down = call(
        last_down_kernel,
        shape((units, columns), bf16),
        (2 * dp_count * slot_count * units * columns, 4 * units * columns),
        *sums_down,
        *(x for pair in zip(over, across) for x in pair),
        out_space=pltpu.HBM,
        scratch=[
            pltpu.VMEM((units, columns), bf16),
            pltpu.SemaphoreType.DMA((PIECES,)),
        ],
    )
    picked = call(
        functools.partial(pick_kernel, order, tuple(back_order), rows),
        shape(routes_t.shape, f32),
        (slot_count, slot_count),
        routes_t,
        found,
    )
    return (grad_down[None], grad_a[None, None], grad_b[None, None], picked.T)


def shards(out_grad, routes, gates, pre_gate, pre_up, down_weight):
    wide_count = lax.axis_size("wide")
    narrow_count = lax.axis_size("narrow")
    experts = wide_count * narrow_count
    rows = out_grad.shape[0]
    slot_count = pre_gate.shape[2]
    whole_blocks = (
        slot_count == experts * rows
        and wide_count > 1
        and all(n & (n - 1) == 0 for n in (lax.axis_size("dp"), wide_count, narrow_count))
        and experts <= LANES
        and LANES % rows == 0
        and (slot_count // 2) % LANES == 0
    )
    plan = shards_gather if whole_blocks else shards_exchange
    return plan(out_grad, routes, gates, pre_gate, pre_up, down_weight)


def solution(mesh):
    placed = (
        P(("dp", "wide", "narrow"), None),
        P(("dp", "wide", "narrow"), None),
        P(("dp", "wide", "narrow"), None),
        P("dp", ("wide", "narrow"), None, None),
        P("dp", ("wide", "narrow"), None, None),
        P(("wide", "narrow"), None, None),
    )
    return jax.shard_map(
        shards,
        mesh=mesh,
        in_specs=placed,
        out_specs=(
            P(("wide", "narrow"), None, "dp"),
            P("dp", ("wide", "narrow"), None, None),
            P("dp", ("wide", "narrow"), None, None),
            P(("dp", "wide", "narrow"), None),
        ),
        check_vma=False,
    )
```

```python
import functools

import jax
import jax.numpy as jnp
from jax import lax
from jax.experimental import pallas as pl
from jax.experimental.pallas import tpu as pltpu
from jax.sharding import PartitionSpec as P

LANES = 128
CUTS = 2
PARTS = 4
VMEM_LIMIT = 14 * 1024 * 1024


def shards_exchange(out_grad, routes, gates, pre_gate, pre_up, down_weight):
    wide_count = lax.axis_size("wide")
    narrow_count = lax.axis_size("narrow")
    experts = wide_count * narrow_count
    token_count, top_count = routes.shape
    slot_count = pre_gate.shape[2]
    capacity = slot_count // experts
    expert_ids = jnp.arange(experts, dtype=jnp.int32)
    named_hits = (routes[:, :, None] == expert_ids[None, None, :]).astype(jnp.int32)
    hit_counts = jnp.sum(named_hits, axis=1)
    before = jnp.cumsum(hit_counts, axis=0) - hit_counts
    position = jnp.sum(named_hits * before[:, None, :], axis=2)
    target = routes * capacity + position
    slot_ids = jnp.arange(slot_count, dtype=jnp.int32)
    placed = target[:, :, None] == slot_ids[None, None, :]
    choose = jnp.sum(placed.astype(jnp.bfloat16), axis=1)
    outgoing = lax.dot_general(
        choose, out_grad, (((0,), (0,)), ((), ())), preferred_element_type=jnp.float32
    ).astype(jnp.bfloat16)
    gate_out = jnp.sum(
        jnp.where(placed, gates[:, :, None].astype(jnp.float32), 0.0), axis=(0, 1)
    ).astype(jnp.bfloat16)
    outgoing = outgoing.reshape(wide_count, narrow_count, capacity, outgoing.shape[1])
    gate_out = gate_out.reshape(wide_count, narrow_count, capacity)
    incoming, gate_in = (
        lax.all_to_all(
            lax.all_to_all(outgoing, "wide", split_axis=0, concat_axis=0, tiled=True),
            "narrow",
            split_axis=1,
            concat_axis=1,
            tiled=True,
        ),
        lax.all_to_all(
            lax.all_to_all(gate_out, "wide", split_axis=0, concat_axis=0, tiled=True),
            "narrow",
            split_axis=1,
            concat_axis=1,
            tiled=True,
        ),
    )
    routed_rows = incoming.reshape(slot_count, incoming.shape[3])
    gate_col = gate_in.reshape(slot_count).astype(jnp.float32)
    gate_pre = pre_gate[0, 0].astype(jnp.float32)
    up_pre = pre_up[0, 0].astype(jnp.float32)
    weight = down_weight[0]
    sigmoid_a = jax.nn.sigmoid(gate_pre)
    hidden = (gate_pre * sigmoid_a * up_pre).astype(jnp.bfloat16)
    back_prop = lax.dot_general(
        routed_rows, weight, (((1,), (1,)), ((), ())), preferred_element_type=jnp.float32
    )
    slot_grad = jnp.sum(hidden.astype(jnp.float32) * back_prop, axis=1)
    carried = gate_col[:, None] * back_prop
    grad_a = (carried * up_pre * sigmoid_a * (1.0 + gate_pre * (1.0 - sigmoid_a))).astype(
        jnp.bfloat16
    )
    grad_b = (carried * gate_pre * sigmoid_a).astype(jnp.bfloat16)
    scaled = (gate_col[:, None] * hidden.astype(jnp.float32)).astype(jnp.bfloat16)
    all_scaled = lax.all_gather(scaled, "dp", axis=0, tiled=True)
    columns = lax.all_to_all(routed_rows, "dp", split_axis=1, concat_axis=0, tiled=True)
    grad_down = lax.dot_general(
        all_scaled, columns, (((0,), (0,)), ((), ())), preferred_element_type=jnp.float32
    ).astype(jnp.bfloat16)
    slot_back = slot_grad.reshape(wide_count, narrow_count, capacity)
    returned = lax.all_to_all(
        lax.all_to_all(slot_back, "wide", split_axis=0, concat_axis=0, tiled=True),
        "narrow",
        split_axis=1,
        concat_axis=1,
        tiled=True,
    )
    grad_gates = jnp.take(returned.reshape(slot_count), target.reshape(-1)).reshape(
        token_count, top_count
    )
    return (grad_down[None], grad_a[None, None], grad_b[None, None], grad_gates)


def swap(x, axis, bits):
    count = lax.axis_size(axis)
    return lax.ppermute(x, axis, [(i, i ^ bits) for i in range(count)])


def after(x, *done):
    return lax.optimization_barrier((x,) + done)[0]


def call(kernel, outs, cost, *args, hbm=0, scratch=(), deps=(), out_specs=None):
    flops, moved = cost
    body = kernel
    if deps:

        def body(*refs):
            return kernel(*refs[: len(args)], *refs[len(args) + len(deps) :])

    return pl.pallas_call(
        body,
        out_shape=outs,
        in_specs=[pl.BlockSpec(memory_space=pltpu.HBM)] * hbm
        + [pl.BlockSpec(memory_space=pltpu.VMEM)] * (len(args) - hbm)
        + [pl.BlockSpec(memory_space=pl.ANY)] * len(deps),
        out_specs=jax.tree.map(lambda _: pl.BlockSpec(memory_space=pltpu.VMEM), outs)
        if out_specs is None
        else out_specs,
        scratch_shapes=scratch,
        compiler_params=pltpu.CompilerParams(vmem_limit_bytes=VMEM_LIMIT),
        cost_estimate=pl.CostEstimate(flops=flops, bytes_accessed=moved, transcendentals=0),
    )(*args, *deps)


def in_hbm(*arrays):
    return [pltpu.with_memory_space_constraint(x, pltpu.HBM) for x in arrays]


def peer(xors):
    wide_bits, narrow_bits = xors
    return (lax.axis_index("wide") ^ wide_bits) * lax.axis_size("narrow") + (
        lax.axis_index("narrow") ^ narrow_bits
    )


def first_kernel(
    grad_hbm, routes_hbm, gates_hbm, out_ref, token_ref, routes_ref, gates_ref, sems
):
    rows, features = grad_hbm.shape
    token_ref[...] = jnp.zeros(token_ref.shape, token_ref.dtype)
    copies = [
        pltpu.make_async_copy(routes_hbm, routes_ref, sems.at[0]),
        pltpu.make_async_copy(gates_hbm, gates_ref, sems.at[1]),
        pltpu.make_async_copy(grad_hbm, out_ref.at[:, pl.ds(0, features)], sems.at[2]),
    ]
    for copy in copies:
        copy.start()
    copies[0].wait()
    copies[1].wait()
    routes = routes_ref[...]
    gates = gates_ref[...].astype(jnp.float32)
    ids = lax.broadcasted_iota(jnp.int32, (LANES, rows), 0)
    table = jnp.zeros((LANES, rows), jnp.float32)
    for k in range(routes.shape[0]):
        table = table + jnp.where(ids == routes[k : k + 1, :], gates[k : k + 1, :], 0.0)
    table = jnp.concatenate([table, jnp.zeros((LANES, LANES - rows), jnp.float32)], axis=1)
    out_ref[:, features:] = table.T[:rows, :].astype(out_ref.dtype)
    copies[2].wait()


def hidden_kernel(
    order, rows, pre_gate_hbm, pre_up_hbm, hidden_ref, rest_ref, pre_gate_ref, pre_up_ref, sems
):
    copies = [
        pltpu.make_async_copy(pre_gate_hbm, pre_gate_ref, sems.at[0]),
        pltpu.make_async_copy(pre_up_hbm, pre_up_ref, sems.at[1]),
    ]
    for copy in copies:
        copy.start()
    for copy in copies:
        copy.wait()
    half = len(order) // 2
    for place, xors in enumerate(order):
        source = pl.ds(pl.multiple_of(peer(xors) * rows, rows), rows)
        value = pre_gate_ref[source, :].astype(jnp.float32)
        up = pre_up_ref[source, :].astype(jnp.float32)
        result = (value * jax.nn.sigmoid(value) * up).astype(hidden_ref.dtype)
        hidden_ref[place * rows : (place + 1) * rows, :] = result
        if place >= half:
            rest_ref[(place - half) * rows : (place - half + 1) * rows, :] = result


def turn_kernel(one_hbm, two_ref, *refs):
    one_ref, sems = refs[-2:]
    outs = refs[:-2]
    units, features = one_ref.shape
    cut = outs[0].shape[0]
    copies = [
        pltpu.make_async_copy(
            one_hbm.at[pl.ds(at, LANES)], one_ref.at[pl.ds(at, LANES)], sems.at[step]
        )
        for step, at in enumerate(range(0, units, LANES))
    ]
    for copy in copies:
        copy.start()
    for held, parts, waits in ((two_ref, outs[PARTS:], ()), (one_ref, outs[:PARTS], copies)):
        for step, at in enumerate(range(0, units, LANES)):
            if waits:
                waits[step].wait()
            for to in range(0, features, LANES):
                line = to % cut
                parts[to // cut][line : line + LANES, at : at + LANES] = held[
                    at : at + LANES, to : to + LANES
                ].T


def back_kernel(features, blocks, columns, hidden_ref, other_hidden_ref, *refs):
    group_refs, refs = refs[:blocks], refs[blocks:]
    turned_refs, refs = refs[: 2 * PARTS], refs[2 * PARTS :]
    back_ref, other_back_ref, sums_ref, own_ref = refs
    held = jnp.concatenate([group_ref[...] for group_ref in group_refs], axis=0)
    rows = held.shape[0]
    for expert, (act_ref, result_ref) in enumerate(
        ((hidden_ref, back_ref), (other_hidden_ref, other_back_ref))
    ):
        back = jnp.zeros(result_ref.shape, jnp.float32)
        for part in range(PARTS):
            part_ref = turned_refs[expert * PARTS + part]
            depth = part_ref.shape[0]
            back = back + jnp.dot(
                held[:, part * depth : (part + 1) * depth],
                part_ref[...],
                preferred_element_type=jnp.float32,
            )
        result_ref[...] = back
        product = act_ref[:rows, :].astype(jnp.float32) * back
        folded = product[:, :LANES]
        for at in range(LANES, product.shape[1], LANES):
            folded = folded + product[:, at : at + LANES]
        for at in range(0, rows, LANES):
            row = (expert * rows + at) // LANES
            sums_ref[row : row + 1, :] = jnp.sum(
                folded[at : at + LANES, :].T, axis=0, keepdims=True
            )
    copy_columns(features, columns, 0, group_refs, own_ref)


def copy_columns(features, columns, bits, group_refs, out_ref):
    start = pl.multiple_of((lax.axis_index("dp") ^ bits) * columns, columns)
    step = out_ref.shape[0] // len(group_refs)
    for block, group_ref in enumerate(group_refs):
        here = slice(block * step, (block + 1) * step)
        out_ref[here, :columns] = group_ref[:, pl.ds(start, columns)]
        out_ref[here, columns:] = group_ref[:, features:]


def cut_kernel(features, columns, blocks, *refs):
    for bits, cut_ref in enumerate(refs[blocks:], 1):
        copy_columns(features, columns, bits, refs[:blocks], cut_ref)


def own_gates(table):
    lane = lax.broadcasted_iota(jnp.int32, table.shape, 1)
    return jnp.sum(
        jnp.where(lane == peer((0, 0)), table.astype(jnp.float32), 0.0), axis=1, keepdims=True
    )


def grads_kernel(
    order,
    rows,
    columns,
    held_ref,
    rest_ref,
    back_ref,
    rest_back_ref,
    hidden_ref,
    pre_gate_ref,
    pre_up_ref,
    grad_gate_ref,
    grad_up_ref,
    scaled_ref,
):
    half = len(order) // 2
    for place, xors in enumerate(order):
        tokens_ref, products_ref = ((held_ref, back_ref), (rest_ref, rest_back_ref))[place // half]
        there = slice((place % half) * rows, (place % half + 1) * rows)
        gate = own_gates(tokens_ref[there, columns:])
        here = slice(place * rows, (place + 1) * rows)
        source = pl.ds(pl.multiple_of(peer(xors) * rows, rows), rows)
        value = pre_gate_ref[source, :].astype(jnp.float32)
        up = pre_up_ref[source, :].astype(jnp.float32)
        sig = jax.nn.sigmoid(value)
        carried = gate * products_ref[there, :]
        grad_gate_ref[source, :] = (carried * up * sig * (1.0 + value * (1.0 - sig))).astype(
            grad_gate_ref.dtype
        )
        grad_up_ref[source, :] = (carried * value * sig).astype(grad_up_ref.dtype)
        scaled_ref[here, :] = (gate * hidden_ref[here, :].astype(jnp.float32)).astype(
            scaled_ref.dtype
        )


def scale(hidden, table):
    return (own_gates(table) * hidden.astype(jnp.float32)).astype(jnp.bfloat16)


def down_kernel(scaled_ref, held_ref, rest_ref, *refs):
    out_ref, held_out_ref, sems = refs[-3:]
    columns = out_ref.shape[1]
    scaled, tokens = [scaled_ref[...]], [held_ref[:, :columns], rest_ref[:, :columns]]
    for at in range(0, len(refs) - 3, CUTS + 2):
        hidden_ref, *part_refs = refs[at : at + CUTS + 2]
        start = 0
        for part_ref in part_refs:
            stop = start + part_ref.shape[0]
            scaled.append(scale(hidden_ref[start:stop, :], part_ref[:, columns:]))
            tokens.append(part_ref[:, :columns])
            start = stop
    scaled = jnp.concatenate(scaled, axis=0)
    tokens = jnp.concatenate(tokens, axis=0)
    copies = []
    for at in range(0, out_ref.shape[0], 2 * LANES):
        here = pl.ds(at, 2 * LANES)
        held_out_ref[here, :] = lax.dot_general(
            scaled[:, at : at + 2 * LANES],
            tokens,
            (((0,), (0,)), ((), ())),
            preferred_element_type=jnp.float32,
        ).astype(out_ref.dtype)
        copies.append(
            pltpu.make_async_copy(held_out_ref.at[here], out_ref.at[here], sems.at[len(copies)])
        )
        copies[-1].start()
    for copy in copies:
        copy.wait()


def pick_kernel(order, back_order, rows, routes_ref, sums_ref, out_ref):
    routes = routes_ref[...]
    total = jnp.zeros(out_ref.shape, jnp.float32)
    per = sums_ref.shape[1] // 2
    for line, (wide_bits, narrow_bits) in enumerate(back_order):
        start = order.index((wide_bits, narrow_bits)) * rows
        at = start % LANES
        for expert in range(2):
            row = expert * per + start // LANES
            found = sums_ref[line, row : row + 1, :][:, at : at + rows]
            chosen = routes == peer((wide_bits ^ expert, narrow_bits))
            total = total + jnp.where(chosen, found, 0.0)
    out_ref[...] = total


def shards_gather(out_grad, routes, gates, pre_gate, pre_up, down_weight):
    dp_count = lax.axis_size("dp")
    wide_count = lax.axis_size("wide")
    narrow_count = lax.axis_size("narrow")
    rows, features = out_grad.shape
    slot_count, units = pre_gate.shape[2:]
    half_count = slot_count // 2
    columns = features // dp_count
    routes_t = routes.T
    gates_t = gates.T
    pre_gate = pre_gate[0, 0]
    pre_up = pre_up[0, 0]
    weight = down_weight[0]
    bf16, f32 = jnp.bfloat16, jnp.float32
    shape = jax.ShapeDtypeStruct

    near = max(narrow_count // 2, 1)
    wide_bits = [1 << b for b in range(1, wide_count.bit_length() - 1)]
    reach = [0] + list(range(near, narrow_count)) + list(range(1, near))
    order = [(0, bits) for bits in reach]
    for bits in wide_bits + [1]:
        order += [(w ^ bits, n) for w, n in order]
    order = tuple(order)

    payload, token = call(
        first_kernel,
        (shape((rows, features + LANES), bf16), shape((8, LANES), f32)),
        (rows * features, 4 * rows * features),
        *in_hbm(out_grad, routes_t, gates_t),
        hbm=3,
        scratch=[
            pltpu.VMEM(routes_t.shape, routes_t.dtype),
            pltpu.VMEM(gates_t.shape, gates_t.dtype),
            pltpu.SemaphoreType.DMA((3,)),
        ],
    )
    hidden, rest_hidden = call(
        functools.partial(hidden_kernel, order, rows),
        (shape((slot_count, units), bf16), shape((half_count, units), bf16)),
        (20 * slot_count * units, 6 * slot_count * units),
        *in_hbm(pre_gate, pre_up),
        hbm=2,
        deps=(token,),
        scratch=[
            pltpu.VMEM(pre_gate.shape, pre_gate.dtype),
            pltpu.VMEM(pre_up.shape, pre_up.dtype),
            pltpu.SemaphoreType.DMA((2,)),
        ],
    )
    other_weight = swap(after(weight, token), "wide", 1)
    along = [swap(payload, "narrow", bits) if bits else payload for bits in reach]
    turned = call(
        turn_kernel,
        (shape((features // PARTS, units), bf16),) * (2 * PARTS),
        (0, 8 * features * units),
        *in_hbm(weight),
        other_weight,
        hbm=1,
        deps=(token,),
        scratch=[
            pltpu.VMEM(weight.shape, weight.dtype),
            pltpu.SemaphoreType.DMA((units // LANES,)),
        ],
    )
    over = [swap(hidden, "dp", bits) for bits in range(1, dp_count)]
    other_hidden = swap(after(rest_hidden, *along[near:]), "wide", 1)
    groups = [jnp.concatenate(along[:near], axis=0)]
    if along[near:]:
        groups.append(jnp.concatenate(along[near:], axis=0))
    for bits in wide_bits:
        groups += [swap(group, "wide", bits) for group in groups]
    middle = len(groups) // 2
    groups[middle] = after(groups[middle], *turned, *over)
    cuts = call(
        functools.partial(cut_kernel, features, columns, len(groups)),
        (shape((half_count, columns + LANES), bf16),) * (dp_count - 1),
        (0, 4 * half_count * columns),
        *groups,
    )
    crossed = [swap(cut, "dp", bits) for bits, cut in enumerate(cuts, 1)]
    back, other_back, sums, held = call(
        functools.partial(back_kernel, features, len(groups), columns),
        (
            shape((half_count, units), f32),
            shape((half_count, units), f32),
            shape((slot_count // LANES, LANES), f32),
            shape((half_count, columns + LANES), bf16),
        ),
        (2 * slot_count * units * features, 4 * units * features),
        hidden,
        other_hidden,
        *groups,
        *turned,
    )
    found = sums[None]
    back_order = [(0, 0)]
    for bits in wide_bits:
        found = jnp.concatenate([found, swap(found, "wide", bits)], axis=0)
        back_order += [(w ^ bits, n) for w, n in back_order]
    rest = swap(held, "wide", 1)
    rest_back = swap(other_back, "wide", 1)
    grad_a, grad_b, scaled = call(
        functools.partial(grads_kernel, order, rows, columns),
        (shape((slot_count, units), bf16),) * 3,
        (30 * slot_count * units, 12 * slot_count * units),
        held,
        rest,
        back,
        rest_back,
        hidden,
        pre_gate,
        pre_up,
    )
    steps = [1 << b for b in range(narrow_count.bit_length() - 1)]
    for bits in steps[:-1]:
        found = jnp.concatenate([after(found, scaled), swap(found, "narrow", bits)], axis=0)
        back_order += [(w, n ^ bits) for w, n in back_order]
    others = []
    cut = half_count // CUTS
    for hidden_there, one in zip(over, crossed):
        others += [hidden_there, one]
        others += [swap(one[at : at + cut], "wide", 1) for at in range(0, half_count, cut)]
    grad_down = call(
        down_kernel,
        shape((units, columns), bf16),
        (2 * dp_count * slot_count * units * columns, 4 * units * columns),
        scaled,
        held,
        rest,
        *others,
        out_specs=pl.BlockSpec(memory_space=pltpu.HBM),
        scratch=[
            pltpu.VMEM((units, columns), bf16),
            pltpu.SemaphoreType.DMA((units // (2 * LANES),)),
        ],
    )
    for bits in steps[-1:]:
        found = jnp.concatenate([after(found, grad_down), swap(found, "narrow", bits)], axis=0)
        back_order += [(w, n ^ bits) for w, n in back_order]
    picked = call(
        functools.partial(pick_kernel, order, tuple(back_order), rows),
        shape(routes_t.shape, f32),
        (slot_count, slot_count),
        routes_t,
        found,
    )
    return (grad_down[None], grad_a[None, None], grad_b[None, None], picked.T)


def shards(out_grad, routes, gates, pre_gate, pre_up, down_weight):
    wide_count = lax.axis_size("wide")
    narrow_count = lax.axis_size("narrow")
    experts = wide_count * narrow_count
    rows = out_grad.shape[0]
    slot_count = pre_gate.shape[2]
    whole_blocks = (
        slot_count == experts * rows
        and wide_count > 1
        and all(n & (n - 1) == 0 for n in (lax.axis_size("dp"), wide_count, narrow_count))
        and experts <= LANES
        and LANES % rows == 0
        and (slot_count // 2) % LANES == 0
    )
    plan = shards_gather if whole_blocks else shards_exchange
    return plan(out_grad, routes, gates, pre_gate, pre_up, down_weight)


def solution(mesh):
    placed = (
        P(("dp", "wide", "narrow"), None),
        P(("dp", "wide", "narrow"), None),
        P(("dp", "wide", "narrow"), None),
        P("dp", ("wide", "narrow"), None, None),
        P("dp", ("wide", "narrow"), None, None),
        P(("wide", "narrow"), None, None),
    )
    return jax.shard_map(
        shards,
        mesh=mesh,
        in_specs=placed,
        out_specs=(
            P(("wide", "narrow"), None, "dp"),
            P("dp", ("wide", "narrow"), None, None),
            P("dp", ("wide", "narrow"), None, None),
            P(("dp", "wide", "narrow"), None),
        ),
        check_vma=False,
    )
```

```python
import functools

import jax
import jax.numpy as jnp
from jax import lax
from jax.experimental import pallas as pl
from jax.experimental.pallas import tpu as pltpu
from jax.sharding import PartitionSpec as P

LANES = 128
CUTS = 2
PARTS = 4
VMEM_LIMIT = 14 * 1024 * 1024


def shards_exchange(out_grad, routes, gates, pre_gate, pre_up, down_weight):
    wide_count = lax.axis_size("wide")
    narrow_count = lax.axis_size("narrow")
    experts = wide_count * narrow_count
    token_count, top_count = routes.shape
    slot_count = pre_gate.shape[2]
    capacity = slot_count // experts
    expert_ids = jnp.arange(experts, dtype=jnp.int32)
    named_hits = (routes[:, :, None] == expert_ids[None, None, :]).astype(jnp.int32)
    hit_counts = jnp.sum(named_hits, axis=1)
    before = jnp.cumsum(hit_counts, axis=0) - hit_counts
    position = jnp.sum(named_hits * before[:, None, :], axis=2)
    target = routes * capacity + position
    slot_ids = jnp.arange(slot_count, dtype=jnp.int32)
    placed = target[:, :, None] == slot_ids[None, None, :]
    choose = jnp.sum(placed.astype(jnp.bfloat16), axis=1)
    outgoing = lax.dot_general(
        choose, out_grad, (((0,), (0,)), ((), ())), preferred_element_type=jnp.float32
    ).astype(jnp.bfloat16)
    gate_out = jnp.sum(
        jnp.where(placed, gates[:, :, None].astype(jnp.float32), 0.0), axis=(0, 1)
    ).astype(jnp.bfloat16)
    outgoing = outgoing.reshape(wide_count, narrow_count, capacity, outgoing.shape[1])
    gate_out = gate_out.reshape(wide_count, narrow_count, capacity)
    incoming, gate_in = (
        lax.all_to_all(
            lax.all_to_all(outgoing, "wide", split_axis=0, concat_axis=0, tiled=True),
            "narrow",
            split_axis=1,
            concat_axis=1,
            tiled=True,
        ),
        lax.all_to_all(
            lax.all_to_all(gate_out, "wide", split_axis=0, concat_axis=0, tiled=True),
            "narrow",
            split_axis=1,
            concat_axis=1,
            tiled=True,
        ),
    )
    routed_rows = incoming.reshape(slot_count, incoming.shape[3])
    gate_col = gate_in.reshape(slot_count).astype(jnp.float32)
    gate_pre = pre_gate[0, 0].astype(jnp.float32)
    up_pre = pre_up[0, 0].astype(jnp.float32)
    weight = down_weight[0]
    sigmoid_a = jax.nn.sigmoid(gate_pre)
    hidden = (gate_pre * sigmoid_a * up_pre).astype(jnp.bfloat16)
    back_prop = lax.dot_general(
        routed_rows, weight, (((1,), (1,)), ((), ())), preferred_element_type=jnp.float32
    )
    slot_grad = jnp.sum(hidden.astype(jnp.float32) * back_prop, axis=1)
    carried = gate_col[:, None] * back_prop
    grad_a = (carried * up_pre * sigmoid_a * (1.0 + gate_pre * (1.0 - sigmoid_a))).astype(
        jnp.bfloat16
    )
    grad_b = (carried * gate_pre * sigmoid_a).astype(jnp.bfloat16)
    scaled = (gate_col[:, None] * hidden.astype(jnp.float32)).astype(jnp.bfloat16)
    all_scaled = lax.all_gather(scaled, "dp", axis=0, tiled=True)
    columns = lax.all_to_all(routed_rows, "dp", split_axis=1, concat_axis=0, tiled=True)
    grad_down = lax.dot_general(
        all_scaled, columns, (((0,), (0,)), ((), ())), preferred_element_type=jnp.float32
    ).astype(jnp.bfloat16)
    slot_back = slot_grad.reshape(wide_count, narrow_count, capacity)
    returned = lax.all_to_all(
        lax.all_to_all(slot_back, "wide", split_axis=0, concat_axis=0, tiled=True),
        "narrow",
        split_axis=1,
        concat_axis=1,
        tiled=True,
    )
    grad_gates = jnp.take(returned.reshape(slot_count), target.reshape(-1)).reshape(
        token_count, top_count
    )
    return (grad_down[None], grad_a[None, None], grad_b[None, None], grad_gates)


def swap(x, axis, bits):
    count = lax.axis_size(axis)
    return lax.ppermute(x, axis, [(i, i ^ bits) for i in range(count)])


def after(x, *done):
    return lax.optimization_barrier((x,) + done)[0]


def call(kernel, outs, cost, *args, hbm=0, scratch=(), deps=(), out_specs=None):
    flops, moved = cost
    body = kernel
    if deps:

        def body(*refs):
            return kernel(*refs[: len(args)], *refs[len(args) + len(deps) :])

    return pl.pallas_call(
        body,
        out_shape=outs,
        in_specs=[pl.BlockSpec(memory_space=pltpu.HBM)] * hbm
        + [pl.BlockSpec(memory_space=pltpu.VMEM)] * (len(args) - hbm)
        + [pl.BlockSpec(memory_space=pl.ANY)] * len(deps),
        out_specs=jax.tree.map(lambda _: pl.BlockSpec(memory_space=pltpu.VMEM), outs)
        if out_specs is None
        else out_specs,
        scratch_shapes=scratch,
        compiler_params=pltpu.CompilerParams(vmem_limit_bytes=VMEM_LIMIT),
        cost_estimate=pl.CostEstimate(flops=flops, bytes_accessed=moved, transcendentals=0),
    )(*args, *deps)


def in_hbm(*arrays):
    return [pltpu.with_memory_space_constraint(x, pltpu.HBM) for x in arrays]


def peer(xors):
    wide_bits, narrow_bits = xors
    return (lax.axis_index("wide") ^ wide_bits) * lax.axis_size("narrow") + (
        lax.axis_index("narrow") ^ narrow_bits
    )


def first_kernel(
    grad_hbm, routes_hbm, gates_hbm, out_ref, token_ref, routes_ref, gates_ref, sems
):
    rows, features = grad_hbm.shape
    token_ref[...] = jnp.zeros(token_ref.shape, token_ref.dtype)
    copies = [
        pltpu.make_async_copy(routes_hbm, routes_ref, sems.at[0]),
        pltpu.make_async_copy(gates_hbm, gates_ref, sems.at[1]),
        pltpu.make_async_copy(grad_hbm, out_ref.at[:, pl.ds(0, features)], sems.at[2]),
    ]
    for copy in copies:
        copy.start()
    copies[0].wait()
    copies[1].wait()
    routes = routes_ref[...]
    gates = gates_ref[...].astype(jnp.float32)
    ids = lax.broadcasted_iota(jnp.int32, (LANES, rows), 0)
    table = jnp.zeros((LANES, rows), jnp.float32)
    for k in range(routes.shape[0]):
        table = table + jnp.where(ids == routes[k : k + 1, :], gates[k : k + 1, :], 0.0)
    table = jnp.concatenate([table, jnp.zeros((LANES, LANES - rows), jnp.float32)], axis=1)
    out_ref[:, features:] = table.T[:rows, :].astype(out_ref.dtype)
    copies[2].wait()


def hidden_kernel(
    order, rows, pre_gate_hbm, pre_up_hbm, hidden_ref, rest_ref, pre_gate_ref, pre_up_ref, sems
):
    copies = [
        pltpu.make_async_copy(pre_gate_hbm, pre_gate_ref, sems.at[0]),
        pltpu.make_async_copy(pre_up_hbm, pre_up_ref, sems.at[1]),
    ]
    for copy in copies:
        copy.start()
    for copy in copies:
        copy.wait()
    half = len(order) // 2
    for place, xors in enumerate(order):
        source = pl.ds(pl.multiple_of(peer(xors) * rows, rows), rows)
        value = pre_gate_ref[source, :].astype(jnp.float32)
        up = pre_up_ref[source, :].astype(jnp.float32)
        result = (value * jax.nn.sigmoid(value) * up).astype(hidden_ref.dtype)
        hidden_ref[place * rows : (place + 1) * rows, :] = result
        if place >= half:
            rest_ref[(place - half) * rows : (place - half + 1) * rows, :] = result


def turn_kernel(one_hbm, two_ref, *refs):
    one_ref, sems = refs[-2:]
    outs = refs[:-2]
    units, features = one_ref.shape
    cut = outs[0].shape[0]
    copies = [
        pltpu.make_async_copy(
            one_hbm.at[pl.ds(at, LANES)], one_ref.at[pl.ds(at, LANES)], sems.at[step]
        )
        for step, at in enumerate(range(0, units, LANES))
    ]
    for copy in copies:
        copy.start()
    for held, parts, waits in ((two_ref, outs[PARTS:], ()), (one_ref, outs[:PARTS], copies)):
        for step, at in enumerate(range(0, units, LANES)):
            if waits:
                waits[step].wait()
            for to in range(0, features, LANES):
                line = to % cut
                parts[to // cut][line : line + LANES, at : at + LANES] = held[
                    at : at + LANES, to : to + LANES
                ].T


def back_kernel(features, blocks, columns, hidden_ref, other_hidden_ref, *refs):
    group_refs, refs = refs[:blocks], refs[blocks:]
    turned_refs, refs = refs[: 2 * PARTS], refs[2 * PARTS :]
    back_ref, other_back_ref, sums_ref, own_ref = refs
    held = jnp.concatenate([group_ref[...] for group_ref in group_refs], axis=0)
    rows = held.shape[0]
    for expert, (act_ref, result_ref) in enumerate(
        ((hidden_ref, back_ref), (other_hidden_ref, other_back_ref))
    ):
        back = jnp.zeros(result_ref.shape, jnp.float32)
        for part in range(PARTS):
            part_ref = turned_refs[expert * PARTS + part]
            depth = part_ref.shape[0]
            back = back + jnp.dot(
                held[:, part * depth : (part + 1) * depth],
                part_ref[...],
                preferred_element_type=jnp.float32,
            )
        result_ref[...] = back
        product = act_ref[:rows, :].astype(jnp.float32) * back
        folded = product[:, :LANES]
        for at in range(LANES, product.shape[1], LANES):
            folded = folded + product[:, at : at + LANES]
        for at in range(0, rows, LANES):
            row = (expert * rows + at) // LANES
            sums_ref[row : row + 1, :] = jnp.sum(
                folded[at : at + LANES, :].T, axis=0, keepdims=True
            )
    copy_columns(features, columns, 0, group_refs, own_ref)


def copy_columns(features, columns, bits, group_refs, out_ref):
    start = pl.multiple_of((lax.axis_index("dp") ^ bits) * columns, columns)
    step = out_ref.shape[0] // len(group_refs)
    for block, group_ref in enumerate(group_refs):
        here = slice(block * step, (block + 1) * step)
        out_ref[here, :columns] = group_ref[:, pl.ds(start, columns)]
        out_ref[here, columns:] = group_ref[:, features:]


def cut_kernel(features, columns, blocks, *refs):
    for bits, cut_ref in enumerate(refs[blocks:], 1):
        copy_columns(features, columns, bits, refs[:blocks], cut_ref)


def own_gates(table):
    lane = lax.broadcasted_iota(jnp.int32, table.shape, 1)
    return jnp.sum(
        jnp.where(lane == peer((0, 0)), table.astype(jnp.float32), 0.0), axis=1, keepdims=True
    )


def grads_kernel(
    order,
    rows,
    columns,
    held_ref,
    rest_ref,
    back_ref,
    rest_back_ref,
    hidden_ref,
    pre_gate_ref,
    pre_up_ref,
    grad_gate_ref,
    grad_up_ref,
    scaled_ref,
):
    half = len(order) // 2
    for place, xors in enumerate(order):
        tokens_ref, products_ref = ((held_ref, back_ref), (rest_ref, rest_back_ref))[place // half]
        there = slice((place % half) * rows, (place % half + 1) * rows)
        gate = own_gates(tokens_ref[there, columns:])
        here = slice(place * rows, (place + 1) * rows)
        source = pl.ds(pl.multiple_of(peer(xors) * rows, rows), rows)
        value = pre_gate_ref[source, :].astype(jnp.float32)
        up = pre_up_ref[source, :].astype(jnp.float32)
        sig = jax.nn.sigmoid(value)
        carried = gate * products_ref[there, :]
        grad_gate_ref[source, :] = (carried * up * sig * (1.0 + value * (1.0 - sig))).astype(
            grad_gate_ref.dtype
        )
        grad_up_ref[source, :] = (carried * value * sig).astype(grad_up_ref.dtype)
        scaled_ref[here, :] = (gate * hidden_ref[here, :].astype(jnp.float32)).astype(
            scaled_ref.dtype
        )


def scale(hidden, table):
    return (own_gates(table) * hidden.astype(jnp.float32)).astype(jnp.bfloat16)


def down_kernel(scaled_ref, held_ref, rest_ref, *refs):
    out_ref, held_out_ref, sems = refs[-3:]
    columns = out_ref.shape[1]
    scaled, tokens = [scaled_ref[...]], [held_ref[:, :columns], rest_ref[:, :columns]]
    for at in range(0, len(refs) - 3, CUTS + 2):
        hidden_ref, *part_refs = refs[at : at + CUTS + 2]
        start = 0
        for part_ref in part_refs:
            stop = start + part_ref.shape[0]
            scaled.append(scale(hidden_ref[start:stop, :], part_ref[:, columns:]))
            tokens.append(part_ref[:, :columns])
            start = stop
    scaled = jnp.concatenate(scaled, axis=0)
    tokens = jnp.concatenate(tokens, axis=0)
    copies = []
    for at in range(0, out_ref.shape[0], 2 * LANES):
        here = pl.ds(at, 2 * LANES)
        held_out_ref[here, :] = lax.dot_general(
            scaled[:, at : at + 2 * LANES],
            tokens,
            (((0,), (0,)), ((), ())),
            preferred_element_type=jnp.float32,
        ).astype(out_ref.dtype)
        copies.append(
            pltpu.make_async_copy(held_out_ref.at[here], out_ref.at[here], sems.at[len(copies)])
        )
        copies[-1].start()
    for copy in copies:
        copy.wait()


def pick_kernel(order, back_order, rows, routes_ref, sums_ref, out_ref):
    routes = routes_ref[...]
    total = jnp.zeros(out_ref.shape, jnp.float32)
    per = sums_ref.shape[1] // 2
    for line, (wide_bits, narrow_bits) in enumerate(back_order):
        start = order.index((wide_bits, narrow_bits)) * rows
        at = start % LANES
        for expert in range(2):
            row = expert * per + start // LANES
            found = sums_ref[line, row : row + 1, :][:, at : at + rows]
            chosen = routes == peer((wide_bits ^ expert, narrow_bits))
            total = total + jnp.where(chosen, found, 0.0)
    out_ref[...] = total


def shards_gather(out_grad, routes, gates, pre_gate, pre_up, down_weight):
    dp_count = lax.axis_size("dp")
    wide_count = lax.axis_size("wide")
    narrow_count = lax.axis_size("narrow")
    rows, features = out_grad.shape
    slot_count, units = pre_gate.shape[2:]
    half_count = slot_count // 2
    columns = features // dp_count
    routes_t = routes.T
    gates_t = gates.T
    pre_gate = pre_gate[0, 0]
    pre_up = pre_up[0, 0]
    weight = down_weight[0]
    bf16, f32 = jnp.bfloat16, jnp.float32
    shape = jax.ShapeDtypeStruct

    near = max(narrow_count // 2, 1)
    wide_bits = [1 << b for b in range(1, wide_count.bit_length() - 1)]
    reach = [0] + list(range(near, narrow_count)) + list(range(1, near))
    order = [(0, bits) for bits in reach]
    for bits in wide_bits + [1]:
        order += [(w ^ bits, n) for w, n in order]
    order = tuple(order)

    payload, token = call(
        first_kernel,
        (shape((rows, features + LANES), bf16), shape((8, LANES), f32)),
        (rows * features, 4 * rows * features),
        *in_hbm(out_grad, routes_t, gates_t),
        hbm=3,
        scratch=[
            pltpu.VMEM(routes_t.shape, routes_t.dtype),
            pltpu.VMEM(gates_t.shape, gates_t.dtype),
            pltpu.SemaphoreType.DMA((3,)),
        ],
    )
    hidden, rest_hidden = call(
        functools.partial(hidden_kernel, order, rows),
        (shape((slot_count, units), bf16), shape((half_count, units), bf16)),
        (20 * slot_count * units, 6 * slot_count * units),
        *in_hbm(pre_gate, pre_up),
        hbm=2,
        deps=(token,),
        scratch=[
            pltpu.VMEM(pre_gate.shape, pre_gate.dtype),
            pltpu.VMEM(pre_up.shape, pre_up.dtype),
            pltpu.SemaphoreType.DMA((2,)),
        ],
    )
    other_weight = swap(after(weight, token), "wide", 1)
    along = [swap(payload, "narrow", bits) if bits else payload for bits in reach]
    turned = call(
        turn_kernel,
        (shape((features // PARTS, units), bf16),) * (2 * PARTS),
        (0, 8 * features * units),
        *in_hbm(weight),
        other_weight,
        hbm=1,
        deps=(token,),
        scratch=[
            pltpu.VMEM(weight.shape, weight.dtype),
            pltpu.SemaphoreType.DMA((units // LANES,)),
        ],
    )
    over = [swap(hidden, "dp", bits) for bits in range(1, dp_count)]
    other_hidden = swap(after(rest_hidden, *along[near:]), "wide", 1)
    groups = [jnp.concatenate(along[:near], axis=0)]
    if along[near:]:
        groups.append(jnp.concatenate(along[near:], axis=0))
    for bits in wide_bits:
        groups += [swap(group, "wide", bits) for group in groups]
    middle = len(groups) // 2
    groups[middle] = after(groups[middle], *turned)
    cuts = call(
        functools.partial(cut_kernel, features, columns, len(groups)),
        (shape((half_count, columns + LANES), bf16),) * (dp_count - 1),
        (0, 4 * half_count * columns),
        *groups,
    )
    crossed = [swap(cut, "dp", bits) for bits, cut in enumerate(cuts, 1)]
    back, other_back, sums, held = call(
        functools.partial(back_kernel, features, len(groups), columns),
        (
            shape((half_count, units), f32),
            shape((half_count, units), f32),
            shape((slot_count // LANES, LANES), f32),
            shape((half_count, columns + LANES), bf16),
        ),
        (2 * slot_count * units * features, 4 * units * features),
        hidden,
        other_hidden,
        *groups,
        *turned,
    )
    found = sums[None]
    back_order = [(0, 0)]
    for bits in wide_bits:
        found = jnp.concatenate([after(found, *over), swap(found, "wide", bits)], axis=0)
        back_order += [(w ^ bits, n) for w, n in back_order]
    rest = swap(held, "wide", 1)
    rest_back = swap(other_back, "wide", 1)
    grad_a, grad_b, scaled = call(
        functools.partial(grads_kernel, order, rows, columns),
        (shape((slot_count, units), bf16),) * 3,
        (30 * slot_count * units, 12 * slot_count * units),
        held,
        rest,
        back,
        rest_back,
        hidden,
        pre_gate,
        pre_up,
    )
    steps = [1 << b for b in range(narrow_count.bit_length() - 1)]
    for bits in steps[:-1]:
        found = jnp.concatenate([after(found, scaled), swap(found, "narrow", bits)], axis=0)
        back_order += [(w, n ^ bits) for w, n in back_order]
    others = []
    cut = half_count // CUTS
    for hidden_there, one in zip(over, crossed):
        others += [hidden_there, one]
        others += [swap(one[at : at + cut], "wide", 1) for at in range(0, half_count, cut)]
    grad_down = call(
        down_kernel,
        shape((units, columns), bf16),
        (2 * dp_count * slot_count * units * columns, 4 * units * columns),
        scaled,
        held,
        rest,
        *others,
        out_specs=pl.BlockSpec(memory_space=pltpu.HBM),
        scratch=[
            pltpu.VMEM((units, columns), bf16),
            pltpu.SemaphoreType.DMA((units // (2 * LANES),)),
        ],
    )
    for bits in steps[-1:]:
        found = jnp.concatenate([after(found, grad_down), swap(found, "narrow", bits)], axis=0)
        back_order += [(w, n ^ bits) for w, n in back_order]
    picked = call(
        functools.partial(pick_kernel, order, tuple(back_order), rows),
        shape(routes_t.shape, f32),
        (slot_count, slot_count),
        routes_t,
        found,
    )
    return (grad_down[None], grad_a[None, None], grad_b[None, None], picked.T)


def shards(out_grad, routes, gates, pre_gate, pre_up, down_weight):
    wide_count = lax.axis_size("wide")
    narrow_count = lax.axis_size("narrow")
    experts = wide_count * narrow_count
    rows = out_grad.shape[0]
    slot_count = pre_gate.shape[2]
    whole_blocks = (
        slot_count == experts * rows
        and wide_count > 1
        and all(n & (n - 1) == 0 for n in (lax.axis_size("dp"), wide_count, narrow_count))
        and experts <= LANES
        and LANES % rows == 0
        and (slot_count // 2) % LANES == 0
    )
    plan = shards_gather if whole_blocks else shards_exchange
    return plan(out_grad, routes, gates, pre_gate, pre_up, down_weight)


def solution(mesh):
    placed = (
        P(("dp", "wide", "narrow"), None),
        P(("dp", "wide", "narrow"), None),
        P(("dp", "wide", "narrow"), None),
        P("dp", ("wide", "narrow"), None, None),
        P("dp", ("wide", "narrow"), None, None),
        P(("wide", "narrow"), None, None),
    )
    return jax.shard_map(
        shards,
        mesh=mesh,
        in_specs=placed,
        out_specs=(
            P(("wide", "narrow"), None, "dp"),
            P("dp", ("wide", "narrow"), None, None),
            P("dp", ("wide", "narrow"), None, None),
            P(("dp", "wide", "narrow"), None),
        ),
        check_vma=False,
    )
```

```python
import functools

import jax
import jax.numpy as jnp
from jax import lax
from jax.experimental import pallas as pl
from jax.experimental.pallas import tpu as pltpu
from jax.sharding import PartitionSpec as P

LANES = 128
CUTS = 2
PARTS = 4
VMEM_LIMIT = 14 * 1024 * 1024


def shards_exchange(out_grad, routes, gates, pre_gate, pre_up, down_weight):
    wide_count = lax.axis_size("wide")
    narrow_count = lax.axis_size("narrow")
    experts = wide_count * narrow_count
    token_count, top_count = routes.shape
    slot_count = pre_gate.shape[2]
    capacity = slot_count // experts
    expert_ids = jnp.arange(experts, dtype=jnp.int32)
    named_hits = (routes[:, :, None] == expert_ids[None, None, :]).astype(jnp.int32)
    hit_counts = jnp.sum(named_hits, axis=1)
    before = jnp.cumsum(hit_counts, axis=0) - hit_counts
    position = jnp.sum(named_hits * before[:, None, :], axis=2)
    target = routes * capacity + position
    slot_ids = jnp.arange(slot_count, dtype=jnp.int32)
    placed = target[:, :, None] == slot_ids[None, None, :]
    choose = jnp.sum(placed.astype(jnp.bfloat16), axis=1)
    outgoing = lax.dot_general(
        choose, out_grad, (((0,), (0,)), ((), ())), preferred_element_type=jnp.float32
    ).astype(jnp.bfloat16)
    gate_out = jnp.sum(
        jnp.where(placed, gates[:, :, None].astype(jnp.float32), 0.0), axis=(0, 1)
    ).astype(jnp.bfloat16)
    outgoing = outgoing.reshape(wide_count, narrow_count, capacity, outgoing.shape[1])
    gate_out = gate_out.reshape(wide_count, narrow_count, capacity)
    incoming, gate_in = (
        lax.all_to_all(
            lax.all_to_all(outgoing, "wide", split_axis=0, concat_axis=0, tiled=True),
            "narrow",
            split_axis=1,
            concat_axis=1,
            tiled=True,
        ),
        lax.all_to_all(
            lax.all_to_all(gate_out, "wide", split_axis=0, concat_axis=0, tiled=True),
            "narrow",
            split_axis=1,
            concat_axis=1,
            tiled=True,
        ),
    )
    routed_rows = incoming.reshape(slot_count, incoming.shape[3])
    gate_col = gate_in.reshape(slot_count).astype(jnp.float32)
    gate_pre = pre_gate[0, 0].astype(jnp.float32)
    up_pre = pre_up[0, 0].astype(jnp.float32)
    weight = down_weight[0]
    sigmoid_a = jax.nn.sigmoid(gate_pre)
    hidden = (gate_pre * sigmoid_a * up_pre).astype(jnp.bfloat16)
    back_prop = lax.dot_general(
        routed_rows, weight, (((1,), (1,)), ((), ())), preferred_element_type=jnp.float32
    )
    slot_grad = jnp.sum(hidden.astype(jnp.float32) * back_prop, axis=1)
    carried = gate_col[:, None] * back_prop
    grad_a = (carried * up_pre * sigmoid_a * (1.0 + gate_pre * (1.0 - sigmoid_a))).astype(
        jnp.bfloat16
    )
    grad_b = (carried * gate_pre * sigmoid_a).astype(jnp.bfloat16)
    scaled = (gate_col[:, None] * hidden.astype(jnp.float32)).astype(jnp.bfloat16)
    all_scaled = lax.all_gather(scaled, "dp", axis=0, tiled=True)
    columns = lax.all_to_all(routed_rows, "dp", split_axis=1, concat_axis=0, tiled=True)
    grad_down = lax.dot_general(
        all_scaled, columns, (((0,), (0,)), ((), ())), preferred_element_type=jnp.float32
    ).astype(jnp.bfloat16)
    slot_back = slot_grad.reshape(wide_count, narrow_count, capacity)
    returned = lax.all_to_all(
        lax.all_to_all(slot_back, "wide", split_axis=0, concat_axis=0, tiled=True),
        "narrow",
        split_axis=1,
        concat_axis=1,
        tiled=True,
    )
    grad_gates = jnp.take(returned.reshape(slot_count), target.reshape(-1)).reshape(
        token_count, top_count
    )
    return (grad_down[None], grad_a[None, None], grad_b[None, None], grad_gates)


def swap(x, axis, bits):
    count = lax.axis_size(axis)
    return lax.ppermute(x, axis, [(i, i ^ bits) for i in range(count)])


def after(x, *done):
    return lax.optimization_barrier((x,) + done)[0]


def call(kernel, outs, cost, *args, hbm=0, scratch=(), deps=(), out_specs=None):
    flops, moved = cost
    body = kernel
    if deps:

        def body(*refs):
            return kernel(*refs[: len(args)], *refs[len(args) + len(deps) :])

    return pl.pallas_call(
        body,
        out_shape=outs,
        in_specs=[pl.BlockSpec(memory_space=pltpu.HBM)] * hbm
        + [pl.BlockSpec(memory_space=pltpu.VMEM)] * (len(args) - hbm)
        + [pl.BlockSpec(memory_space=pl.ANY)] * len(deps),
        out_specs=jax.tree.map(lambda _: pl.BlockSpec(memory_space=pltpu.VMEM), outs)
        if out_specs is None
        else out_specs,
        scratch_shapes=scratch,
        compiler_params=pltpu.CompilerParams(vmem_limit_bytes=VMEM_LIMIT),
        cost_estimate=pl.CostEstimate(flops=flops, bytes_accessed=moved, transcendentals=0),
    )(*args, *deps)


def in_hbm(*arrays):
    return [pltpu.with_memory_space_constraint(x, pltpu.HBM) for x in arrays]


def peer(xors):
    wide_bits, narrow_bits = xors
    return (lax.axis_index("wide") ^ wide_bits) * lax.axis_size("narrow") + (
        lax.axis_index("narrow") ^ narrow_bits
    )


def first_kernel(
    grad_hbm, routes_hbm, gates_hbm, out_ref, token_ref, routes_ref, gates_ref, sems
):
    rows, features = grad_hbm.shape
    token_ref[...] = jnp.zeros(token_ref.shape, token_ref.dtype)
    copies = [
        pltpu.make_async_copy(routes_hbm, routes_ref, sems.at[0]),
        pltpu.make_async_copy(gates_hbm, gates_ref, sems.at[1]),
        pltpu.make_async_copy(grad_hbm, out_ref.at[:, pl.ds(0, features)], sems.at[2]),
    ]
    for copy in copies:
        copy.start()
    copies[0].wait()
    copies[1].wait()
    routes = routes_ref[...]
    gates = gates_ref[...].astype(jnp.float32)
    ids = lax.broadcasted_iota(jnp.int32, (LANES, rows), 0)
    table = jnp.zeros((LANES, rows), jnp.float32)
    for k in range(routes.shape[0]):
        table = table + jnp.where(ids == routes[k : k + 1, :], gates[k : k + 1, :], 0.0)
    table = jnp.concatenate([table, jnp.zeros((LANES, LANES - rows), jnp.float32)], axis=1)
    out_ref[:, features:] = table.T[:rows, :].astype(out_ref.dtype)
    copies[2].wait()


def hidden_kernel(
    order, rows, pre_gate_hbm, pre_up_hbm, hidden_ref, rest_ref, pre_gate_ref, pre_up_ref, sems
):
    copies = [
        pltpu.make_async_copy(pre_gate_hbm, pre_gate_ref, sems.at[0]),
        pltpu.make_async_copy(pre_up_hbm, pre_up_ref, sems.at[1]),
    ]
    for copy in copies:
        copy.start()
    for copy in copies:
        copy.wait()
    half = len(order) // 2
    for place, xors in enumerate(order):
        source = pl.ds(pl.multiple_of(peer(xors) * rows, rows), rows)
        value = pre_gate_ref[source, :].astype(jnp.float32)
        up = pre_up_ref[source, :].astype(jnp.float32)
        result = (value * jax.nn.sigmoid(value) * up).astype(hidden_ref.dtype)
        hidden_ref[place * rows : (place + 1) * rows, :] = result
        if place >= half:
            rest_ref[(place - half) * rows : (place - half + 1) * rows, :] = result


def turn_kernel(one_hbm, two_ref, *refs):
    one_ref, sems = refs[-2:]
    outs = refs[:-2]
    units, features = one_ref.shape
    cut = outs[0].shape[0]
    copies = [
        pltpu.make_async_copy(
            one_hbm.at[pl.ds(at, LANES)], one_ref.at[pl.ds(at, LANES)], sems.at[step]
        )
        for step, at in enumerate(range(0, units, LANES))
    ]
    for copy in copies:
        copy.start()
    for held, parts, waits in ((two_ref, outs[PARTS:], ()), (one_ref, outs[:PARTS], copies)):
        for step, at in enumerate(range(0, units, LANES)):
            if waits:
                waits[step].wait()
            for to in range(0, features, LANES):
                line = to % cut
                parts[to // cut][line : line + LANES, at : at + LANES] = held[
                    at : at + LANES, to : to + LANES
                ].T


def back_kernel(features, blocks, columns, hidden_ref, other_hidden_ref, *refs):
    group_refs, refs = refs[:blocks], refs[blocks:]
    turned_refs, refs = refs[: 2 * PARTS], refs[2 * PARTS :]
    back_ref, other_back_ref, sums_ref, own_ref = refs
    held = jnp.concatenate([group_ref[...] for group_ref in group_refs], axis=0)
    rows = held.shape[0]
    for expert, (act_ref, result_ref) in enumerate(
        ((hidden_ref, back_ref), (other_hidden_ref, other_back_ref))
    ):
        back = jnp.zeros(result_ref.shape, jnp.float32)
        for part in range(PARTS):
            part_ref = turned_refs[expert * PARTS + part]
            depth = part_ref.shape[0]
            back = back + jnp.dot(
                held[:, part * depth : (part + 1) * depth],
                part_ref[...],
                preferred_element_type=jnp.float32,
            )
        result_ref[...] = back
        product = act_ref[:rows, :].astype(jnp.float32) * back
        folded = product[:, :LANES]
        for at in range(LANES, product.shape[1], LANES):
            folded = folded + product[:, at : at + LANES]
        for at in range(0, rows, LANES):
            row = (expert * rows + at) // LANES
            sums_ref[row : row + 1, :] = jnp.sum(
                folded[at : at + LANES, :].T, axis=0, keepdims=True
            )
    copy_columns(features, columns, 0, group_refs, own_ref)


def copy_columns(features, columns, bits, group_refs, out_ref):
    start = pl.multiple_of((lax.axis_index("dp") ^ bits) * columns, columns)
    step = out_ref.shape[0] // len(group_refs)
    for block, group_ref in enumerate(group_refs):
        here = slice(block * step, (block + 1) * step)
        out_ref[here, :columns] = group_ref[:, pl.ds(start, columns)]
        out_ref[here, columns:] = group_ref[:, features:]


def cut_kernel(features, columns, blocks, *refs):
    for bits, cut_ref in enumerate(refs[blocks:], 1):
        copy_columns(features, columns, bits, refs[:blocks], cut_ref)


def own_gates(table):
    lane = lax.broadcasted_iota(jnp.int32, table.shape, 1)
    return jnp.sum(
        jnp.where(lane == peer((0, 0)), table.astype(jnp.float32), 0.0), axis=1, keepdims=True
    )


def slopes_kernel(order, rows, pre_gate_ref, pre_up_ref, gate_slope_ref, up_slope_ref):
    for place, xors in enumerate(order):
        here = slice(place * rows, (place + 1) * rows)
        source = pl.ds(pl.multiple_of(peer(xors) * rows, rows), rows)
        value = pre_gate_ref[source, :].astype(jnp.float32)
        up = pre_up_ref[source, :].astype(jnp.float32)
        sig = jax.nn.sigmoid(value)
        gate_slope_ref[here, :] = up * sig * (1.0 + value * (1.0 - sig))
        up_slope_ref[here, :] = value * sig


def grads_kernel(
    order,
    rows,
    columns,
    held_ref,
    rest_ref,
    back_ref,
    rest_back_ref,
    hidden_ref,
    gate_slope_ref,
    up_slope_ref,
    grad_gate_ref,
    grad_up_ref,
    scaled_ref,
):
    half = len(order) // 2
    for place, xors in enumerate(order):
        tokens_ref, products_ref = ((held_ref, back_ref), (rest_ref, rest_back_ref))[place // half]
        there = slice((place % half) * rows, (place % half + 1) * rows)
        gate = own_gates(tokens_ref[there, columns:])
        here = slice(place * rows, (place + 1) * rows)
        source = pl.ds(pl.multiple_of(peer(xors) * rows, rows), rows)
        carried = gate * products_ref[there, :]
        grad_gate_ref[source, :] = (carried * gate_slope_ref[here, :]).astype(grad_gate_ref.dtype)
        grad_up_ref[source, :] = (carried * up_slope_ref[here, :]).astype(grad_up_ref.dtype)
        scaled_ref[here, :] = (gate * hidden_ref[here, :].astype(jnp.float32)).astype(
            scaled_ref.dtype
        )


def scale(hidden, table):
    return (own_gates(table) * hidden.astype(jnp.float32)).astype(jnp.bfloat16)


def down_kernel(scaled_ref, held_ref, rest_ref, *refs):
    out_ref, held_out_ref, sems = refs[-3:]
    columns = out_ref.shape[1]
    scaled, tokens = [scaled_ref[...]], [held_ref[:, :columns], rest_ref[:, :columns]]
    for at in range(0, len(refs) - 3, CUTS + 2):
        hidden_ref, *part_refs = refs[at : at + CUTS + 2]
        start = 0
        for part_ref in part_refs:
            stop = start + part_ref.shape[0]
            scaled.append(scale(hidden_ref[start:stop, :], part_ref[:, columns:]))
            tokens.append(part_ref[:, :columns])
            start = stop
    scaled = jnp.concatenate(scaled, axis=0)
    tokens = jnp.concatenate(tokens, axis=0)
    copies = []
    for at in range(0, out_ref.shape[0], 2 * LANES):
        here = pl.ds(at, 2 * LANES)
        held_out_ref[here, :] = lax.dot_general(
            scaled[:, at : at + 2 * LANES],
            tokens,
            (((0,), (0,)), ((), ())),
            preferred_element_type=jnp.float32,
        ).astype(out_ref.dtype)
        copies.append(
            pltpu.make_async_copy(held_out_ref.at[here], out_ref.at[here], sems.at[len(copies)])
        )
        copies[-1].start()
    for copy in copies:
        copy.wait()


def pick_kernel(order, back_order, rows, routes_ref, sums_ref, out_ref):
    routes = routes_ref[...]
    total = jnp.zeros(out_ref.shape, jnp.float32)
    per = sums_ref.shape[1] // 2
    for line, (wide_bits, narrow_bits) in enumerate(back_order):
        start = order.index((wide_bits, narrow_bits)) * rows
        at = start % LANES
        for expert in range(2):
            row = expert * per + start // LANES
            found = sums_ref[line, row : row + 1, :][:, at : at + rows]
            chosen = routes == peer((wide_bits ^ expert, narrow_bits))
            total = total + jnp.where(chosen, found, 0.0)
    out_ref[...] = total


def shards_gather(out_grad, routes, gates, pre_gate, pre_up, down_weight):
    dp_count = lax.axis_size("dp")
    wide_count = lax.axis_size("wide")
    narrow_count = lax.axis_size("narrow")
    rows, features = out_grad.shape
    slot_count, units = pre_gate.shape[2:]
    half_count = slot_count // 2
    columns = features // dp_count
    routes_t = routes.T
    gates_t = gates.T
    pre_gate = pre_gate[0, 0]
    pre_up = pre_up[0, 0]
    weight = down_weight[0]
    bf16, f32 = jnp.bfloat16, jnp.float32
    shape = jax.ShapeDtypeStruct

    near = max(narrow_count // 2, 1)
    wide_bits = [1 << b for b in range(1, wide_count.bit_length() - 1)]
    reach = [0] + list(range(near, narrow_count)) + list(range(1, near))
    order = [(0, bits) for bits in reach]
    for bits in wide_bits + [1]:
        order += [(w ^ bits, n) for w, n in order]
    order = tuple(order)

    payload, token = call(
        first_kernel,
        (shape((rows, features + LANES), bf16), shape((8, LANES), f32)),
        (rows * features, 4 * rows * features),
        *in_hbm(out_grad, routes_t, gates_t),
        hbm=3,
        scratch=[
            pltpu.VMEM(routes_t.shape, routes_t.dtype),
            pltpu.VMEM(gates_t.shape, gates_t.dtype),
            pltpu.SemaphoreType.DMA((3,)),
        ],
    )
    hidden, rest_hidden = call(
        functools.partial(hidden_kernel, order, rows),
        (shape((slot_count, units), bf16), shape((half_count, units), bf16)),
        (20 * slot_count * units, 6 * slot_count * units),
        *in_hbm(pre_gate, pre_up),
        hbm=2,
        deps=(token,),
        scratch=[
            pltpu.VMEM(pre_gate.shape, pre_gate.dtype),
            pltpu.VMEM(pre_up.shape, pre_up.dtype),
            pltpu.SemaphoreType.DMA((2,)),
        ],
    )
    other_weight = swap(after(weight, token), "wide", 1)
    along = [swap(payload, "narrow", bits) if bits else payload for bits in reach]
    turned = call(
        turn_kernel,
        (shape((features // PARTS, units), bf16),) * (2 * PARTS),
        (0, 8 * features * units),
        *in_hbm(weight),
        other_weight,
        hbm=1,
        deps=(token,),
        scratch=[
            pltpu.VMEM(weight.shape, weight.dtype),
            pltpu.SemaphoreType.DMA((units // LANES,)),
        ],
    )
    over = [swap(hidden, "dp", bits) for bits in range(1, dp_count)]
    other_hidden = swap(after(rest_hidden, *along[near:]), "wide", 1)
    groups = [jnp.concatenate(along[:near], axis=0)]
    if along[near:]:
        groups.append(jnp.concatenate(along[near:], axis=0))
    for bits in wide_bits:
        groups += [swap(group, "wide", bits) for group in groups]
    middle = len(groups) // 2
    groups[middle] = after(groups[middle], *turned)
    cuts = call(
        functools.partial(cut_kernel, features, columns, len(groups)),
        (shape((half_count, columns + LANES), bf16),) * (dp_count - 1),
        (0, 4 * half_count * columns),
        *groups,
    )
    crossed = [swap(cut, "dp", bits) for bits, cut in enumerate(cuts, 1)]
    back, other_back, sums, held = call(
        functools.partial(back_kernel, features, len(groups), columns),
        (
            shape((half_count, units), f32),
            shape((half_count, units), f32),
            shape((slot_count // LANES, LANES), f32),
            shape((half_count, columns + LANES), bf16),
        ),
        (2 * slot_count * units * features, 4 * units * features),
        hidden,
        other_hidden,
        *groups,
        *turned,
    )
    slopes = call(
        functools.partial(slopes_kernel, order, rows),
        (shape((slot_count, units), f32),) * 2,
        (20 * slot_count * units, 12 * slot_count * units),
        pre_gate,
        pre_up,
        deps=(sums,),
    )
    found = sums[None]
    back_order = [(0, 0)]
    for bits in wide_bits:
        found = jnp.concatenate([after(found, *over, *slopes), swap(found, "wide", bits)], axis=0)
        back_order += [(w ^ bits, n) for w, n in back_order]
    rest = swap(held, "wide", 1)
    rest_back = swap(other_back, "wide", 1)
    grad_a, grad_b, scaled = call(
        functools.partial(grads_kernel, order, rows, columns),
        (shape((slot_count, units), bf16),) * 3,
        (30 * slot_count * units, 12 * slot_count * units),
        held,
        rest,
        back,
        rest_back,
        hidden,
        *slopes,
    )
    steps = [1 << b for b in range(narrow_count.bit_length() - 1)]
    for bits in steps[:-1]:
        found = jnp.concatenate([after(found, scaled), swap(found, "narrow", bits)], axis=0)
        back_order += [(w, n ^ bits) for w, n in back_order]
    others = []
    cut = half_count // CUTS
    for hidden_there, one in zip(over, crossed):
        others += [hidden_there, one]
        others += [swap(one[at : at + cut], "wide", 1) for at in range(0, half_count, cut)]
    grad_down = call(
        down_kernel,
        shape((units, columns), bf16),
        (2 * dp_count * slot_count * units * columns, 4 * units * columns),
        scaled,
        held,
        rest,
        *others,
        out_specs=pl.BlockSpec(memory_space=pltpu.HBM),
        scratch=[
            pltpu.VMEM((units, columns), bf16),
            pltpu.SemaphoreType.DMA((units // (2 * LANES),)),
        ],
    )
    for bits in steps[-1:]:
        found = jnp.concatenate([after(found, grad_down), swap(found, "narrow", bits)], axis=0)
        back_order += [(w, n ^ bits) for w, n in back_order]
    picked = call(
        functools.partial(pick_kernel, order, tuple(back_order), rows),
        shape(routes_t.shape, f32),
        (slot_count, slot_count),
        routes_t,
        found,
    )
    return (grad_down[None], grad_a[None, None], grad_b[None, None], picked.T)


def shards(out_grad, routes, gates, pre_gate, pre_up, down_weight):
    wide_count = lax.axis_size("wide")
    narrow_count = lax.axis_size("narrow")
    experts = wide_count * narrow_count
    rows = out_grad.shape[0]
    slot_count = pre_gate.shape[2]
    whole_blocks = (
        slot_count == experts * rows
        and wide_count > 1
        and all(n & (n - 1) == 0 for n in (lax.axis_size("dp"), wide_count, narrow_count))
        and experts <= LANES
        and LANES % rows == 0
        and (slot_count // 2) % LANES == 0
    )
    plan = shards_gather if whole_blocks else shards_exchange
    return plan(out_grad, routes, gates, pre_gate, pre_up, down_weight)


def solution(mesh):
    placed = (
        P(("dp", "wide", "narrow"), None),
        P(("dp", "wide", "narrow"), None),
        P(("dp", "wide", "narrow"), None),
        P("dp", ("wide", "narrow"), None, None),
        P("dp", ("wide", "narrow"), None, None),
        P(("wide", "narrow"), None, None),
    )
    return jax.shard_map(
        shards,
        mesh=mesh,
        in_specs=placed,
        out_specs=(
            P(("wide", "narrow"), None, "dp"),
            P("dp", ("wide", "narrow"), None, None),
            P("dp", ("wide", "narrow"), None, None),
            P(("dp", "wide", "narrow"), None),
        ),
        check_vma=False,
    )
```

```python
import functools

import jax
import jax.numpy as jnp
from jax import lax
from jax.experimental import pallas as pl
from jax.experimental.pallas import tpu as pltpu
from jax.sharding import PartitionSpec as P

LANES = 128
CUTS = 2
PARTS = 4
VMEM_LIMIT = 14 * 1024 * 1024


def shards_exchange(out_grad, routes, gates, pre_gate, pre_up, down_weight):
    wide_count = lax.axis_size("wide")
    narrow_count = lax.axis_size("narrow")
    experts = wide_count * narrow_count
    token_count, top_count = routes.shape
    slot_count = pre_gate.shape[2]
    capacity = slot_count // experts
    expert_ids = jnp.arange(experts, dtype=jnp.int32)
    named_hits = (routes[:, :, None] == expert_ids[None, None, :]).astype(jnp.int32)
    hit_counts = jnp.sum(named_hits, axis=1)
    before = jnp.cumsum(hit_counts, axis=0) - hit_counts
    position = jnp.sum(named_hits * before[:, None, :], axis=2)
    target = routes * capacity + position
    slot_ids = jnp.arange(slot_count, dtype=jnp.int32)
    placed = target[:, :, None] == slot_ids[None, None, :]
    choose = jnp.sum(placed.astype(jnp.bfloat16), axis=1)
    outgoing = lax.dot_general(
        choose, out_grad, (((0,), (0,)), ((), ())), preferred_element_type=jnp.float32
    ).astype(jnp.bfloat16)
    gate_out = jnp.sum(
        jnp.where(placed, gates[:, :, None].astype(jnp.float32), 0.0), axis=(0, 1)
    ).astype(jnp.bfloat16)
    outgoing = outgoing.reshape(wide_count, narrow_count, capacity, outgoing.shape[1])
    gate_out = gate_out.reshape(wide_count, narrow_count, capacity)
    incoming, gate_in = (
        lax.all_to_all(
            lax.all_to_all(outgoing, "wide", split_axis=0, concat_axis=0, tiled=True),
            "narrow",
            split_axis=1,
            concat_axis=1,
            tiled=True,
        ),
        lax.all_to_all(
            lax.all_to_all(gate_out, "wide", split_axis=0, concat_axis=0, tiled=True),
            "narrow",
            split_axis=1,
            concat_axis=1,
            tiled=True,
        ),
    )
    routed_rows = incoming.reshape(slot_count, incoming.shape[3])
    gate_col = gate_in.reshape(slot_count).astype(jnp.float32)
    gate_pre = pre_gate[0, 0].astype(jnp.float32)
    up_pre = pre_up[0, 0].astype(jnp.float32)
    weight = down_weight[0]
    sigmoid_a = jax.nn.sigmoid(gate_pre)
    hidden = (gate_pre * sigmoid_a * up_pre).astype(jnp.bfloat16)
    back_prop = lax.dot_general(
        routed_rows, weight, (((1,), (1,)), ((), ())), preferred_element_type=jnp.float32
    )
    slot_grad = jnp.sum(hidden.astype(jnp.float32) * back_prop, axis=1)
    carried = gate_col[:, None] * back_prop
    grad_a = (carried * up_pre * sigmoid_a * (1.0 + gate_pre * (1.0 - sigmoid_a))).astype(
        jnp.bfloat16
    )
    grad_b = (carried * gate_pre * sigmoid_a).astype(jnp.bfloat16)
    scaled = (gate_col[:, None] * hidden.astype(jnp.float32)).astype(jnp.bfloat16)
    all_scaled = lax.all_gather(scaled, "dp", axis=0, tiled=True)
    columns = lax.all_to_all(routed_rows, "dp", split_axis=1, concat_axis=0, tiled=True)
    grad_down = lax.dot_general(
        all_scaled, columns, (((0,), (0,)), ((), ())), preferred_element_type=jnp.float32
    ).astype(jnp.bfloat16)
    slot_back = slot_grad.reshape(wide_count, narrow_count, capacity)
    returned = lax.all_to_all(
        lax.all_to_all(slot_back, "wide", split_axis=0, concat_axis=0, tiled=True),
        "narrow",
        split_axis=1,
        concat_axis=1,
        tiled=True,
    )
    grad_gates = jnp.take(returned.reshape(slot_count), target.reshape(-1)).reshape(
        token_count, top_count
    )
    return (grad_down[None], grad_a[None, None], grad_b[None, None], grad_gates)


def swap(x, axis, bits):
    count = lax.axis_size(axis)
    return lax.ppermute(x, axis, [(i, i ^ bits) for i in range(count)])


def after(x, *done):
    return lax.optimization_barrier((x,) + done)[0]


def call(kernel, outs, cost, *args, hbm=0, scratch=(), deps=(), out_specs=None):
    flops, moved = cost
    body = kernel
    if deps:

        def body(*refs):
            return kernel(*refs[: len(args)], *refs[len(args) + len(deps) :])

    return pl.pallas_call(
        body,
        out_shape=outs,
        in_specs=[pl.BlockSpec(memory_space=pltpu.HBM)] * hbm
        + [pl.BlockSpec(memory_space=pltpu.VMEM)] * (len(args) - hbm)
        + [pl.BlockSpec(memory_space=pl.ANY)] * len(deps),
        out_specs=jax.tree.map(lambda _: pl.BlockSpec(memory_space=pltpu.VMEM), outs)
        if out_specs is None
        else out_specs,
        scratch_shapes=scratch,
        compiler_params=pltpu.CompilerParams(vmem_limit_bytes=VMEM_LIMIT),
        cost_estimate=pl.CostEstimate(flops=flops, bytes_accessed=moved, transcendentals=0),
    )(*args, *deps)


def in_hbm(*arrays):
    return [pltpu.with_memory_space_constraint(x, pltpu.HBM) for x in arrays]


def peer(xors):
    wide_bits, narrow_bits = xors
    return (lax.axis_index("wide") ^ wide_bits) * lax.axis_size("narrow") + (
        lax.axis_index("narrow") ^ narrow_bits
    )


def first_kernel(
    grad_hbm, routes_hbm, gates_hbm, out_ref, token_ref, routes_ref, gates_ref, sems
):
    rows, features = grad_hbm.shape
    token_ref[...] = jnp.zeros(token_ref.shape, token_ref.dtype)
    copies = [
        pltpu.make_async_copy(routes_hbm, routes_ref, sems.at[0]),
        pltpu.make_async_copy(gates_hbm, gates_ref, sems.at[1]),
        pltpu.make_async_copy(grad_hbm, out_ref.at[:, pl.ds(0, features)], sems.at[2]),
    ]
    for copy in copies:
        copy.start()
    copies[0].wait()
    copies[1].wait()
    routes = routes_ref[...]
    gates = gates_ref[...].astype(jnp.float32)
    ids = lax.broadcasted_iota(jnp.int32, (LANES, rows), 0)
    table = jnp.zeros((LANES, rows), jnp.float32)
    for k in range(routes.shape[0]):
        table = table + jnp.where(ids == routes[k : k + 1, :], gates[k : k + 1, :], 0.0)
    table = jnp.concatenate([table, jnp.zeros((LANES, LANES - rows), jnp.float32)], axis=1)
    out_ref[:, features:] = table.T[:rows, :].astype(out_ref.dtype)
    copies[2].wait()


def hidden_kernel(
    order, rows, pre_gate_hbm, pre_up_hbm, hidden_ref, rest_ref, pre_gate_ref, pre_up_ref, sems
):
    copies = [
        pltpu.make_async_copy(pre_gate_hbm, pre_gate_ref, sems.at[0]),
        pltpu.make_async_copy(pre_up_hbm, pre_up_ref, sems.at[1]),
    ]
    for copy in copies:
        copy.start()
    for copy in copies:
        copy.wait()
    half = len(order) // 2
    for place, xors in enumerate(order):
        source = pl.ds(pl.multiple_of(peer(xors) * rows, rows), rows)
        value = pre_gate_ref[source, :].astype(jnp.float32)
        up = pre_up_ref[source, :].astype(jnp.float32)
        result = (value * jax.nn.sigmoid(value) * up).astype(hidden_ref.dtype)
        hidden_ref[place * rows : (place + 1) * rows, :] = result
        if place >= half:
            rest_ref[(place - half) * rows : (place - half + 1) * rows, :] = result


def turn_kernel(one_hbm, two_ref, *refs):
    one_ref, sems = refs[-2:]
    outs = refs[:-2]
    units, features = one_ref.shape
    cut = outs[0].shape[0]
    copies = [
        pltpu.make_async_copy(
            one_hbm.at[pl.ds(at, LANES)], one_ref.at[pl.ds(at, LANES)], sems.at[step]
        )
        for step, at in enumerate(range(0, units, LANES))
    ]
    for copy in copies:
        copy.start()
    for held, parts, waits in ((two_ref, outs[PARTS:], ()), (one_ref, outs[:PARTS], copies)):
        for step, at in enumerate(range(0, units, LANES)):
            if waits:
                waits[step].wait()
            for to in range(0, features, LANES):
                line = to % cut
                parts[to // cut][line : line + LANES, at : at + LANES] = held[
                    at : at + LANES, to : to + LANES
                ].T


def back_kernel(features, blocks, columns, hidden_ref, other_hidden_ref, *refs):
    group_refs, refs = refs[:blocks], refs[blocks:]
    turned_refs, refs = refs[: 2 * PARTS], refs[2 * PARTS :]
    back_ref, other_back_ref, sums_ref, own_ref = refs
    held = jnp.concatenate([group_ref[...] for group_ref in group_refs], axis=0)
    rows = held.shape[0]
    for expert, (act_ref, result_ref) in enumerate(
        ((hidden_ref, back_ref), (other_hidden_ref, other_back_ref))
    ):
        back = jnp.zeros(result_ref.shape, jnp.float32)
        for part in range(PARTS):
            part_ref = turned_refs[expert * PARTS + part]
            depth = part_ref.shape[0]
            back = back + jnp.dot(
                held[:, part * depth : (part + 1) * depth],
                part_ref[...],
                preferred_element_type=jnp.float32,
            )
        result_ref[...] = back
        product = act_ref[:rows, :].astype(jnp.float32) * back
        folded = product[:, :LANES]
        for at in range(LANES, product.shape[1], LANES):
            folded = folded + product[:, at : at + LANES]
        for at in range(0, rows, LANES):
            row = (expert * rows + at) // LANES
            sums_ref[row : row + 1, :] = jnp.sum(
                folded[at : at + LANES, :].T, axis=0, keepdims=True
            )
    copy_columns(features, columns, 0, group_refs, own_ref)


def copy_columns(features, columns, bits, group_refs, out_ref):
    start = pl.multiple_of((lax.axis_index("dp") ^ bits) * columns, columns)
    step = out_ref.shape[0] // len(group_refs)
    for block, group_ref in enumerate(group_refs):
        here = slice(block * step, (block + 1) * step)
        out_ref[here, :columns] = group_ref[:, pl.ds(start, columns)]
        out_ref[here, columns:] = group_ref[:, features:]


def cut_kernel(features, columns, blocks, *refs):
    for bits, cut_ref in enumerate(refs[blocks:], 1):
        copy_columns(features, columns, bits, refs[:blocks], cut_ref)


def own_gates(table):
    lane = lax.broadcasted_iota(jnp.int32, table.shape, 1)
    return jnp.sum(
        jnp.where(lane == peer((0, 0)), table.astype(jnp.float32), 0.0), axis=1, keepdims=True
    )


def slopes_kernel(order, rows, pre_gate_ref, pre_up_ref, gate_slope_ref, up_slope_ref):
    for place, xors in enumerate(order):
        here = slice(place * rows, (place + 1) * rows)
        source = pl.ds(pl.multiple_of(peer(xors) * rows, rows), rows)
        value = pre_gate_ref[source, :].astype(jnp.float32)
        up = pre_up_ref[source, :].astype(jnp.float32)
        sig = jax.nn.sigmoid(value)
        gate_slope_ref[here, :] = up * sig * (1.0 + value * (1.0 - sig))
        up_slope_ref[here, :] = value * sig


def grads_kernel(
    order,
    rows,
    columns,
    held_ref,
    rest_ref,
    back_ref,
    rest_back_ref,
    hidden_ref,
    gate_slope_ref,
    up_slope_ref,
    grad_gate_ref,
    grad_up_ref,
    scaled_ref,
):
    half = len(order) // 2
    for place, xors in enumerate(order):
        tokens_ref, products_ref = ((held_ref, back_ref), (rest_ref, rest_back_ref))[place // half]
        there = slice((place % half) * rows, (place % half + 1) * rows)
        gate = own_gates(tokens_ref[there, columns:])
        here = slice(place * rows, (place + 1) * rows)
        source = pl.ds(pl.multiple_of(peer(xors) * rows, rows), rows)
        carried = gate * products_ref[there, :]
        grad_gate_ref[source, :] = (carried * gate_slope_ref[here, :]).astype(grad_gate_ref.dtype)
        grad_up_ref[source, :] = (carried * up_slope_ref[here, :]).astype(grad_up_ref.dtype)
        scaled_ref[here, :] = (gate * hidden_ref[here, :].astype(jnp.float32)).astype(
            scaled_ref.dtype
        )


def scale(hidden, table):
    return (own_gates(table) * hidden.astype(jnp.float32)).astype(jnp.bfloat16)


def down_kernel(scaled_ref, held_ref, rest_ref, *refs):
    out_ref, held_out_ref, sems = refs[-3:]
    columns = out_ref.shape[1]
    scaled, tokens = [scaled_ref[...]], [held_ref[:, :columns], rest_ref[:, :columns]]
    for at in range(0, len(refs) - 3, CUTS + 2):
        hidden_ref, *part_refs = refs[at : at + CUTS + 2]
        start = 0
        for part_ref in part_refs:
            stop = start + part_ref.shape[0]
            scaled.append(scale(hidden_ref[start:stop, :], part_ref[:, columns:]))
            tokens.append(part_ref[:, :columns])
            start = stop
    scaled = jnp.concatenate(scaled, axis=0)
    tokens = jnp.concatenate(tokens, axis=0)
    copies = []
    for at in range(0, out_ref.shape[0], 2 * LANES):
        here = pl.ds(at, 2 * LANES)
        held_out_ref[here, :] = lax.dot_general(
            scaled[:, at : at + 2 * LANES],
            tokens,
            (((0,), (0,)), ((), ())),
            preferred_element_type=jnp.float32,
        ).astype(out_ref.dtype)
        copies.append(
            pltpu.make_async_copy(held_out_ref.at[here], out_ref.at[here], sems.at[len(copies)])
        )
        copies[-1].start()
    for copy in copies:
        copy.wait()


def pick_kernel(order, back_order, rows, routes_ref, sums_ref, out_ref):
    routes = routes_ref[...]
    total = jnp.zeros(out_ref.shape, jnp.float32)
    per = sums_ref.shape[1] // 2
    for line, (wide_bits, narrow_bits) in enumerate(back_order):
        start = order.index((wide_bits, narrow_bits)) * rows
        at = start % LANES
        for expert in range(2):
            row = expert * per + start // LANES
            found = sums_ref[line, row : row + 1, :][:, at : at + rows]
            chosen = routes == peer((wide_bits ^ expert, narrow_bits))
            total = total + jnp.where(chosen, found, 0.0)
    out_ref[...] = total


def shards_gather(out_grad, routes, gates, pre_gate, pre_up, down_weight):
    dp_count = lax.axis_size("dp")
    wide_count = lax.axis_size("wide")
    narrow_count = lax.axis_size("narrow")
    rows, features = out_grad.shape
    slot_count, units = pre_gate.shape[2:]
    half_count = slot_count // 2
    columns = features // dp_count
    routes_t = routes.T
    gates_t = gates.T
    pre_gate = pre_gate[0, 0]
    pre_up = pre_up[0, 0]
    weight = down_weight[0]
    bf16, f32 = jnp.bfloat16, jnp.float32
    shape = jax.ShapeDtypeStruct

    near = max(narrow_count // 2, 1)
    wide_bits = [1 << b for b in range(1, wide_count.bit_length() - 1)]
    reach = [0] + list(range(near, narrow_count)) + list(range(1, near))
    order = [(0, bits) for bits in reach]
    for bits in wide_bits + [1]:
        order += [(w ^ bits, n) for w, n in order]
    order = tuple(order)

    payload, token = call(
        first_kernel,
        (shape((rows, features + LANES), bf16), shape((8, LANES), f32)),
        (rows * features, 4 * rows * features),
        *in_hbm(out_grad, routes_t, gates_t),
        hbm=3,
        scratch=[
            pltpu.VMEM(routes_t.shape, routes_t.dtype),
            pltpu.VMEM(gates_t.shape, gates_t.dtype),
            pltpu.SemaphoreType.DMA((3,)),
        ],
    )
    hidden, rest_hidden = call(
        functools.partial(hidden_kernel, order, rows),
        (shape((slot_count, units), bf16), shape((half_count, units), bf16)),
        (20 * slot_count * units, 6 * slot_count * units),
        *in_hbm(pre_gate, pre_up),
        hbm=2,
        deps=(token,),
        scratch=[
            pltpu.VMEM(pre_gate.shape, pre_gate.dtype),
            pltpu.VMEM(pre_up.shape, pre_up.dtype),
            pltpu.SemaphoreType.DMA((2,)),
        ],
    )
    other_weight = swap(after(weight, token), "wide", 1)
    along = [swap(payload, "narrow", bits) if bits else payload for bits in reach]
    turned = call(
        turn_kernel,
        (shape((features // PARTS, units), bf16),) * (2 * PARTS),
        (0, 8 * features * units),
        *in_hbm(weight),
        other_weight,
        hbm=1,
        deps=(token,),
        scratch=[
            pltpu.VMEM(weight.shape, weight.dtype),
            pltpu.SemaphoreType.DMA((units // LANES,)),
        ],
    )
    over = [swap(hidden, "dp", bits) for bits in range(1, dp_count)]
    other_hidden = swap(after(rest_hidden, *along[near:]), "wide", 1)
    groups = [jnp.concatenate(along[:near], axis=0)]
    if along[near:]:
        groups.append(jnp.concatenate(along[near:], axis=0))
    for bits in wide_bits:
        groups += [swap(group, "wide", bits) for group in groups]
    middle = len(groups) // 2
    groups[middle] = after(groups[middle], *turned)
    cuts = call(
        functools.partial(cut_kernel, features, columns, len(groups)),
        (shape((half_count, columns + LANES), bf16),) * (dp_count - 1),
        (0, 4 * half_count * columns),
        *groups,
    )
    crossed = [swap(cut, "dp", bits) for bits, cut in enumerate(cuts, 1)]
    back, other_back, sums, held = call(
        functools.partial(back_kernel, features, len(groups), columns),
        (
            shape((half_count, units), f32),
            shape((half_count, units), f32),
            shape((slot_count // LANES, LANES), f32),
            shape((half_count, columns + LANES), bf16),
        ),
        (2 * slot_count * units * features, 4 * units * features),
        hidden,
        other_hidden,
        *groups,
        *turned,
    )
    slopes = call(
        functools.partial(slopes_kernel, order, rows),
        (shape((slot_count, units), f32),) * 2,
        (20 * slot_count * units, 12 * slot_count * units),
        pre_gate,
        pre_up,
        deps=(sums,),
    )
    found = sums[None]
    back_order = [(0, 0)]
    hops = [("narrow", 1 << b) for b in reversed(range(narrow_count.bit_length() - 1))]
    hops += [("wide", b) for b in wide_bits]

    def hop(found, back_order, axis, bits, *done):
        wide, narrow = (bits, 0) if axis == "wide" else (0, bits)
        found = jnp.concatenate([after(found, *done), swap(found, axis, bits)], axis=0)
        return found, back_order + [(w ^ wide, n ^ narrow) for w, n in back_order]

    found, back_order = hop(found, back_order, *hops[0], *over, *slopes)
    rest = swap(held, "wide", 1)
    rest_back = swap(other_back, "wide", 1)
    grad_a, grad_b, scaled = call(
        functools.partial(grads_kernel, order, rows, columns),
        (shape((slot_count, units), bf16),) * 3,
        (30 * slot_count * units, 12 * slot_count * units),
        held,
        rest,
        back,
        rest_back,
        hidden,
        *slopes,
    )
    for step in hops[1:-1]:
        found, back_order = hop(found, back_order, *step, scaled)
    others = []
    cut = half_count // CUTS
    for hidden_there, one in zip(over, crossed):
        others += [hidden_there, one]
        others += [swap(one[at : at + cut], "wide", 1) for at in range(0, half_count, cut)]
    grad_down = call(
        down_kernel,
        shape((units, columns), bf16),
        (2 * dp_count * slot_count * units * columns, 4 * units * columns),
        scaled,
        held,
        rest,
        *others,
        out_specs=pl.BlockSpec(memory_space=pltpu.HBM),
        scratch=[
            pltpu.VMEM((units, columns), bf16),
            pltpu.SemaphoreType.DMA((units // (2 * LANES),)),
        ],
    )
    found, back_order = hop(found, back_order, *hops[-1], grad_down)
    picked = call(
        functools.partial(pick_kernel, order, tuple(back_order), rows),
        shape(routes_t.shape, f32),
        (slot_count, slot_count),
        routes_t,
        found,
    )
    return (grad_down[None], grad_a[None, None], grad_b[None, None], picked.T)


def shards(out_grad, routes, gates, pre_gate, pre_up, down_weight):
    wide_count = lax.axis_size("wide")
    narrow_count = lax.axis_size("narrow")
    experts = wide_count * narrow_count
    rows = out_grad.shape[0]
    slot_count, units = pre_gate.shape[2:]
    features = out_grad.shape[1]
    whole_blocks = (
        slot_count == experts * rows
        and wide_count > 1
        and all(n & (n - 1) == 0 for n in (lax.axis_size("dp"), wide_count, narrow_count))
        and experts <= LANES
        and LANES % rows == 0
        and narrow_count > 1
        and rows % 16 == 0
        and (slot_count // 2) % LANES == 0
        and units % (2 * LANES) == 0
        and features % (PARTS * LANES) == 0
        and (features // lax.axis_size("dp")) % LANES == 0
    )
    plan = shards_gather if whole_blocks else shards_exchange
    return plan(out_grad, routes, gates, pre_gate, pre_up, down_weight)


def solution(mesh):
    placed = (
        P(("dp", "wide", "narrow"), None),
        P(("dp", "wide", "narrow"), None),
        P(("dp", "wide", "narrow"), None),
        P("dp", ("wide", "narrow"), None, None),
        P("dp", ("wide", "narrow"), None, None),
        P(("wide", "narrow"), None, None),
    )
    return jax.shard_map(
        shards,
        mesh=mesh,
        in_specs=placed,
        out_specs=(
            P(("wide", "narrow"), None, "dp"),
            P("dp", ("wide", "narrow"), None, None),
            P("dp", ("wide", "narrow"), None, None),
            P(("dp", "wide", "narrow"), None),
        ),
        check_vma=False,
    )
```

```python
import functools

import jax
import jax.numpy as jnp
from jax import lax
from jax.experimental import pallas as pl
from jax.experimental.pallas import tpu as pltpu
from jax.sharding import PartitionSpec as P

LANES = 128
CUTS = 2
PARTS = 4
VMEM_LIMIT = 14 * 1024 * 1024


def shards_exchange(out_grad, routes, gates, pre_gate, pre_up, down_weight):
    wide_count = lax.axis_size("wide")
    narrow_count = lax.axis_size("narrow")
    experts = wide_count * narrow_count
    token_count, top_count = routes.shape
    slot_count = pre_gate.shape[2]
    capacity = slot_count // experts
    expert_ids = jnp.arange(experts, dtype=jnp.int32)
    named_hits = (routes[:, :, None] == expert_ids[None, None, :]).astype(jnp.int32)
    hit_counts = jnp.sum(named_hits, axis=1)
    before = jnp.cumsum(hit_counts, axis=0) - hit_counts
    position = jnp.sum(named_hits * before[:, None, :], axis=2)
    target = routes * capacity + position
    slot_ids = jnp.arange(slot_count, dtype=jnp.int32)
    placed = target[:, :, None] == slot_ids[None, None, :]
    choose = jnp.sum(placed.astype(jnp.bfloat16), axis=1)
    outgoing = lax.dot_general(
        choose, out_grad, (((0,), (0,)), ((), ())), preferred_element_type=jnp.float32
    ).astype(jnp.bfloat16)
    gate_out = jnp.sum(
        jnp.where(placed, gates[:, :, None].astype(jnp.float32), 0.0), axis=(0, 1)
    ).astype(jnp.bfloat16)
    outgoing = outgoing.reshape(wide_count, narrow_count, capacity, outgoing.shape[1])
    gate_out = gate_out.reshape(wide_count, narrow_count, capacity)
    incoming, gate_in = (
        lax.all_to_all(
            lax.all_to_all(outgoing, "wide", split_axis=0, concat_axis=0, tiled=True),
            "narrow",
            split_axis=1,
            concat_axis=1,
            tiled=True,
        ),
        lax.all_to_all(
            lax.all_to_all(gate_out, "wide", split_axis=0, concat_axis=0, tiled=True),
            "narrow",
            split_axis=1,
            concat_axis=1,
            tiled=True,
        ),
    )
    routed_rows = incoming.reshape(slot_count, incoming.shape[3])
    gate_col = gate_in.reshape(slot_count).astype(jnp.float32)
    gate_pre = pre_gate[0, 0].astype(jnp.float32)
    up_pre = pre_up[0, 0].astype(jnp.float32)
    weight = down_weight[0]
    sigmoid_a = jax.nn.sigmoid(gate_pre)
    hidden = (gate_pre * sigmoid_a * up_pre).astype(jnp.bfloat16)
    back_prop = lax.dot_general(
        routed_rows, weight, (((1,), (1,)), ((), ())), preferred_element_type=jnp.float32
    )
    slot_grad = jnp.sum(hidden.astype(jnp.float32) * back_prop, axis=1)
    carried = gate_col[:, None] * back_prop
    grad_a = (carried * up_pre * sigmoid_a * (1.0 + gate_pre * (1.0 - sigmoid_a))).astype(
        jnp.bfloat16
    )
    grad_b = (carried * gate_pre * sigmoid_a).astype(jnp.bfloat16)
    scaled = (gate_col[:, None] * hidden.astype(jnp.float32)).astype(jnp.bfloat16)
    all_scaled = lax.all_gather(scaled, "dp", axis=0, tiled=True)
    columns = lax.all_to_all(routed_rows, "dp", split_axis=1, concat_axis=0, tiled=True)
    grad_down = lax.dot_general(
        all_scaled, columns, (((0,), (0,)), ((), ())), preferred_element_type=jnp.float32
    ).astype(jnp.bfloat16)
    slot_back = slot_grad.reshape(wide_count, narrow_count, capacity)
    returned = lax.all_to_all(
        lax.all_to_all(slot_back, "wide", split_axis=0, concat_axis=0, tiled=True),
        "narrow",
        split_axis=1,
        concat_axis=1,
        tiled=True,
    )
    grad_gates = jnp.take(returned.reshape(slot_count), target.reshape(-1)).reshape(
        token_count, top_count
    )
    return (grad_down[None], grad_a[None, None], grad_b[None, None], grad_gates)


def swap(x, axis, bits):
    count = lax.axis_size(axis)
    return lax.ppermute(x, axis, [(i, i ^ bits) for i in range(count)])


def after(x, *done):
    return lax.optimization_barrier((x,) + done)[0]


def call(kernel, outs, cost, *args, hbm=0, scratch=(), deps=(), out_specs=None):
    flops, moved = cost
    body = kernel
    if deps:

        def body(*refs):
            return kernel(*refs[: len(args)], *refs[len(args) + len(deps) :])

    return pl.pallas_call(
        body,
        out_shape=outs,
        in_specs=[pl.BlockSpec(memory_space=pltpu.HBM)] * hbm
        + [pl.BlockSpec(memory_space=pltpu.VMEM)] * (len(args) - hbm)
        + [pl.BlockSpec(memory_space=pl.ANY)] * len(deps),
        out_specs=jax.tree.map(lambda _: pl.BlockSpec(memory_space=pltpu.VMEM), outs)
        if out_specs is None
        else out_specs,
        scratch_shapes=scratch,
        compiler_params=pltpu.CompilerParams(vmem_limit_bytes=VMEM_LIMIT),
        cost_estimate=pl.CostEstimate(flops=flops, bytes_accessed=moved, transcendentals=0),
    )(*args, *deps)


def in_hbm(*arrays):
    return [pltpu.with_memory_space_constraint(x, pltpu.HBM) for x in arrays]


def peer(xors):
    wide_bits, narrow_bits = xors
    return (lax.axis_index("wide") ^ wide_bits) * lax.axis_size("narrow") + (
        lax.axis_index("narrow") ^ narrow_bits
    )


def first_kernel(
    grad_hbm, routes_hbm, gates_hbm, out_ref, token_ref, routes_ref, gates_ref, sems
):
    rows, features = grad_hbm.shape
    token_ref[...] = jnp.zeros(token_ref.shape, token_ref.dtype)
    copies = [
        pltpu.make_async_copy(routes_hbm, routes_ref, sems.at[0]),
        pltpu.make_async_copy(gates_hbm, gates_ref, sems.at[1]),
        pltpu.make_async_copy(grad_hbm, out_ref.at[:, pl.ds(0, features)], sems.at[2]),
    ]
    for copy in copies:
        copy.start()
    copies[0].wait()
    copies[1].wait()
    routes = routes_ref[...]
    gates = gates_ref[...].astype(jnp.float32)
    ids = lax.broadcasted_iota(jnp.int32, (LANES, rows), 0)
    table = jnp.zeros((LANES, rows), jnp.float32)
    for k in range(routes.shape[0]):
        table = table + jnp.where(ids == routes[k : k + 1, :], gates[k : k + 1, :], 0.0)
    table = jnp.concatenate([table, jnp.zeros((LANES, LANES - rows), jnp.float32)], axis=1)
    out_ref[:, features:] = table.T[:rows, :].astype(out_ref.dtype)
    copies[2].wait()


def hidden_kernel(
    order, rows, pre_gate_hbm, pre_up_hbm, hidden_ref, rest_ref, pre_gate_ref, pre_up_ref, sems
):
    copies = [
        pltpu.make_async_copy(pre_gate_hbm, pre_gate_ref, sems.at[0]),
        pltpu.make_async_copy(pre_up_hbm, pre_up_ref, sems.at[1]),
    ]
    for copy in copies:
        copy.start()
    for copy in copies:
        copy.wait()
    half = len(order) // 2
    for place, xors in enumerate(order):
        source = pl.ds(pl.multiple_of(peer(xors) * rows, rows), rows)
        value = pre_gate_ref[source, :].astype(jnp.float32)
        up = pre_up_ref[source, :].astype(jnp.float32)
        result = (value * jax.nn.sigmoid(value) * up).astype(hidden_ref.dtype)
        hidden_ref[place * rows : (place + 1) * rows, :] = result
        if place >= half:
            rest_ref[(place - half) * rows : (place - half + 1) * rows, :] = result


def turn_kernel(one_hbm, two_ref, *refs):
    one_ref, sems = refs[-2:]
    outs = refs[:-2]
    units, features = one_ref.shape
    cut = outs[0].shape[0]
    copies = [
        pltpu.make_async_copy(
            one_hbm.at[pl.ds(at, LANES)], one_ref.at[pl.ds(at, LANES)], sems.at[step]
        )
        for step, at in enumerate(range(0, units, LANES))
    ]
    for copy in copies:
        copy.start()
    for held, parts, waits in ((two_ref, outs[PARTS:], ()), (one_ref, outs[:PARTS], copies)):
        for step, at in enumerate(range(0, units, LANES)):
            if waits:
                waits[step].wait()
            for to in range(0, features, LANES):
                line = to % cut
                parts[to // cut][line : line + LANES, at : at + LANES] = held[
                    at : at + LANES, to : to + LANES
                ].T


def back_kernel(features, blocks, columns, hidden_ref, other_hidden_ref, *refs):
    group_refs, refs = refs[:blocks], refs[blocks:]
    turned_refs, refs = refs[: 2 * PARTS], refs[2 * PARTS :]
    back_ref, other_back_ref, sums_ref = refs
    held = jnp.concatenate([group_ref[...] for group_ref in group_refs], axis=0)
    rows = held.shape[0]
    for expert, (act_ref, result_ref) in enumerate(
        ((hidden_ref, back_ref), (other_hidden_ref, other_back_ref))
    ):
        back = jnp.zeros(result_ref.shape, jnp.float32)
        for part in range(PARTS):
            part_ref = turned_refs[expert * PARTS + part]
            depth = part_ref.shape[0]
            back = back + jnp.dot(
                held[:, part * depth : (part + 1) * depth],
                part_ref[...],
                preferred_element_type=jnp.float32,
            )
        result_ref[...] = back
        product = act_ref[:rows, :].astype(jnp.float32) * back
        folded = product[:, :LANES]
        for at in range(LANES, product.shape[1], LANES):
            folded = folded + product[:, at : at + LANES]
        for at in range(0, rows, LANES):
            row = (expert * rows + at) // LANES
            sums_ref[row : row + 1, :] = jnp.sum(
                folded[at : at + LANES, :].T, axis=0, keepdims=True
            )


def copy_columns(features, columns, bits, group_refs, out_ref):
    start = pl.multiple_of((lax.axis_index("dp") ^ bits) * columns, columns)
    step = out_ref.shape[0] // len(group_refs)
    for block, group_ref in enumerate(group_refs):
        here = slice(block * step, (block + 1) * step)
        out_ref[here, :columns] = group_ref[:, pl.ds(start, columns)]
        out_ref[here, columns:] = group_ref[:, features:]


def cut_kernel(features, columns, blocks, *refs):
    for bits, cut_ref in enumerate(refs[blocks:]):
        copy_columns(features, columns, bits, refs[:blocks], cut_ref)


def own_gates(table):
    lane = lax.broadcasted_iota(jnp.int32, table.shape, 1)
    return jnp.sum(
        jnp.where(lane == peer((0, 0)), table.astype(jnp.float32), 0.0), axis=1, keepdims=True
    )


def slopes_kernel(order, rows, pre_gate_ref, pre_up_ref, gate_slope_ref, up_slope_ref):
    for place, xors in enumerate(order):
        here = slice(place * rows, (place + 1) * rows)
        source = pl.ds(pl.multiple_of(peer(xors) * rows, rows), rows)
        value = pre_gate_ref[source, :].astype(jnp.float32)
        up = pre_up_ref[source, :].astype(jnp.float32)
        sig = jax.nn.sigmoid(value)
        gate_slope_ref[here, :] = up * sig * (1.0 + value * (1.0 - sig))
        up_slope_ref[here, :] = value * sig


def grads_kernel(
    order,
    rows,
    columns,
    held_ref,
    rest_ref,
    back_ref,
    rest_back_ref,
    hidden_ref,
    gate_slope_ref,
    up_slope_ref,
    grad_gate_ref,
    grad_up_ref,
    scaled_ref,
):
    half = len(order) // 2
    for place, xors in enumerate(order):
        tokens_ref, products_ref = ((held_ref, back_ref), (rest_ref, rest_back_ref))[place // half]
        there = slice((place % half) * rows, (place % half + 1) * rows)
        gate = own_gates(tokens_ref[there, columns:])
        here = slice(place * rows, (place + 1) * rows)
        source = pl.ds(pl.multiple_of(peer(xors) * rows, rows), rows)
        carried = gate * products_ref[there, :]
        grad_gate_ref[source, :] = (carried * gate_slope_ref[here, :]).astype(grad_gate_ref.dtype)
        grad_up_ref[source, :] = (carried * up_slope_ref[here, :]).astype(grad_up_ref.dtype)
        scaled_ref[here, :] = (gate * hidden_ref[here, :].astype(jnp.float32)).astype(
            scaled_ref.dtype
        )


def scale(hidden, table):
    return (own_gates(table) * hidden.astype(jnp.float32)).astype(jnp.bfloat16)


def down_kernel(scaled_ref, held_ref, rest_ref, *refs):
    out_ref, held_out_ref, sems = refs[-3:]
    columns = out_ref.shape[1]
    scaled, tokens = [scaled_ref[...]], [held_ref[:, :columns], rest_ref[:, :columns]]
    for at in range(0, len(refs) - 3, CUTS + 2):
        hidden_ref, *part_refs = refs[at : at + CUTS + 2]
        start = 0
        for part_ref in part_refs:
            stop = start + part_ref.shape[0]
            scaled.append(scale(hidden_ref[start:stop, :], part_ref[:, columns:]))
            tokens.append(part_ref[:, :columns])
            start = stop
    scaled = jnp.concatenate(scaled, axis=0)
    tokens = jnp.concatenate(tokens, axis=0)
    copies = []
    for at in range(0, out_ref.shape[0], LANES):
        here = pl.ds(at, LANES)
        held_out_ref[here, :] = lax.dot_general(
            scaled[:, at : at + LANES],
            tokens,
            (((0,), (0,)), ((), ())),
            preferred_element_type=jnp.float32,
        ).astype(out_ref.dtype)
        copies.append(
            pltpu.make_async_copy(held_out_ref.at[here], out_ref.at[here], sems.at[len(copies)])
        )
        copies[-1].start()
    for copy in copies:
        copy.wait()


def pick_kernel(order, back_order, rows, routes_ref, sums_ref, out_ref):
    routes = routes_ref[...]
    total = jnp.zeros(out_ref.shape, jnp.float32)
    per = sums_ref.shape[1] // 2
    for line, (wide_bits, narrow_bits) in enumerate(back_order):
        start = order.index((wide_bits, narrow_bits)) * rows
        at = start % LANES
        for expert in range(2):
            row = expert * per + start // LANES
            found = sums_ref[line, row : row + 1, :][:, at : at + rows]
            chosen = routes == peer((wide_bits ^ expert, narrow_bits))
            total = total + jnp.where(chosen, found, 0.0)
    out_ref[...] = total


def shards_gather(out_grad, routes, gates, pre_gate, pre_up, down_weight):
    dp_count = lax.axis_size("dp")
    wide_count = lax.axis_size("wide")
    narrow_count = lax.axis_size("narrow")
    rows, features = out_grad.shape
    slot_count, units = pre_gate.shape[2:]
    half_count = slot_count // 2
    columns = features // dp_count
    routes_t = routes.T
    gates_t = gates.T
    pre_gate = pre_gate[0, 0]
    pre_up = pre_up[0, 0]
    weight = down_weight[0]
    bf16, f32 = jnp.bfloat16, jnp.float32
    shape = jax.ShapeDtypeStruct

    near = max(narrow_count // 2, 1)
    wide_bits = [1 << b for b in range(1, wide_count.bit_length() - 1)]
    reach = [0] + list(range(near, narrow_count)) + list(range(1, near))
    order = [(0, bits) for bits in reach]
    for bits in wide_bits + [1]:
        order += [(w ^ bits, n) for w, n in order]
    order = tuple(order)

    payload, token = call(
        first_kernel,
        (shape((rows, features + LANES), bf16), shape((8, LANES), f32)),
        (rows * features, 4 * rows * features),
        *in_hbm(out_grad, routes_t, gates_t),
        hbm=3,
        scratch=[
            pltpu.VMEM(routes_t.shape, routes_t.dtype),
            pltpu.VMEM(gates_t.shape, gates_t.dtype),
            pltpu.SemaphoreType.DMA((3,)),
        ],
    )
    hidden, rest_hidden = call(
        functools.partial(hidden_kernel, order, rows),
        (shape((slot_count, units), bf16), shape((half_count, units), bf16)),
        (20 * slot_count * units, 6 * slot_count * units),
        *in_hbm(pre_gate, pre_up),
        hbm=2,
        deps=(token,),
        scratch=[
            pltpu.VMEM(pre_gate.shape, pre_gate.dtype),
            pltpu.VMEM(pre_up.shape, pre_up.dtype),
            pltpu.SemaphoreType.DMA((2,)),
        ],
    )
    other_weight = swap(after(weight, token), "wide", 1)
    along = [swap(payload, "narrow", bits) if bits else payload for bits in reach]
    turned = call(
        turn_kernel,
        (shape((features // PARTS, units), bf16),) * (2 * PARTS),
        (0, 8 * features * units),
        *in_hbm(weight),
        other_weight,
        hbm=1,
        deps=(token,),
        scratch=[
            pltpu.VMEM(weight.shape, weight.dtype),
            pltpu.SemaphoreType.DMA((units // LANES,)),
        ],
    )
    over = [swap(hidden, "dp", bits) for bits in range(1, dp_count)]
    other_hidden = swap(after(rest_hidden, *along[near:]), "wide", 1)
    groups = [jnp.concatenate(along[:near], axis=0)]
    if along[near:]:
        groups.append(jnp.concatenate(along[near:], axis=0))
    for bits in wide_bits:
        groups += [swap(group, "wide", bits) for group in groups]
    middle = len(groups) // 2
    groups[middle] = after(groups[middle], *turned)
    held, *cuts = call(
        functools.partial(cut_kernel, features, columns, len(groups)),
        (shape((half_count, columns + LANES), bf16),) * dp_count,
        (0, 4 * half_count * columns),
        *groups,
    )
    crossed = [swap(cut, "dp", bits) for bits, cut in enumerate(cuts, 1)]
    back, other_back, sums = call(
        functools.partial(back_kernel, features, len(groups), columns),
        (
            shape((half_count, units), f32),
            shape((half_count, units), f32),
            shape((slot_count // LANES, LANES), f32),
        ),
        (2 * slot_count * units * features, 4 * units * features),
        hidden,
        other_hidden,
        *groups,
        *turned,
    )
    slopes = call(
        functools.partial(slopes_kernel, order, rows),
        (shape((slot_count, units), f32),) * 2,
        (20 * slot_count * units, 12 * slot_count * units),
        pre_gate,
        pre_up,
        deps=(sums,),
    )
    found = sums[None]
    back_order = [(0, 0)]
    hops = [("narrow", 1 << b) for b in reversed(range(narrow_count.bit_length() - 1))]
    hops += [("wide", b) for b in wide_bits]

    def hop(found, back_order, axis, bits, *done):
        wide, narrow = (bits, 0) if axis == "wide" else (0, bits)
        found = jnp.concatenate([after(found, *done), swap(found, axis, bits)], axis=0)
        return found, back_order + [(w ^ wide, n ^ narrow) for w, n in back_order]

    found, back_order = hop(found, back_order, *hops[0], *over, *slopes)
    rest = swap(after(held, sums), "wide", 1)
    rest_back = swap(other_back, "wide", 1)
    grad_a, grad_b, scaled = call(
        functools.partial(grads_kernel, order, rows, columns),
        (shape((slot_count, units), bf16),) * 3,
        (30 * slot_count * units, 12 * slot_count * units),
        held,
        rest,
        back,
        rest_back,
        hidden,
        *slopes,
    )
    for step in hops[1:-1]:
        found, back_order = hop(found, back_order, *step, scaled)
    others = []
    cut = half_count // CUTS
    for hidden_there, one in zip(over, crossed):
        others += [hidden_there, one]
        others += [swap(one[at : at + cut], "wide", 1) for at in range(0, half_count, cut)]
    grad_down = call(
        down_kernel,
        shape((units, columns), bf16),
        (2 * dp_count * slot_count * units * columns, 4 * units * columns),
        scaled,
        held,
        rest,
        *others,
        out_specs=pl.BlockSpec(memory_space=pltpu.HBM),
        scratch=[
            pltpu.VMEM((units, columns), bf16),
            pltpu.SemaphoreType.DMA((units // LANES,)),
        ],
    )
    found, back_order = hop(found, back_order, *hops[-1], grad_down)
    picked = call(
        functools.partial(pick_kernel, order, tuple(back_order), rows),
        shape(routes_t.shape, f32),
        (slot_count, slot_count),
        routes_t,
        found,
    )
    return (grad_down[None], grad_a[None, None], grad_b[None, None], picked.T)


def shards(out_grad, routes, gates, pre_gate, pre_up, down_weight):
    wide_count = lax.axis_size("wide")
    narrow_count = lax.axis_size("narrow")
    experts = wide_count * narrow_count
    rows = out_grad.shape[0]
    slot_count, units = pre_gate.shape[2:]
    features = out_grad.shape[1]
    whole_blocks = (
        slot_count == experts * rows
        and wide_count > 1
        and all(n & (n - 1) == 0 for n in (lax.axis_size("dp"), wide_count, narrow_count))
        and experts <= LANES
        and LANES % rows == 0
        and narrow_count > 1
        and rows % 16 == 0
        and (slot_count // 2) % LANES == 0
        and units % (2 * LANES) == 0
        and features % (PARTS * LANES) == 0
        and (features // lax.axis_size("dp")) % LANES == 0
    )
    plan = shards_gather if whole_blocks else shards_exchange
    return plan(out_grad, routes, gates, pre_gate, pre_up, down_weight)


def solution(mesh):
    placed = (
        P(("dp", "wide", "narrow"), None),
        P(("dp", "wide", "narrow"), None),
        P(("dp", "wide", "narrow"), None),
        P("dp", ("wide", "narrow"), None, None),
        P("dp", ("wide", "narrow"), None, None),
        P(("wide", "narrow"), None, None),
    )
    return jax.shard_map(
        shards,
        mesh=mesh,
        in_specs=placed,
        out_specs=(
            P(("wide", "narrow"), None, "dp"),
            P("dp", ("wide", "narrow"), None, None),
            P("dp", ("wide", "narrow"), None, None),
            P(("dp", "wide", "narrow"), None),
        ),
        check_vma=False,
    )
```

```python
import functools

import jax
import jax.numpy as jnp
from jax import lax
from jax.experimental import pallas as pl
from jax.experimental.pallas import tpu as pltpu
from jax.sharding import PartitionSpec as P

LANES = 128
CUTS = 2
PARTS = 4
VMEM_LIMIT = 14 * 1024 * 1024


def shards_exchange(out_grad, routes, gates, pre_gate, pre_up, down_weight):
    wide_count = lax.axis_size("wide")
    narrow_count = lax.axis_size("narrow")
    experts = wide_count * narrow_count
    token_count, top_count = routes.shape
    slot_count = pre_gate.shape[2]
    capacity = slot_count // experts
    expert_ids = jnp.arange(experts, dtype=jnp.int32)
    named_hits = (routes[:, :, None] == expert_ids[None, None, :]).astype(jnp.int32)
    hit_counts = jnp.sum(named_hits, axis=1)
    before = jnp.cumsum(hit_counts, axis=0) - hit_counts
    position = jnp.sum(named_hits * before[:, None, :], axis=2)
    target = routes * capacity + position
    slot_ids = jnp.arange(slot_count, dtype=jnp.int32)
    placed = target[:, :, None] == slot_ids[None, None, :]
    choose = jnp.sum(placed.astype(jnp.bfloat16), axis=1)
    outgoing = lax.dot_general(
        choose, out_grad, (((0,), (0,)), ((), ())), preferred_element_type=jnp.float32
    ).astype(jnp.bfloat16)
    gate_out = jnp.sum(
        jnp.where(placed, gates[:, :, None].astype(jnp.float32), 0.0), axis=(0, 1)
    ).astype(jnp.bfloat16)
    outgoing = outgoing.reshape(wide_count, narrow_count, capacity, outgoing.shape[1])
    gate_out = gate_out.reshape(wide_count, narrow_count, capacity)
    incoming, gate_in = (
        lax.all_to_all(
            lax.all_to_all(outgoing, "wide", split_axis=0, concat_axis=0, tiled=True),
            "narrow",
            split_axis=1,
            concat_axis=1,
            tiled=True,
        ),
        lax.all_to_all(
            lax.all_to_all(gate_out, "wide", split_axis=0, concat_axis=0, tiled=True),
            "narrow",
            split_axis=1,
            concat_axis=1,
            tiled=True,
        ),
    )
    routed_rows = incoming.reshape(slot_count, incoming.shape[3])
    gate_col = gate_in.reshape(slot_count).astype(jnp.float32)
    gate_pre = pre_gate[0, 0].astype(jnp.float32)
    up_pre = pre_up[0, 0].astype(jnp.float32)
    weight = down_weight[0]
    sigmoid_a = jax.nn.sigmoid(gate_pre)
    hidden = (gate_pre * sigmoid_a * up_pre).astype(jnp.bfloat16)
    back_prop = lax.dot_general(
        routed_rows, weight, (((1,), (1,)), ((), ())), preferred_element_type=jnp.float32
    )
    slot_grad = jnp.sum(hidden.astype(jnp.float32) * back_prop, axis=1)
    carried = gate_col[:, None] * back_prop
    grad_a = (carried * up_pre * sigmoid_a * (1.0 + gate_pre * (1.0 - sigmoid_a))).astype(
        jnp.bfloat16
    )
    grad_b = (carried * gate_pre * sigmoid_a).astype(jnp.bfloat16)
    scaled = (gate_col[:, None] * hidden.astype(jnp.float32)).astype(jnp.bfloat16)
    all_scaled = lax.all_gather(scaled, "dp", axis=0, tiled=True)
    columns = lax.all_to_all(routed_rows, "dp", split_axis=1, concat_axis=0, tiled=True)
    grad_down = lax.dot_general(
        all_scaled, columns, (((0,), (0,)), ((), ())), preferred_element_type=jnp.float32
    ).astype(jnp.bfloat16)
    slot_back = slot_grad.reshape(wide_count, narrow_count, capacity)
    returned = lax.all_to_all(
        lax.all_to_all(slot_back, "wide", split_axis=0, concat_axis=0, tiled=True),
        "narrow",
        split_axis=1,
        concat_axis=1,
        tiled=True,
    )
    grad_gates = jnp.take(returned.reshape(slot_count), target.reshape(-1)).reshape(
        token_count, top_count
    )
    return (grad_down[None], grad_a[None, None], grad_b[None, None], grad_gates)


def swap(x, axis, bits):
    count = lax.axis_size(axis)
    return lax.ppermute(x, axis, [(i, i ^ bits) for i in range(count)])


def after(x, *done):
    return lax.optimization_barrier((x,) + done)[0]


def call(kernel, outs, cost, *args, hbm=0, scratch=(), deps=(), out_specs=None):
    flops, moved = cost
    body = kernel
    if deps:

        def body(*refs):
            return kernel(*refs[: len(args)], *refs[len(args) + len(deps) :])

    return pl.pallas_call(
        body,
        out_shape=outs,
        in_specs=[pl.BlockSpec(memory_space=pltpu.HBM)] * hbm
        + [pl.BlockSpec(memory_space=pltpu.VMEM)] * (len(args) - hbm)
        + [pl.BlockSpec(memory_space=pl.ANY)] * len(deps),
        out_specs=jax.tree.map(lambda _: pl.BlockSpec(memory_space=pltpu.VMEM), outs)
        if out_specs is None
        else out_specs,
        scratch_shapes=scratch,
        compiler_params=pltpu.CompilerParams(vmem_limit_bytes=VMEM_LIMIT),
        cost_estimate=pl.CostEstimate(flops=flops, bytes_accessed=moved, transcendentals=0),
    )(*args, *deps)


def in_hbm(*arrays):
    return [pltpu.with_memory_space_constraint(x, pltpu.HBM) for x in arrays]


def peer(xors):
    wide_bits, narrow_bits = xors
    return (lax.axis_index("wide") ^ wide_bits) * lax.axis_size("narrow") + (
        lax.axis_index("narrow") ^ narrow_bits
    )


def first_kernel(
    grad_hbm, routes_hbm, gates_hbm, out_ref, token_ref, routes_ref, gates_ref, sems
):
    rows, features = grad_hbm.shape
    token_ref[...] = jnp.zeros(token_ref.shape, token_ref.dtype)
    copies = [
        pltpu.make_async_copy(routes_hbm, routes_ref, sems.at[0]),
        pltpu.make_async_copy(gates_hbm, gates_ref, sems.at[1]),
        pltpu.make_async_copy(grad_hbm, out_ref.at[:, pl.ds(0, features)], sems.at[2]),
    ]
    for copy in copies:
        copy.start()
    copies[0].wait()
    copies[1].wait()
    routes = routes_ref[...]
    gates = gates_ref[...].astype(jnp.float32)
    ids = lax.broadcasted_iota(jnp.int32, (LANES, rows), 0)
    table = jnp.zeros((LANES, rows), jnp.float32)
    for k in range(routes.shape[0]):
        table = table + jnp.where(ids == routes[k : k + 1, :], gates[k : k + 1, :], 0.0)
    table = jnp.concatenate([table, jnp.zeros((LANES, LANES - rows), jnp.float32)], axis=1)
    out_ref[:, features:] = table.T[:rows, :].astype(out_ref.dtype)
    copies[2].wait()


def hidden_kernel(
    order, rows, pre_gate_hbm, pre_up_hbm, hidden_ref, rest_ref, pre_gate_ref, pre_up_ref, sems
):
    copies = [
        pltpu.make_async_copy(pre_gate_hbm, pre_gate_ref, sems.at[0]),
        pltpu.make_async_copy(pre_up_hbm, pre_up_ref, sems.at[1]),
    ]
    for copy in copies:
        copy.start()
    for copy in copies:
        copy.wait()
    half = len(order) // 2
    for place, xors in enumerate(order):
        source = pl.ds(pl.multiple_of(peer(xors) * rows, rows), rows)
        value = pre_gate_ref[source, :].astype(jnp.float32)
        up = pre_up_ref[source, :].astype(jnp.float32)
        result = (value * jax.nn.sigmoid(value) * up).astype(hidden_ref.dtype)
        hidden_ref[place * rows : (place + 1) * rows, :] = result
        if place >= half:
            rest_ref[(place - half) * rows : (place - half + 1) * rows, :] = result


def turn_kernel(one_hbm, two_ref, *refs):
    one_ref, sems = refs[-2:]
    outs = refs[:-2]
    units, features = one_ref.shape
    cut = outs[0].shape[0]
    copies = [
        pltpu.make_async_copy(
            one_hbm.at[pl.ds(at, LANES)], one_ref.at[pl.ds(at, LANES)], sems.at[step]
        )
        for step, at in enumerate(range(0, units, LANES))
    ]
    for copy in copies:
        copy.start()
    for held, parts, waits in ((two_ref, outs[PARTS:], ()), (one_ref, outs[:PARTS], copies)):
        for step, at in enumerate(range(0, units, LANES)):
            if waits:
                waits[step].wait()
            for to in range(0, features, LANES):
                line = to % cut
                parts[to // cut][line : line + LANES, at : at + LANES] = held[
                    at : at + LANES, to : to + LANES
                ].T


def back_kernel(features, blocks, columns, hidden_ref, other_hidden_ref, *refs):
    group_refs, refs = refs[:blocks], refs[blocks:]
    turned_refs, refs = refs[: 2 * PARTS], refs[2 * PARTS :]
    back_ref, other_back_ref, sums_ref = refs
    held = jnp.concatenate([group_ref[...] for group_ref in group_refs], axis=0)
    rows = held.shape[0]
    for expert, (act_ref, result_ref) in enumerate(
        ((hidden_ref, back_ref), (other_hidden_ref, other_back_ref))
    ):
        back = jnp.zeros(result_ref.shape, jnp.float32)
        for part in range(PARTS):
            part_ref = turned_refs[expert * PARTS + part]
            depth = part_ref.shape[0]
            back = back + jnp.dot(
                held[:, part * depth : (part + 1) * depth],
                part_ref[...],
                preferred_element_type=jnp.float32,
            )
        result_ref[...] = back
        product = act_ref[:rows, :].astype(jnp.float32) * back
        folded = product[:, :LANES]
        for at in range(LANES, product.shape[1], LANES):
            folded = folded + product[:, at : at + LANES]
        for at in range(0, rows, LANES):
            row = (expert * rows + at) // LANES
            sums_ref[row : row + 1, :] = jnp.sum(
                folded[at : at + LANES, :].T, axis=0, keepdims=True
            )


def copy_columns(features, columns, bits, group_refs, out_ref):
    start = pl.multiple_of((lax.axis_index("dp") ^ bits) * columns, columns)
    step = out_ref.shape[0] // len(group_refs)
    for block, group_ref in enumerate(group_refs):
        here = slice(block * step, (block + 1) * step)
        out_ref[here, :columns] = group_ref[:, pl.ds(start, columns)]
        out_ref[here, columns:] = group_ref[:, features:]


def cut_kernel(features, columns, blocks, *refs):
    for bits, cut_ref in enumerate(refs[blocks:]):
        copy_columns(features, columns, bits, refs[:blocks], cut_ref)


def own_gates(table):
    lane = lax.broadcasted_iota(jnp.int32, table.shape, 1)
    return jnp.sum(
        jnp.where(lane == peer((0, 0)), table.astype(jnp.float32), 0.0), axis=1, keepdims=True
    )


def slopes_kernel(order, rows, pre_gate_ref, pre_up_ref, gate_slope_ref, up_slope_ref):
    for place, xors in enumerate(order):
        here = slice(place * rows, (place + 1) * rows)
        source = pl.ds(pl.multiple_of(peer(xors) * rows, rows), rows)
        value = pre_gate_ref[source, :].astype(jnp.float32)
        up = pre_up_ref[source, :].astype(jnp.float32)
        sig = jax.nn.sigmoid(value)
        gate_slope_ref[here, :] = up * sig * (1.0 + value * (1.0 - sig))
        up_slope_ref[here, :] = value * sig


def grads_kernel(
    order,
    rows,
    columns,
    held_ref,
    rest_ref,
    back_ref,
    rest_back_ref,
    hidden_ref,
    gate_slope_ref,
    up_slope_ref,
    grad_gate_ref,
    grad_up_ref,
    scaled_ref,
):
    half = len(order) // 2
    for place, xors in enumerate(order):
        tokens_ref, products_ref = ((held_ref, back_ref), (rest_ref, rest_back_ref))[place // half]
        there = slice((place % half) * rows, (place % half + 1) * rows)
        gate = own_gates(tokens_ref[there, columns:])
        here = slice(place * rows, (place + 1) * rows)
        source = pl.ds(pl.multiple_of(peer(xors) * rows, rows), rows)
        carried = gate * products_ref[there, :]
        grad_gate_ref[source, :] = (carried * gate_slope_ref[here, :]).astype(grad_gate_ref.dtype)
        grad_up_ref[source, :] = (carried * up_slope_ref[here, :]).astype(grad_up_ref.dtype)
        scaled_ref[here, :] = (gate * hidden_ref[here, :].astype(jnp.float32)).astype(
            scaled_ref.dtype
        )


def scale(hidden, table):
    return (own_gates(table) * hidden.astype(jnp.float32)).astype(jnp.bfloat16)


def down_kernel(scaled_ref, held_ref, rest_ref, *refs):
    out_ref, held_out_ref, sems = refs[-3:]
    columns = out_ref.shape[1]
    scaled, tokens = [scaled_ref[...]], [held_ref[:, :columns], rest_ref[:, :columns]]
    for at in range(0, len(refs) - 3, CUTS + 2):
        hidden_ref, *part_refs = refs[at : at + CUTS + 2]
        start = 0
        for part_ref in part_refs:
            stop = start + part_ref.shape[0]
            scaled.append(scale(hidden_ref[start:stop, :], part_ref[:, columns:]))
            tokens.append(part_ref[:, :columns])
            start = stop
    scaled = jnp.concatenate(scaled, axis=0)
    tokens = jnp.concatenate(tokens, axis=0)
    copies = []
    for at in range(0, out_ref.shape[0], LANES):
        here = pl.ds(at, LANES)
        held_out_ref[here, :] = lax.dot_general(
            scaled[:, at : at + LANES],
            tokens,
            (((0,), (0,)), ((), ())),
            preferred_element_type=jnp.float32,
        ).astype(out_ref.dtype)
        copies.append(
            pltpu.make_async_copy(held_out_ref.at[here], out_ref.at[here], sems.at[len(copies)])
        )
        copies[-1].start()
    for copy in copies:
        copy.wait()


def pick_kernel(order, back_order, rows, routes_ref, sums_ref, out_ref):
    routes = routes_ref[...]
    total = jnp.zeros(out_ref.shape, jnp.float32)
    per = sums_ref.shape[1] // 2
    for line, (wide_bits, narrow_bits) in enumerate(back_order):
        start = order.index((wide_bits, narrow_bits)) * rows
        at = start % LANES
        for expert in range(2):
            row = expert * per + start // LANES
            found = sums_ref[line, row : row + 1, :][:, at : at + rows]
            chosen = routes == peer((wide_bits ^ expert, narrow_bits))
            total = total + jnp.where(chosen, found, 0.0)
    out_ref[...] = total


def shards_gather(out_grad, routes, gates, pre_gate, pre_up, down_weight):
    dp_count = lax.axis_size("dp")
    wide_count = lax.axis_size("wide")
    narrow_count = lax.axis_size("narrow")
    rows, features = out_grad.shape
    slot_count, units = pre_gate.shape[2:]
    half_count = slot_count // 2
    columns = features // dp_count
    routes_t = routes.T
    gates_t = gates.T
    pre_gate = pre_gate[0, 0]
    pre_up = pre_up[0, 0]
    weight = down_weight[0]
    bf16, f32 = jnp.bfloat16, jnp.float32
    shape = jax.ShapeDtypeStruct

    near = max(narrow_count // 2, 1)
    wide_bits = [1 << b for b in range(1, wide_count.bit_length() - 1)]
    reach = [0] + list(range(near, narrow_count)) + list(range(1, near))
    order = [(0, bits) for bits in reach]
    for bits in wide_bits + [1]:
        order += [(w ^ bits, n) for w, n in order]
    order = tuple(order)

    payload, token = call(
        first_kernel,
        (shape((rows, features + LANES), bf16), shape((8, LANES), f32)),
        (rows * features, 4 * rows * features),
        *in_hbm(out_grad, routes_t, gates_t),
        hbm=3,
        scratch=[
            pltpu.VMEM(routes_t.shape, routes_t.dtype),
            pltpu.VMEM(gates_t.shape, gates_t.dtype),
            pltpu.SemaphoreType.DMA((3,)),
        ],
    )
    hidden, rest_hidden = call(
        functools.partial(hidden_kernel, order, rows),
        (shape((slot_count, units), bf16), shape((half_count, units), bf16)),
        (20 * slot_count * units, 6 * slot_count * units),
        *in_hbm(pre_gate, pre_up),
        hbm=2,
        deps=(token,),
        scratch=[
            pltpu.VMEM(pre_gate.shape, pre_gate.dtype),
            pltpu.VMEM(pre_up.shape, pre_up.dtype),
            pltpu.SemaphoreType.DMA((2,)),
        ],
    )
    other_weight = swap(after(weight, token), "wide", 1)
    along = [swap(payload, "narrow", bits) if bits else payload for bits in reach]
    turned = call(
        turn_kernel,
        (shape((features // PARTS, units), bf16),) * (2 * PARTS),
        (0, 8 * features * units),
        *in_hbm(weight),
        other_weight,
        hbm=1,
        deps=(token,),
        scratch=[
            pltpu.VMEM(weight.shape, weight.dtype),
            pltpu.SemaphoreType.DMA((units // LANES,)),
        ],
    )
    over = [swap(hidden, "dp", bits) for bits in range(1, dp_count)]
    other_hidden = swap(after(rest_hidden, *along[near:]), "wide", 1)
    groups = [jnp.concatenate(along[:near], axis=0)]
    if along[near:]:
        groups.append(jnp.concatenate(along[near:], axis=0))
    for bits in wide_bits:
        groups += [swap(group, "wide", bits) for group in groups]
    middle = len(groups) // 2
    groups[middle] = after(groups[middle], *turned)
    held, *cuts = call(
        functools.partial(cut_kernel, features, columns, len(groups)),
        (shape((half_count, columns + LANES), bf16),) * dp_count,
        (0, 4 * half_count * columns),
        *groups,
    )
    crossed = [swap(cut, "dp", bits) for bits, cut in enumerate(cuts, 1)]
    back, other_back, sums = call(
        functools.partial(back_kernel, features, len(groups), columns),
        (
            shape((half_count, units), f32),
            shape((half_count, units), f32),
            shape((slot_count // LANES, LANES), f32),
        ),
        (2 * slot_count * units * features, 4 * units * features),
        hidden,
        other_hidden,
        *groups,
        *turned,
    )
    slopes = call(
        functools.partial(slopes_kernel, order, rows),
        (shape((slot_count, units), f32),) * 2,
        (20 * slot_count * units, 12 * slot_count * units),
        pre_gate,
        pre_up,
        deps=(sums,),
    )
    found = sums[None]
    back_order = [(0, 0)]
    hops = [("narrow", 1 << b) for b in range(narrow_count.bit_length() - 1)]
    hops += [("wide", b) for b in wide_bits]

    def hop(found, back_order, axis, bits, *done):
        wide, narrow = (bits, 0) if axis == "wide" else (0, bits)
        found = jnp.concatenate([after(found, *done), swap(found, axis, bits)], axis=0)
        return found, back_order + [(w ^ wide, n ^ narrow) for w, n in back_order]

    found, back_order = hop(found, back_order, *hops[0], *over, *slopes)
    rest = swap(after(held, sums), "wide", 1)
    rest_back = swap(other_back, "wide", 1)
    grad_a, grad_b, scaled = call(
        functools.partial(grads_kernel, order, rows, columns),
        (shape((slot_count, units), bf16),) * 3,
        (30 * slot_count * units, 12 * slot_count * units),
        held,
        rest,
        back,
        rest_back,
        hidden,
        *slopes,
    )
    for step in hops[1:-1]:
        found, back_order = hop(found, back_order, *step, scaled)
    others = []
    cut = half_count // CUTS
    for hidden_there, one in zip(over, crossed):
        others += [hidden_there, one]
        others += [swap(one[at : at + cut], "wide", 1) for at in range(0, half_count, cut)]
    grad_down = call(
        down_kernel,
        shape((units, columns), bf16),
        (2 * dp_count * slot_count * units * columns, 4 * units * columns),
        scaled,
        held,
        rest,
        *others,
        out_specs=pl.BlockSpec(memory_space=pltpu.HBM),
        scratch=[
            pltpu.VMEM((units, columns), bf16),
            pltpu.SemaphoreType.DMA((units // LANES,)),
        ],
    )
    found, back_order = hop(found, back_order, *hops[-1], grad_down)
    picked = call(
        functools.partial(pick_kernel, order, tuple(back_order), rows),
        shape(routes_t.shape, f32),
        (slot_count, slot_count),
        routes_t,
        found,
    )
    return (grad_down[None], grad_a[None, None], grad_b[None, None], picked.T)


def shards(out_grad, routes, gates, pre_gate, pre_up, down_weight):
    wide_count = lax.axis_size("wide")
    narrow_count = lax.axis_size("narrow")
    experts = wide_count * narrow_count
    rows = out_grad.shape[0]
    slot_count, units = pre_gate.shape[2:]
    features = out_grad.shape[1]
    whole_blocks = (
        slot_count == experts * rows
        and wide_count > 1
        and all(n & (n - 1) == 0 for n in (lax.axis_size("dp"), wide_count, narrow_count))
        and experts <= LANES
        and LANES % rows == 0
        and narrow_count > 1
        and rows % 16 == 0
        and (slot_count // 2) % LANES == 0
        and units % (2 * LANES) == 0
        and features % (PARTS * LANES) == 0
        and (features // lax.axis_size("dp")) % LANES == 0
    )
    plan = shards_gather if whole_blocks else shards_exchange
    return plan(out_grad, routes, gates, pre_gate, pre_up, down_weight)


def solution(mesh):
    placed = (
        P(("dp", "wide", "narrow"), None),
        P(("dp", "wide", "narrow"), None),
        P(("dp", "wide", "narrow"), None),
        P("dp", ("wide", "narrow"), None, None),
        P("dp", ("wide", "narrow"), None, None),
        P(("wide", "narrow"), None, None),
    )
    return jax.shard_map(
        shards,
        mesh=mesh,
        in_specs=placed,
        out_specs=(
            P(("wide", "narrow"), None, "dp"),
            P("dp", ("wide", "narrow"), None, None),
            P("dp", ("wide", "narrow"), None, None),
            P(("dp", "wide", "narrow"), None),
        ),
        check_vma=False,
    )
```

```python
import functools

import jax
import jax.numpy as jnp
from jax import lax
from jax.experimental import pallas as pl
from jax.experimental.pallas import tpu as pltpu
from jax.sharding import PartitionSpec as P

LANES = 128
CUTS = 2
PARTS = 4
VMEM_LIMIT = 14 * 1024 * 1024


def shards_exchange(out_grad, routes, gates, pre_gate, pre_up, down_weight):
    wide_count = lax.axis_size("wide")
    narrow_count = lax.axis_size("narrow")
    experts = wide_count * narrow_count
    token_count, top_count = routes.shape
    slot_count = pre_gate.shape[2]
    capacity = slot_count // experts
    expert_ids = jnp.arange(experts, dtype=jnp.int32)
    named_hits = (routes[:, :, None] == expert_ids[None, None, :]).astype(jnp.int32)
    hit_counts = jnp.sum(named_hits, axis=1)
    before = jnp.cumsum(hit_counts, axis=0) - hit_counts
    position = jnp.sum(named_hits * before[:, None, :], axis=2)
    target = routes * capacity + position
    slot_ids = jnp.arange(slot_count, dtype=jnp.int32)
    placed = target[:, :, None] == slot_ids[None, None, :]
    choose = jnp.sum(placed.astype(jnp.bfloat16), axis=1)
    outgoing = lax.dot_general(
        choose, out_grad, (((0,), (0,)), ((), ())), preferred_element_type=jnp.float32
    ).astype(jnp.bfloat16)
    gate_out = jnp.sum(
        jnp.where(placed, gates[:, :, None].astype(jnp.float32), 0.0), axis=(0, 1)
    ).astype(jnp.bfloat16)
    outgoing = outgoing.reshape(wide_count, narrow_count, capacity, outgoing.shape[1])
    gate_out = gate_out.reshape(wide_count, narrow_count, capacity)
    incoming, gate_in = (
        lax.all_to_all(
            lax.all_to_all(outgoing, "wide", split_axis=0, concat_axis=0, tiled=True),
            "narrow",
            split_axis=1,
            concat_axis=1,
            tiled=True,
        ),
        lax.all_to_all(
            lax.all_to_all(gate_out, "wide", split_axis=0, concat_axis=0, tiled=True),
            "narrow",
            split_axis=1,
            concat_axis=1,
            tiled=True,
        ),
    )
    routed_rows = incoming.reshape(slot_count, incoming.shape[3])
    gate_col = gate_in.reshape(slot_count).astype(jnp.float32)
    gate_pre = pre_gate[0, 0].astype(jnp.float32)
    up_pre = pre_up[0, 0].astype(jnp.float32)
    weight = down_weight[0]
    sigmoid_a = jax.nn.sigmoid(gate_pre)
    hidden = (gate_pre * sigmoid_a * up_pre).astype(jnp.bfloat16)
    back_prop = lax.dot_general(
        routed_rows, weight, (((1,), (1,)), ((), ())), preferred_element_type=jnp.float32
    )
    slot_grad = jnp.sum(hidden.astype(jnp.float32) * back_prop, axis=1)
    carried = gate_col[:, None] * back_prop
    grad_a = (carried * up_pre * sigmoid_a * (1.0 + gate_pre * (1.0 - sigmoid_a))).astype(
        jnp.bfloat16
    )
    grad_b = (carried * gate_pre * sigmoid_a).astype(jnp.bfloat16)
    scaled = (gate_col[:, None] * hidden.astype(jnp.float32)).astype(jnp.bfloat16)
    all_scaled = lax.all_gather(scaled, "dp", axis=0, tiled=True)
    columns = lax.all_to_all(routed_rows, "dp", split_axis=1, concat_axis=0, tiled=True)
    grad_down = lax.dot_general(
        all_scaled, columns, (((0,), (0,)), ((), ())), preferred_element_type=jnp.float32
    ).astype(jnp.bfloat16)
    slot_back = slot_grad.reshape(wide_count, narrow_count, capacity)
    returned = lax.all_to_all(
        lax.all_to_all(slot_back, "wide", split_axis=0, concat_axis=0, tiled=True),
        "narrow",
        split_axis=1,
        concat_axis=1,
        tiled=True,
    )
    grad_gates = jnp.take(returned.reshape(slot_count), target.reshape(-1)).reshape(
        token_count, top_count
    )
    return (grad_down[None], grad_a[None, None], grad_b[None, None], grad_gates)


def swap(x, axis, bits):
    count = lax.axis_size(axis)
    return lax.ppermute(x, axis, [(i, i ^ bits) for i in range(count)])


def after(x, *done):
    return lax.optimization_barrier((x,) + done)[0]


def call(kernel, outs, cost, *args, hbm=0, scratch=(), deps=(), out_specs=None):
    flops, moved = cost
    body = kernel
    if deps:

        def body(*refs):
            return kernel(*refs[: len(args)], *refs[len(args) + len(deps) :])

    return pl.pallas_call(
        body,
        out_shape=outs,
        in_specs=[pl.BlockSpec(memory_space=pltpu.HBM)] * hbm
        + [pl.BlockSpec(memory_space=pltpu.VMEM)] * (len(args) - hbm)
        + [pl.BlockSpec(memory_space=pl.ANY)] * len(deps),
        out_specs=jax.tree.map(lambda _: pl.BlockSpec(memory_space=pltpu.VMEM), outs)
        if out_specs is None
        else out_specs,
        scratch_shapes=scratch,
        compiler_params=pltpu.CompilerParams(vmem_limit_bytes=VMEM_LIMIT),
        cost_estimate=pl.CostEstimate(flops=flops, bytes_accessed=moved, transcendentals=0),
    )(*args, *deps)


def in_hbm(*arrays):
    return [pltpu.with_memory_space_constraint(x, pltpu.HBM) for x in arrays]


def peer(xors):
    wide_bits, narrow_bits = xors
    return (lax.axis_index("wide") ^ wide_bits) * lax.axis_size("narrow") + (
        lax.axis_index("narrow") ^ narrow_bits
    )


def first_kernel(
    grad_hbm, routes_hbm, gates_hbm, out_ref, token_ref, routes_ref, gates_ref, sems
):
    rows, features = grad_hbm.shape
    token_ref[...] = jnp.zeros(token_ref.shape, token_ref.dtype)
    copies = [
        pltpu.make_async_copy(routes_hbm, routes_ref, sems.at[0]),
        pltpu.make_async_copy(gates_hbm, gates_ref, sems.at[1]),
        pltpu.make_async_copy(grad_hbm, out_ref.at[:, pl.ds(0, features)], sems.at[2]),
    ]
    for copy in copies:
        copy.start()
    copies[0].wait()
    copies[1].wait()
    routes = routes_ref[...]
    gates = gates_ref[...].astype(jnp.float32)
    ids = lax.broadcasted_iota(jnp.int32, (LANES, rows), 0)
    table = jnp.zeros((LANES, rows), jnp.float32)
    for k in range(routes.shape[0]):
        table = table + jnp.where(ids == routes[k : k + 1, :], gates[k : k + 1, :], 0.0)
    table = jnp.concatenate([table, jnp.zeros((LANES, LANES - rows), jnp.float32)], axis=1)
    out_ref[:, features:] = table.T[:rows, :].astype(out_ref.dtype)
    copies[2].wait()


def hidden_kernel(
    order, rows, pre_gate_hbm, pre_up_hbm, hidden_ref, rest_ref, pre_gate_ref, pre_up_ref, sems
):
    copies = [
        pltpu.make_async_copy(pre_gate_hbm, pre_gate_ref, sems.at[0]),
        pltpu.make_async_copy(pre_up_hbm, pre_up_ref, sems.at[1]),
    ]
    for copy in copies:
        copy.start()
    for copy in copies:
        copy.wait()
    half = len(order) // 2
    for place, xors in enumerate(order):
        source = pl.ds(pl.multiple_of(peer(xors) * rows, rows), rows)
        value = pre_gate_ref[source, :].astype(jnp.float32)
        up = pre_up_ref[source, :].astype(jnp.float32)
        result = (value * jax.nn.sigmoid(value) * up).astype(hidden_ref.dtype)
        hidden_ref[place * rows : (place + 1) * rows, :] = result
        if place >= half:
            rest_ref[(place - half) * rows : (place - half + 1) * rows, :] = result


def turn_kernel(one_hbm, two_ref, *refs):
    one_ref, sems = refs[-2:]
    outs = refs[:-2]
    units, features = one_ref.shape
    cut = outs[0].shape[0]
    copies = [
        pltpu.make_async_copy(
            one_hbm.at[pl.ds(at, LANES)], one_ref.at[pl.ds(at, LANES)], sems.at[step]
        )
        for step, at in enumerate(range(0, units, LANES))
    ]
    for copy in copies:
        copy.start()
    for held, parts, waits in ((two_ref, outs[PARTS:], ()), (one_ref, outs[:PARTS], copies)):
        for step, at in enumerate(range(0, units, LANES)):
            if waits:
                waits[step].wait()
            for to in range(0, features, LANES):
                line = to % cut
                parts[to // cut][line : line + LANES, at : at + LANES] = held[
                    at : at + LANES, to : to + LANES
                ].T


def back_kernel(features, blocks, columns, hidden_ref, other_hidden_ref, *refs):
    group_refs, refs = refs[:blocks], refs[blocks:]
    turned_refs, refs = refs[: 2 * PARTS], refs[2 * PARTS :]
    back_ref, other_back_ref, sums_ref = refs
    held = jnp.concatenate([group_ref[...] for group_ref in group_refs], axis=0)
    rows = held.shape[0]
    for expert, (act_ref, result_ref) in enumerate(
        ((hidden_ref, back_ref), (other_hidden_ref, other_back_ref))
    ):
        back = jnp.zeros(result_ref.shape, jnp.float32)
        for part in range(PARTS):
            part_ref = turned_refs[expert * PARTS + part]
            depth = part_ref.shape[0]
            back = back + jnp.dot(
                held[:, part * depth : (part + 1) * depth],
                part_ref[...],
                preferred_element_type=jnp.float32,
            )
        result_ref[...] = back
        product = act_ref[:rows, :].astype(jnp.float32) * back
        folded = product[:, :LANES]
        for at in range(LANES, product.shape[1], LANES):
            folded = folded + product[:, at : at + LANES]
        for at in range(0, rows, LANES):
            row = (expert * rows + at) // LANES
            sums_ref[row : row + 1, :] = jnp.sum(
                folded[at : at + LANES, :].T, axis=0, keepdims=True
            )


def copy_columns(features, columns, bits, group_refs, out_ref):
    start = pl.multiple_of((lax.axis_index("dp") ^ bits) * columns, columns)
    step = out_ref.shape[0] // len(group_refs)
    for block, group_ref in enumerate(group_refs):
        here = slice(block * step, (block + 1) * step)
        out_ref[here, :columns] = group_ref[:, pl.ds(start, columns)]
        out_ref[here, columns:] = group_ref[:, features:]


def cut_kernel(features, columns, blocks, *refs):
    for bits, cut_ref in enumerate(refs[blocks:]):
        copy_columns(features, columns, bits, refs[:blocks], cut_ref)


def own_gates(table):
    lane = lax.broadcasted_iota(jnp.int32, table.shape, 1)
    return jnp.sum(
        jnp.where(lane == peer((0, 0)), table.astype(jnp.float32), 0.0), axis=1, keepdims=True
    )


def slopes_kernel(order, rows, pre_gate_ref, pre_up_ref, gate_slope_ref, up_slope_ref):
    for place, xors in enumerate(order):
        here = slice(place * rows, (place + 1) * rows)
        source = pl.ds(pl.multiple_of(peer(xors) * rows, rows), rows)
        value = pre_gate_ref[source, :].astype(jnp.float32)
        up = pre_up_ref[source, :].astype(jnp.float32)
        sig = jax.nn.sigmoid(value)
        gate_slope_ref[here, :] = up * sig * (1.0 + value * (1.0 - sig))
        up_slope_ref[here, :] = value * sig


def grads_kernel(
    order,
    rows,
    columns,
    held_ref,
    rest_ref,
    back_ref,
    rest_back_ref,
    hidden_ref,
    gate_slope_ref,
    up_slope_ref,
    grad_gate_ref,
    grad_up_ref,
    scaled_ref,
):
    half = len(order) // 2
    for place, xors in enumerate(order):
        tokens_ref, products_ref = ((held_ref, back_ref), (rest_ref, rest_back_ref))[place // half]
        there = slice((place % half) * rows, (place % half + 1) * rows)
        gate = own_gates(tokens_ref[there, columns:])
        here = slice(place * rows, (place + 1) * rows)
        source = pl.ds(pl.multiple_of(peer(xors) * rows, rows), rows)
        carried = gate * products_ref[there, :]
        grad_gate_ref[source, :] = (carried * gate_slope_ref[here, :]).astype(grad_gate_ref.dtype)
        grad_up_ref[source, :] = (carried * up_slope_ref[here, :]).astype(grad_up_ref.dtype)
        scaled_ref[here, :] = (gate * hidden_ref[here, :].astype(jnp.float32)).astype(
            scaled_ref.dtype
        )


def scale(hidden, table):
    return (own_gates(table) * hidden.astype(jnp.float32)).astype(jnp.bfloat16)


def down_kernel(scaled_ref, held_ref, rest_ref, *refs):
    out_ref, held_out_ref, sems = refs[-3:]
    columns = out_ref.shape[1]
    scaled, tokens = [scaled_ref[...]], [held_ref[:, :columns], rest_ref[:, :columns]]
    for at in range(0, len(refs) - 3, CUTS + 2):
        hidden_ref, *part_refs = refs[at : at + CUTS + 2]
        start = 0
        for part_ref in part_refs:
            stop = start + part_ref.shape[0]
            scaled.append(scale(hidden_ref[start:stop, :], part_ref[:, columns:]))
            tokens.append(part_ref[:, :columns])
            start = stop
    scaled = jnp.concatenate(scaled, axis=0)
    tokens = jnp.concatenate(tokens, axis=0)
    copies = []
    for at in range(0, out_ref.shape[0], LANES):
        here = pl.ds(at, LANES)
        held_out_ref[here, :] = lax.dot_general(
            scaled[:, at : at + LANES],
            tokens,
            (((0,), (0,)), ((), ())),
            preferred_element_type=jnp.float32,
        ).astype(out_ref.dtype)
        copies.append(
            pltpu.make_async_copy(held_out_ref.at[here], out_ref.at[here], sems.at[len(copies)])
        )
        copies[-1].start()
    for copy in copies:
        copy.wait()


def pick_kernel(order, back_order, rows, routes_ref, sums_ref, out_ref):
    routes = routes_ref[...]
    total = jnp.zeros(out_ref.shape, jnp.float32)
    per = sums_ref.shape[1] // 2
    for line, (wide_bits, narrow_bits) in enumerate(back_order):
        start = order.index((wide_bits, narrow_bits)) * rows
        at = start % LANES
        for expert in range(2):
            row = expert * per + start // LANES
            found = sums_ref[line, row : row + 1, :][:, at : at + rows]
            chosen = routes == peer((wide_bits ^ expert, narrow_bits))
            total = total + jnp.where(chosen, found, 0.0)
    out_ref[...] = total


def shards_gather(out_grad, routes, gates, pre_gate, pre_up, down_weight):
    dp_count = lax.axis_size("dp")
    wide_count = lax.axis_size("wide")
    narrow_count = lax.axis_size("narrow")
    rows, features = out_grad.shape
    slot_count, units = pre_gate.shape[2:]
    half_count = slot_count // 2
    columns = features // dp_count
    routes_t = routes.T
    gates_t = gates.T
    pre_gate = pre_gate[0, 0]
    pre_up = pre_up[0, 0]
    weight = down_weight[0]
    bf16, f32 = jnp.bfloat16, jnp.float32
    shape = jax.ShapeDtypeStruct

    near = max(narrow_count // 2, 1)
    wide_bits = [1 << b for b in range(1, wide_count.bit_length() - 1)]
    reach = [0] + list(range(near, narrow_count)) + list(range(1, near))
    order = [(0, bits) for bits in reach]
    for bits in wide_bits + [1]:
        order += [(w ^ bits, n) for w, n in order]
    order = tuple(order)

    payload, token = call(
        first_kernel,
        (shape((rows, features + LANES), bf16), shape((8, LANES), f32)),
        (rows * features, 4 * rows * features),
        *in_hbm(out_grad, routes_t, gates_t),
        hbm=3,
        scratch=[
            pltpu.VMEM(routes_t.shape, routes_t.dtype),
            pltpu.VMEM(gates_t.shape, gates_t.dtype),
            pltpu.SemaphoreType.DMA((3,)),
        ],
    )
    hidden, rest_hidden = call(
        functools.partial(hidden_kernel, order, rows),
        (shape((slot_count, units), bf16), shape((half_count, units), bf16)),
        (20 * slot_count * units, 6 * slot_count * units),
        *in_hbm(pre_gate, pre_up),
        hbm=2,
        deps=(token,),
        scratch=[
            pltpu.VMEM(pre_gate.shape, pre_gate.dtype),
            pltpu.VMEM(pre_up.shape, pre_up.dtype),
            pltpu.SemaphoreType.DMA((2,)),
        ],
    )
    other_weight = swap(after(weight, token), "wide", 1)
    along = [swap(payload, "narrow", bits) if bits else payload for bits in reach]
    turned = call(
        turn_kernel,
        (shape((features // PARTS, units), bf16),) * (2 * PARTS),
        (0, 8 * features * units),
        *in_hbm(weight),
        other_weight,
        hbm=1,
        deps=(token,),
        scratch=[
            pltpu.VMEM(weight.shape, weight.dtype),
            pltpu.SemaphoreType.DMA((units // LANES,)),
        ],
    )
    over = [swap(hidden, "dp", bits) for bits in range(1, dp_count)]
    other_hidden = swap(after(rest_hidden, *along[near:]), "wide", 1)
    groups = [jnp.concatenate(along[:near], axis=0)]
    if along[near:]:
        groups.append(jnp.concatenate(along[near:], axis=0))
    for bits in wide_bits:
        groups += [swap(group, "wide", bits) for group in groups]
    middle = len(groups) // 2
    groups[middle] = after(groups[middle], *turned)
    held, *cuts = call(
        functools.partial(cut_kernel, features, columns, len(groups)),
        (shape((half_count, columns + LANES), bf16),) * dp_count,
        (0, 4 * half_count * columns),
        *groups,
    )
    crossed = [swap(cut, "dp", bits) for bits, cut in enumerate(cuts, 1)]
    back, other_back, sums = call(
        functools.partial(back_kernel, features, len(groups), columns),
        (
            shape((half_count, units), f32),
            shape((half_count, units), f32),
            shape((slot_count // LANES, LANES), f32),
        ),
        (2 * slot_count * units * features, 4 * units * features),
        hidden,
        other_hidden,
        *groups,
        *turned,
    )
    slopes = call(
        functools.partial(slopes_kernel, order, rows),
        (shape((slot_count, units), f32),) * 2,
        (20 * slot_count * units, 12 * slot_count * units),
        pre_gate,
        pre_up,
        deps=(sums,),
    )
    found = after(sums, *over)[None]
    back_order = [(0, 0)]
    hops = [("narrow", 1 << b) for b in reversed(range(narrow_count.bit_length() - 1))]
    hops += [("wide", b) for b in wide_bits]

    def hop(found, back_order, axis, bits, *done):
        wide, narrow = (bits, 0) if axis == "wide" else (0, bits)
        found = jnp.concatenate([after(found, *done), swap(found, axis, bits)], axis=0)
        return found, back_order + [(w ^ wide, n ^ narrow) for w, n in back_order]

    found, back_order = hop(found, back_order, *hops[0], *slopes)
    rest = swap(after(held, sums), "wide", 1)
    rest_back = swap(other_back, "wide", 1)
    grad_a, grad_b, scaled = call(
        functools.partial(grads_kernel, order, rows, columns),
        (shape((slot_count, units), bf16),) * 3,
        (30 * slot_count * units, 12 * slot_count * units),
        held,
        rest,
        back,
        rest_back,
        hidden,
        *slopes,
    )
    for step in hops[1:-1]:
        found, back_order = hop(found, back_order, *step, scaled)
    others = []
    cut = half_count // CUTS
    for hidden_there, one in zip(over, crossed):
        others += [hidden_there, one]
        others += [swap(one[at : at + cut], "wide", 1) for at in range(0, half_count, cut)]
    grad_down = call(
        down_kernel,
        shape((units, columns), bf16),
        (2 * dp_count * slot_count * units * columns, 4 * units * columns),
        scaled,
        held,
        rest,
        *others,
        out_specs=pl.BlockSpec(memory_space=pltpu.HBM),
        scratch=[
            pltpu.VMEM((units, columns), bf16),
            pltpu.SemaphoreType.DMA((units // LANES,)),
        ],
    )
    found, back_order = hop(found, back_order, *hops[-1], grad_down)
    picked = call(
        functools.partial(pick_kernel, order, tuple(back_order), rows),
        shape(routes_t.shape, f32),
        (slot_count, slot_count),
        routes_t,
        found,
    )
    return (grad_down[None], grad_a[None, None], grad_b[None, None], picked.T)


def shards(out_grad, routes, gates, pre_gate, pre_up, down_weight):
    wide_count = lax.axis_size("wide")
    narrow_count = lax.axis_size("narrow")
    experts = wide_count * narrow_count
    rows = out_grad.shape[0]
    slot_count, units = pre_gate.shape[2:]
    features = out_grad.shape[1]
    whole_blocks = (
        slot_count == experts * rows
        and wide_count > 1
        and all(n & (n - 1) == 0 for n in (lax.axis_size("dp"), wide_count, narrow_count))
        and experts <= LANES
        and LANES % rows == 0
        and narrow_count > 1
        and rows % 16 == 0
        and (slot_count // 2) % LANES == 0
        and units % (2 * LANES) == 0
        and features % (PARTS * LANES) == 0
        and (features // lax.axis_size("dp")) % LANES == 0
    )
    plan = shards_gather if whole_blocks else shards_exchange
    return plan(out_grad, routes, gates, pre_gate, pre_up, down_weight)


def solution(mesh):
    placed = (
        P(("dp", "wide", "narrow"), None),
        P(("dp", "wide", "narrow"), None),
        P(("dp", "wide", "narrow"), None),
        P("dp", ("wide", "narrow"), None, None),
        P("dp", ("wide", "narrow"), None, None),
        P(("wide", "narrow"), None, None),
    )
    return jax.shard_map(
        shards,
        mesh=mesh,
        in_specs=placed,
        out_specs=(
            P(("wide", "narrow"), None, "dp"),
            P("dp", ("wide", "narrow"), None, None),
            P("dp", ("wide", "narrow"), None, None),
            P(("dp", "wide", "narrow"), None),
        ),
        check_vma=False,
    )
```
